32 devices in a mesh: groups: 2 (over x), space: 16 (over z, y, core).
Axes of the slice: x: 2, y: 2, z: 4, core: 2. Of those that a mesh axis runs over, the one named last changes fastest.
Arguments:
- grid_in: bfloat16 [96, 1440, 128], P(('groups', 'space')), parts along dimension 0, may hold values from -6 to 6
- upstream: bfloat16 [96, 1440, 128], P(('groups', 'space')), parts along dimension 0, may hold values from -6 to 6
- mix_weight: bfloat16 [2, 128, 128], replicated, may hold values from -0.375 to 0.375
- degree_filter: bfloat16 [512, 128], replicated, may hold values from 0.25 to 2
Outputs:
- grad_in: bfloat16 [96, 1440, 128], P(('groups', 'space')), parts along dimension 0
- grad_weight: float32 [4, 128, 128], P('groups'), parts along dimension 0
- grad_filter: float32 [1024, 128], P('groups'), parts along dimension 0
The draws below stay inside these ranges and needn't reach their ends.
There are 2 independent parts, one for each index of `groups`. The reference program is written for one: setup_inputs(seed, part) draws one part's arguments, and reference() takes and returns one part's arrays. A program takes and returns all parts, laid end to end along the dimension named above; an argument that names none is the same for every part. Nothing has to cross between parts.
All inputs are finite; a program needn't handle non-finite values.
Results may differ from the reference program's by a relative error of at most 0.02.
Values may be sent and summed in bfloat16 or wider, within the bound.
No kernel may reach another device: no remote copies, remote signals or barrier semaphores. Data moves between devices by JAX's collectives and lax.ppermute only.
A program may use at most 128 MiB of HBM per device.

```python
import math
import jax
import jax.numpy as jnp
from jax import lax

C = 128
NLON = 1440
MODES = 512
NLAT = 48


def block_levels(stream_key, dims, cuts, smallest, high):
    def one(position, parts):
        heights = jax.random.uniform(jax.random.fold_in(jax.random.fold_in(stream_key, 6), position), (parts,), jnp.float32, smallest / len(cuts), high / len(cuts))
        return jnp.repeat(jnp.exp(heights), dims[position] // parts).reshape((-1,) + (1,) * (len(dims) - position - 1))

    gain = one(*cuts[0])
    for cut in cuts[1:]:
        gain = gain * one(*cut)
    return gain


def bell_draw(rng, shape, scale, limit, pieces=(), kind=jnp.bfloat16):
    factor_of = block_levels(rng, shape, pieces, -0.22, 0.18) if pieces else 1.0
    array = jax.random.normal(rng, shape, jnp.float32) * scale * factor_of
    return jnp.minimum(jnp.maximum(array, -limit), limit).astype(kind)


def setup_inputs(seed: int = 0, part: int = 0) -> dict:
    key_list = jax.random.split(jax.random.key(seed), 5)
    part_splits = jax.random.split(jax.random.fold_in(key_list[4], part), 5)
    return {
        "grid_in": bell_draw(part_splits[0], (NLAT, NLON, C), 1.0, 6.0, ((0, 16),)),
        "upstream": bell_draw(part_splits[1], (NLAT, NLON, C), 1.0, 6.0, ((0, 16),)),
        "mix_weight": bell_draw(key_list[2], (2, C, C), (2 * C) ** -0.5, 0.375),
        "degree_filter": jnp.clip(jax.random.uniform(key_list[3], (MODES, C), jnp.float32, 0.25, 2.0), 0.25, 2.0).astype(jnp.bfloat16),
    }


def latitude_angles(lat_count):
    lat_index = jnp.arange(lat_count, dtype=jnp.float32)
    return math.pi * (lat_index + 0.5) / lat_count

def latitude_weights(lat_count):
    return math.pi / lat_count * jnp.sin(latitude_angles(lat_count))

def legendre_rows(m_values, lat_count, mode_count):
    angles = latitude_angles(lat_count)
    cosine = jnp.cos(angles)[None, :]
    sine_lat = jnp.sin(angles)[None, :]
    orders = m_values.astype(jnp.float32)[:, None]
    log_start = 0.5 * (jnp.log(2.0 * orders + 1.0) - math.log(2.0))
    log_start = log_start + 0.5 * (lax.lgamma(2.0 * orders + 1.0) - 2.0 * lax.lgamma(orders + 1.0) - orders * math.log(4.0))
    log_start = log_start + orders * jnp.log(sine_lat)

    def degree_block(carry, block_index):
        p_now, p_prev, log_scale = carry
        outputs = []
        for inner_step in range(32):
            degree = (block_index * 32 + inner_step).astype(jnp.float32)
            active = degree > orders
            denom = jnp.maximum(degree * degree - orders * orders, 1.0)
            coef_a = jnp.sqrt((4.0 * degree * degree - 1.0) / denom)
            lower = jnp.maximum((degree - 1.0) * (degree - 1.0) - orders * orders, 0.0)
            coef_b = jnp.sqrt(lower * (2.0 * degree + 1.0) / (jnp.maximum(2.0 * degree - 3.0, 1.0) * denom))
            p_next = jnp.where(active, coef_a * cosine * p_now - coef_b * p_prev, p_now)
            p_prev = jnp.where(active, p_now, p_prev)
            p_now = p_next
            outputs.append(jnp.where(degree >= orders, p_now * jnp.exp(log_scale), 0.0))
        magnitude = jnp.maximum(jnp.abs(p_now), jnp.abs(p_prev))
        next_carry = (p_now / magnitude, p_prev / magnitude, log_scale + jnp.log(magnitude))
        return (next_carry, jnp.stack(outputs, 1))
    ones_grid = jnp.ones((m_values.shape[0], lat_count), jnp.float32)
    start_carry = (ones_grid, jnp.zeros_like(ones_grid), log_start * ones_grid)
    block_ids = jnp.arange(mode_count // 32, dtype=jnp.int32)
    final_carry, stacked = lax.scan(degree_block, start_carry, block_ids)
    return jnp.transpose(stacked, (1, 0, 2, 3)).reshape(m_values.shape[0], mode_count, lat_count)

def fourier_tables(m_order, lon_count):
    lon_index = jnp.arange(lon_count, dtype=jnp.int32)
    phases = m_order[:, None] * lon_index[None, :] % lon_count
    angles = 2.0 * math.pi / lon_count * phases.astype(jnp.float32)
    factor = 1.0 / math.sqrt(lon_count)
    analysis = jnp.stack([jnp.cos(angles) * factor, -jnp.sin(angles) * factor], 1)
    analysis = analysis.reshape(2 * m_order.shape[0], lon_count).astype(jnp.bfloat16)
    doubling = jnp.where(m_order == 0, 1.0, 2.0).astype(jnp.bfloat16)
    synthesis = analysis * jnp.repeat(doubling, 2)[:, None]
    return (analysis, synthesis)

def mixing_matrix(mix_weight):
    upper = jnp.concatenate([mix_weight[0], mix_weight[1]], 1)
    lower = jnp.concatenate([-mix_weight[1], mix_weight[0]], 1)
    return jnp.concatenate([upper, lower], 0)

def fold_weight(block_grad):
    half = block_grad.shape[0] // 2
    real_part = block_grad[:half, :half] + block_grad[half:, half:]
    imag_part = block_grad[:half, half:] - block_grad[half:, :half]
    return jnp.stack([real_part, imag_part], 0)

def gelu_slope(field):
    return 0.5 * (1.0 + lax.erf(field * (1.0 / math.sqrt(2.0)))) + field * jnp.exp(-0.5 * field * field) * (1.0 / math.sqrt(2.0 * math.pi))

def product(form, left, right):
    return jnp.einsum(form, left.astype(jnp.float32), right.astype(jnp.float32), precision=lax.Precision.HIGHEST)

def reference(grid_in, upstream, mix_weight, degree_filter):
    lat_count, lon_count, channels = grid_in.shape
    positions = jnp.arange(MODES, dtype=jnp.int32)
    analysis, synthesis = fourier_tables(positions, lon_count)
    wide_weight = mixing_matrix(mix_weight)
    filter_gain = degree_filter.astype(jnp.float32)
    lat_weight = latitude_weights(lat_count)
    block_count = MODES // 32
    block_ids = jnp.arange(block_count, dtype=jnp.int32)
    fourier = product('kn,anc->akc', analysis, grid_in).astype(jnp.bfloat16)
    fourier_blocks = jnp.transpose(fourier.reshape(lat_count, block_count, 32, 2 * channels), (1, 0, 2, 3))

    def forward_pass(block_index, fourier_part):
        m_values = block_index * 32 + jnp.arange(32, dtype=jnp.int32)
        legendre = legendre_rows(m_values, lat_count, MODES)
        synth_table = legendre.astype(jnp.bfloat16)
        anal_table = (legendre * lat_weight).astype(jnp.bfloat16)
        spectrum = product('jla,ajx->jlx', anal_table, fourier_part).astype(jnp.bfloat16)
        scaled = (spectrum.reshape(32, MODES, 2, channels).astype(jnp.float32) * filter_gain[None, :, None, :]).astype(jnp.bfloat16)
        scaled_rows = scaled.reshape(32 * MODES, 2 * channels)
        mixed = jnp.dot(scaled_rows, wide_weight, preferred_element_type=jnp.float32).astype(jnp.bfloat16)
        return (synth_table, anal_table, spectrum, scaled_rows, mixed)

    def forward_block(operands):
        block_index, fourier_part = operands
        synth_table, anal_table, spectrum, scaled_rows, mixed = forward_pass(block_index, fourier_part)
        return product('jla,jlx->ajx', synth_table, mixed.reshape(32, MODES, 2 * channels)).astype(jnp.bfloat16)
    returned = lax.map(forward_block, (block_ids, fourier_blocks))
    returned = jnp.transpose(returned, (1, 0, 2, 3)).reshape(lat_count, 2 * MODES, channels)
    field = product('kn,akc->anc', synthesis, returned)
    slope = (upstream.astype(jnp.float32) * gelu_slope(field)).astype(jnp.bfloat16)
    gfourier = product('kn,anc->akc', synthesis, slope).astype(jnp.bfloat16)
    gradient_blocks = jnp.transpose(gfourier.reshape(lat_count, block_count, 32, 2 * channels), (1, 0, 2, 3))

    def backward_block(operands):
        block_index, fourier_part, gradient_part = operands
        synth_table, anal_table, spectrum, scaled_rows, mixed = forward_pass(block_index, fourier_part)
        gmixed = product('jla,ajx->jlx', synth_table, gradient_part).astype(jnp.bfloat16)
        gmixed_rows = gmixed.reshape(32 * MODES, 2 * channels)
        weight_part = lax.dot_general(scaled_rows, gmixed_rows, (((0,), (0,)), ((), ())), preferred_element_type=jnp.float32)
        gscaled = lax.dot_general(gmixed_rows, wide_weight, (((1,), (1,)), ((), ())), preferred_element_type=jnp.float32)
        gscaled = gscaled.reshape(32, MODES, 2, channels)
        filter_part = lax.optimization_barrier(jnp.sum(gscaled * spectrum.reshape(32, MODES, 2, channels).astype(jnp.float32), axis=(0, 2)))
        gspectrum = (gscaled * filter_gain[None, :, None, :]).astype(jnp.bfloat16).reshape(32, MODES, 2 * channels)
        gfield = product('jla,jlx->ajx', anal_table, gspectrum).astype(jnp.bfloat16)
        return (gfield, weight_part, filter_part)
    gfields, weight_parts, filter_parts = lax.map(backward_block, (block_ids, fourier_blocks, gradient_blocks))
    gfields = jnp.transpose(gfields, (1, 0, 2, 3)).reshape(lat_count, 2 * MODES, channels)
    grad_in = (product('kn,akc->anc', analysis, gfields) + upstream.astype(jnp.float32)).astype(jnp.bfloat16)
    grad_weight = fold_weight(lax.optimization_barrier(jnp.sum(weight_parts, 0))) * (1.0 / MODES)
    grad_filter = lax.optimization_barrier(jnp.sum(filter_parts, 0)) * 0.125
    return (grad_in, grad_weight, grad_filter)
```

```python
import functools
import math

import jax
import jax.numpy as jnp
import ml_dtypes
import numpy as np
from jax import lax
from jax.experimental import pallas as pl
from jax.experimental.pallas import tpu as pltpu
from jax.sharding import PartitionSpec as P

MODES = 512
TABLE_BYTES = 64 * 1024 * 1024
VMEM_BYTES = 18 * 1024 * 1024
DELAY = 2
BF16 = jnp.bfloat16
F32 = jnp.float32


def latitude_angles(lat_count):
    lat_index = jnp.arange(lat_count, dtype=jnp.float32)
    return math.pi * (lat_index + 0.5) / lat_count


def legendre_rows(m_values, lat_count, mode_count):
    angles = latitude_angles(lat_count)
    cosine = jnp.cos(angles)[None, :]
    sine_lat = jnp.sin(angles)[None, :]
    orders = m_values.astype(jnp.float32)[:, None]
    log_start = 0.5 * (jnp.log(2.0 * orders + 1.0) - math.log(2.0))
    log_start = log_start + 0.5 * (
        lax.lgamma(2.0 * orders + 1.0) - 2.0 * lax.lgamma(orders + 1.0) - orders * math.log(4.0)
    )
    log_start = log_start + orders * jnp.log(sine_lat)

    def degree_block(carry, block_index):
        p_now, p_prev, log_scale = carry
        outputs = []
        for inner_step in range(32):
            degree = (block_index * 32 + inner_step).astype(jnp.float32)
            active = degree > orders
            denom = jnp.maximum(degree * degree - orders * orders, 1.0)
            coef_a = jnp.sqrt((4.0 * degree * degree - 1.0) / denom)
            lower = jnp.maximum((degree - 1.0) * (degree - 1.0) - orders * orders, 0.0)
            coef_b = jnp.sqrt(
                lower * (2.0 * degree + 1.0) / (jnp.maximum(2.0 * degree - 3.0, 1.0) * denom)
            )
            p_next = jnp.where(active, coef_a * cosine * p_now - coef_b * p_prev, p_now)
            p_prev = jnp.where(active, p_now, p_prev)
            p_now = p_next
            outputs.append(jnp.where(degree >= orders, p_now * jnp.exp(log_scale), 0.0))
        magnitude = jnp.maximum(jnp.abs(p_now), jnp.abs(p_prev))
        next_carry = (p_now / magnitude, p_prev / magnitude, log_scale + jnp.log(magnitude))
        return (next_carry, jnp.stack(outputs, 1))

    ones_grid = jnp.ones((m_values.shape[0], lat_count), jnp.float32)
    start_carry = (ones_grid, jnp.zeros_like(ones_grid), log_start * ones_grid)
    block_ids = jnp.arange(mode_count // 32, dtype=jnp.int32)
    final_carry, stacked = lax.scan(degree_block, start_carry, block_ids)
    return jnp.transpose(stacked, (1, 0, 2, 3)).reshape(m_values.shape[0], mode_count, lat_count)


@functools.lru_cache(maxsize=2)
def legendre_constant(lat_count, mode_count):
    angles = np.pi * (np.arange(lat_count) + 0.5) / lat_count
    cosine = np.cos(angles)[None, :]
    orders = np.arange(mode_count, dtype=np.float64)[:, None]
    gamma_2m = np.array([math.lgamma(2.0 * m + 1.0) for m in range(mode_count)])[:, None]
    gamma_m = np.array([math.lgamma(m + 1.0) for m in range(mode_count)])[:, None]
    log_scale = 0.5 * np.log((2.0 * orders + 1.0) / 2.0)
    log_scale = log_scale + 0.5 * (gamma_2m - 2.0 * gamma_m - orders * math.log(4.0))
    log_scale = log_scale + orders * np.log(np.sin(angles))[None, :]
    p_now, p_prev = np.ones_like(log_scale), np.zeros_like(log_scale)
    table = np.zeros((mode_count, mode_count, lat_count), ml_dtypes.bfloat16)
    for degree in range(mode_count):
        active = degree > orders
        denom = np.maximum(degree * degree - orders * orders, 1.0)
        coef_a = np.sqrt(max(4.0 * degree * degree - 1.0, 0.0) / denom)
        lower = np.maximum((degree - 1.0) ** 2 - orders * orders, 0.0)
        coef_b = np.sqrt(lower * (2.0 * degree + 1.0) / (max(2.0 * degree - 3.0, 1.0) * denom))
        p_next = np.where(active, coef_a * cosine * p_now - coef_b * p_prev, p_now)
        p_prev = np.where(active, p_now, p_prev)
        p_now = p_next
        value = np.where(degree >= orders, p_now * np.exp(log_scale), 0.0)
        table[:, degree, :] = value.astype(np.float32).astype(ml_dtypes.bfloat16)
        if degree % 32 == 31:
            magnitude = np.maximum(np.abs(p_now), np.abs(p_prev))
            p_now, p_prev = p_now / magnitude, p_prev / magnitude
            log_scale = log_scale + np.log(magnitude)
    return table


@functools.lru_cache(maxsize=2)
def fourier_constant(devices, lon_count):
    half, slots = lon_count // 2, MODES // devices
    tables = []
    for parity in range(2):
        owner = 2 * np.arange(devices // 2)[:, None] + parity
        orders = (np.arange(slots)[None, :] * devices + owner).reshape(-1)
        phases = (orders[None, :] * np.arange(half)[:, None]) % lon_count
        angles = 2.0 * np.pi / lon_count * phases
        both = np.concatenate([np.cos(angles), -np.sin(angles)], 1) / math.sqrt(lon_count)
        tables.append(both.astype(np.float32).astype(ml_dtypes.bfloat16))
    table = np.stack(tables, 0)
    return np.ascontiguousarray(table), np.ascontiguousarray(table.transpose(0, 2, 1))


def degree_starts(devices):
    firsts = [slot * devices // 16 * 16 for slot in range(MODES // devices)]
    rows = [MODES - first for first in firsts]
    offsets = [sum(rows[:slot]) for slot in range(len(rows))]
    return firsts, offsets, sum(rows)


@functools.lru_cache(maxsize=2)
def packed_legendre(devices, lat_count):
    firsts, offsets, total = degree_starts(devices)
    table = legendre_constant(lat_count, MODES)
    packed = np.concatenate(
        [
            table[slot * devices : (slot + 1) * devices, first:]
            for slot, first in enumerate(firsts)
        ],
        1,
    )
    return np.ascontiguousarray(packed), np.ascontiguousarray(packed.transpose(0, 2, 1))


def table_constants(devices, lat_count):
    _, _, total = degree_starts(devices)
    if devices * total * 2 * (lat_count + max(lat_count, 128)) > TABLE_BYTES:
        return None
    return tuple(jnp.asarray(table) for table in packed_legendre(devices, lat_count))


def made_tables(devices, lat_count, me):
    firsts, _, _ = degree_starts(devices)
    slot_orders = jnp.arange(MODES // devices, dtype=jnp.int32) * devices + me
    legendre = legendre_rows(slot_orders, lat_count, MODES).astype(BF16)
    rows = jnp.concatenate([legendre[slot, first:] for slot, first in enumerate(firsts)], 0)
    return rows, rows.T


def mixing_matrix(mix_weight):
    upper = jnp.concatenate([mix_weight[0], mix_weight[1]], 1)
    lower = jnp.concatenate([-mix_weight[1], mix_weight[0]], 1)
    return jnp.concatenate([upper, lower], 0)


def gelu_slope(field):
    return 0.5 * (1.0 + lax.erf(field * (1.0 / math.sqrt(2.0)))) + field * jnp.exp(
        -0.5 * field * field
    ) * (1.0 / math.sqrt(2.0 * math.pi))


def dot(left, right):
    return jnp.dot(left, right, preferred_element_type=F32)


def row_chunks(count):
    size = count // 3 if count % 48 == 0 else count
    return [(start, size) for start in range(0, count, size)]


def store_rows(out_ref, slots, parity, lat, part, value):
    start = (2 * lat + part) * slots
    out_ref[:, parity, start : start + slots, :] = value.reshape(-1, slots, value.shape[1])


def load_rows(ref, slots, parity, lat, part):
    start = (2 * lat + part) * slots
    return ref[:, parity, start : start + slots, :].reshape(-1, ref.shape[3])


def load_pair(ref, slots, parity, lat):
    return jnp.concatenate([load_rows(ref, slots, parity, lat, part) for part in range(2)], 1)


def fetch_kernel(*refs):
    count = (len(refs) - 1) // 2
    sems = refs[-1]
    copies = [
        pltpu.make_async_copy(refs[index], refs[count + index], sems.at[index])
        for index in range(count)
    ]
    for copy in copies:
        copy.start()
    for copy in copies:
        copy.wait()


def fetch_place_kernel(place_ref, source_hbm, out_ref, sems):
    copy = pltpu.make_async_copy(source_hbm.at[place_ref[0]], out_ref, sems.at[0])
    copy.start()
    copy.wait()


def analyse_kernel(
    slots, grid_hbm, columns_hbm, out_ref, grid_ref, columns_ref, folded_ref, sems
):
    lats, lon_count, channels = grid_ref.shape
    half = lon_count // 2
    block = columns_ref.shape[1] // 2
    grid_copies = [
        pltpu.make_async_copy(grid_hbm.at[lat], grid_ref.at[lat], sems.at[lat])
        for lat in range(lats)
    ]
    table_copies = [
        pltpu.make_async_copy(
            columns_hbm.at[parity, part * block : (part + 1) * block, :],
            columns_ref.at[parity, part * block : (part + 1) * block, :],
            sems.at[lats + 2 * parity + part],
        )
        for parity in range(2)
        for part in range(2)
    ]
    for copy in grid_copies + table_copies:
        copy.start()
    for lat in range(lats):
        grid_copies[lat].wait()
        near = grid_ref[lat, :half, :].astype(F32)
        far = grid_ref[lat, half:, :].astype(F32)
        folded_ref[0, :, lat * channels : (lat + 1) * channels] = (near + far).astype(BF16)
        folded_ref[1, :, lat * channels : (lat + 1) * channels] = (near - far).astype(BF16)
    for parity in range(2):
        for part in range(2):
            table_copies[2 * parity + part].wait()
            result = dot(
                columns_ref[parity, part * block : (part + 1) * block, :], folded_ref[parity]
            ).astype(BF16)
            for lat in range(lats):
                lanes = slice(lat * channels, (lat + 1) * channels)
                store_rows(out_ref, slots, parity, lat, part, result[:, lanes])


def slot_rows(ref, part, slot, slots, lats):
    return ref[pl.ds(part * slots + slot, lats, stride=2 * slots), :]


def slot_pair(ref, slot, slots, lats, scale):
    return jnp.concatenate(
        [(slot_rows(ref, part, slot, slots, lats) * scale).astype(BF16) for part in range(2)], 1
    )


def spread(spread_ref, array_hbm, array_ref, sems, later=()):
    blocks = array_ref.shape[0]
    rows = spread_ref.shape[0] // blocks
    copies = [
        pltpu.make_async_copy(array_hbm.at[block], array_ref.at[block], sems.at[block])
        for block in range(blocks)
    ]
    for copy in [*copies, *later]:
        copy.start()
    for block, copy in enumerate(copies):
        copy.wait()
        spread_ref[block * rows : (block + 1) * rows, :] = array_ref[block].astype(F32)


def staggered(count, delay, first_stage, second_stage):
    waiting = []
    for index in range(count):
        waiting.append((index, first_stage(index)))
        if len(waiting) > delay:
            second_stage(*waiting.pop(0))
    for item in waiting:
        second_stage(*item)


def spectrum_kernel(
    devices,
    rows_ref,
    columns_ref,
    gain_ref,
    weight_ref,
    alpha_ref,
    modes_hbm,
    out_ref,
    modes_ref,
    in_s,
    out_s,
    sems,
):
    slots = MODES // devices
    lats = weight_ref.shape[0]
    firsts, offsets, _ = degree_starts(devices)
    spread(in_s, modes_hbm, modes_ref, sems)
    gain = gain_ref[...]
    channels = gain.shape[1]
    lat_weight = weight_ref[...]

    def forward(slot):
        first, offset = firsts[slot], offsets[slot]
        modes = slot_pair(in_s, slot, slots, lats, lat_weight)
        spectrum = dot(rows_ref[offset : offset + MODES - first, :], modes).astype(BF16)
        return spectrum * jnp.concatenate([gain[first:], gain[first:]], 1)

    def back(slot, scaled):
        first, offset = firsts[slot], offsets[slot]
        result = dot(columns_ref[:, offset : offset + MODES - first], scaled)
        result = result * (alpha_ref[...] if slot == 0 else 2.0)
        for part in range(2):
            out_s[pl.ds(part * slots + slot, lats, stride=2 * slots), :] = result[
                :, part * channels : (part + 1) * channels
            ]

    staggered(slots, DELAY, forward, back)
    out_ref[...] = out_s[...].reshape(out_ref.shape).astype(BF16)


def pairs_kernel(devices, weight_ref, modes_hbm, out_ref, modes_ref, in_s, sems):
    slots = MODES // devices
    lats = weight_ref.shape[0]
    spread(in_s, modes_hbm, modes_ref, sems)
    lat_weight = weight_ref[...]
    for slot in range(slots):
        out_ref[slot * lats : (slot + 1) * lats, :] = slot_pair(
            in_s, slot, slots, lats, lat_weight
        )


def gradient_kernel(
    devices,
    pairs_ref,
    rows_ref,
    gain_ref,
    weight_ref,
    alpha_ref,
    part_ref,
    place_ref,
    grads_hbm,
    columns_hbm,
    out_ref,
    filter_ref,
    grads_ref,
    columns_ref,
    grad_s,
    out_s,
    sems,
    columns_sem,
):
    slots = MODES // devices
    lats = weight_ref.shape[0]
    firsts, offsets, _ = degree_starts(devices)
    columns_copy = pltpu.make_async_copy(
        columns_hbm.at[place_ref[0]], columns_ref, columns_sem.at[0]
    )
    spread(grad_s, grads_hbm, grads_ref, sems, [columns_copy])
    gain = gain_ref[...].astype(F32)
    lat_weight = weight_ref[...]
    channels = gain.shape[1]
    filter_ref[...] = jnp.zeros_like(filter_ref)

    def forward(slot):
        first, offset = firsts[slot], offsets[slot]
        scale = alpha_ref[:, :channels] if slot == 0 else 2.0
        modes = pairs_ref[slot * lats : (slot + 1) * lats, :]
        grads = slot_pair(grad_s, slot, slots, lats, scale)
        table = rows_ref[offset : offset + MODES - first, :]
        spectrum = dot(table, modes)
        gscaled = dot(table, grads)
        product = gscaled * spectrum
        filter_ref[first:, :] += product[:, :channels] + product[:, channels:]
        return (gscaled * jnp.concatenate([gain[first:], gain[first:]], 1)).astype(BF16)

    def back(slot, gspectrum):
        first, offset = firsts[slot], offsets[slot]
        if slot == 0:
            columns_copy.wait()
        result = dot(columns_ref[:, offset : offset + MODES - first], gspectrum)
        for part in range(2):
            out_s[pl.ds(part * slots + slot, lats, stride=2 * slots), :] = (
                result[:, part * channels : (part + 1) * channels] * lat_weight
            )

    staggered(slots, DELAY, forward, back)
    rows = lats // devices * 2 * slots
    out_ref[:, :rows, :] = out_s[...].reshape(devices, rows, channels).astype(BF16)
    if out_ref.shape[1] > rows:
        split = rows + MODES // devices
        out_ref[:, rows:split, :] = (
            filter_ref[...].reshape(devices, MODES // devices, channels).astype(BF16)
        )
        out_ref[:, split:, :] = part_ref[...].reshape(devices, -1, channels).astype(BF16)


def slope_kernel(
    slots,
    modes_ref,
    wide_ref,
    wide_t_ref,
    upstream_ref,
    rows_ref,
    columns_hbm,
    out_ref,
    raw_ref,
    columns_ref,
    modes_s,
    folded_s,
    sems,
):
    columns_copies = [
        pltpu.make_async_copy(columns_hbm.at[parity], columns_ref.at[parity], sems.at[parity])
        for parity in range(2)
    ]
    for copy in columns_copies:
        copy.start()
    lats, lon_count, channels = upstream_ref.shape
    half = lon_count // 2
    block = modes_s.shape[1] // 2
    for parity in range(2):
        for lat in range(lats):
            mixed = dot(load_pair(modes_ref, slots, parity, lat), wide_ref[...]).astype(BF16)
            for part in range(2):
                modes_s[
                    parity,
                    part * block : (part + 1) * block,
                    lat * channels : (lat + 1) * channels,
                ] = mixed[:, part * channels : (part + 1) * channels]
    for start, size in row_chunks(half):
        even = dot(rows_ref[0, start : start + size, :], modes_s[0])
        odd = dot(rows_ref[1, start : start + size, :], modes_s[1])
        for lat in range(lats):
            lanes = slice(lat * channels, (lat + 1) * channels)
            near = upstream_ref[lat, start : start + size, :].astype(F32) * gelu_slope(
                even[:, lanes] + odd[:, lanes]
            )
            far = upstream_ref[lat, half + start : half + start + size, :].astype(
                F32
            ) * gelu_slope(even[:, lanes] - odd[:, lanes])
            folded_s[0, start : start + size, lanes] = (near + far).astype(BF16)
            folded_s[1, start : start + size, lanes] = (near - far).astype(BF16)
    for parity in range(2):
        columns_copies[parity].wait()
        parts = [
            dot(
                columns_ref[parity, part * block : (part + 1) * block, :], folded_s[parity]
            ).astype(BF16)
            for part in range(2)
        ]
        for lat in range(lats):
            lanes = slice(lat * channels, (lat + 1) * channels)
            pair = jnp.concatenate([parts[0][:, lanes], parts[1][:, lanes]], 1)
            mixed = dot(pair, wide_t_ref[...]).astype(BF16)
            for part in range(2):
                store_rows(raw_ref, slots, parity, lat, part, parts[part][:, lanes])
                store_rows(
                    out_ref,
                    slots,
                    parity,
                    lat,
                    part,
                    mixed[:, part * channels : (part + 1) * channels],
                )


def weight_kernel(slots, modes_ref, grad_ref, out_ref):
    channels = modes_ref.shape[3]
    total = jnp.zeros((2 * channels, 2 * channels), F32)
    for parity in range(2):
        for lat in range(modes_ref.shape[2] // (2 * slots)):
            total = total + lax.dot_general(
                load_pair(modes_ref, slots, parity, lat),
                load_pair(grad_ref, slots, parity, lat),
                (((0,), (0,)), ((), ())),
                preferred_element_type=F32,
            )
    out_ref[:channels, :] = total[:channels, :channels] + total[channels:, channels:]
    out_ref[channels:, :] = total[:channels, channels:] - total[channels:, :channels]


def synthesis_kernel(
    slots, modes_ref, upstream_hbm, rows_hbm, out_ref, upstream_ref, rows_ref, modes_s, sems
):
    lats, lon_count, channels = upstream_ref.shape
    copies = [
        pltpu.make_async_copy(rows_hbm.at[parity], rows_ref.at[parity], sems.at[parity])
        for parity in range(2)
    ]
    copies += [
        pltpu.make_async_copy(upstream_hbm.at[lat], upstream_ref.at[lat], sems.at[2 + lat])
        for lat in range(lats)
    ]
    for copy in copies:
        copy.start()
    half = lon_count // 2
    block = modes_s.shape[1] // 2
    for parity in range(2):
        for part in range(2):
            for lat in range(lats):
                modes_s[
                    parity,
                    part * block : (part + 1) * block,
                    lat * channels : (lat + 1) * channels,
                ] = load_rows(modes_ref, slots, parity, lat, part)
    for copy in copies:
        copy.wait()
    for start, size in row_chunks(half):
        even = dot(rows_ref[0, start : start + size, :], modes_s[0])
        odd = dot(rows_ref[1, start : start + size, :], modes_s[1])
        for lat in range(lats):
            lanes = slice(lat * channels, (lat + 1) * channels)
            for sign, base in ((1.0, start), (-1.0, half + start)):
                total = even[:, lanes] + sign * odd[:, lanes]
                total = total + upstream_ref[lat, base : base + size, :].astype(F32)
                out_ref[lat, base : base + size, :] = total.astype(BF16)


def total_kernel(received_ref, out_ref):
    rows = out_ref.shape[1]
    start = received_ref.shape[1] - rows
    total = received_ref[0, start:, :].astype(F32)
    for device in range(1, received_ref.shape[0]):
        total = total + received_ref[device, start:, :].astype(F32)
    out_ref[...] = jnp.broadcast_to(total.astype(BF16)[None], out_ref.shape)


def call(kernel, out_shape, scratch, flops, operands, streamed=()):
    outs = out_shape if isinstance(out_shape, (list, tuple)) else [out_shape]
    moved = sum(2 * math.prod(array.shape) for array in [*operands, *streamed, *outs])
    vmem = pl.BlockSpec(memory_space=pltpu.VMEM)
    return pl.pallas_call(
        kernel,
        out_shape=out_shape,
        in_specs=[
            pl.BlockSpec(memory_space=pltpu.SMEM if array.dtype == jnp.int32 else pltpu.VMEM)
            for array in operands
        ]
        + [pl.BlockSpec(memory_space=pl.ANY)] * len(streamed),
        out_specs=jax.tree.map(lambda _: vmem, out_shape),
        scratch_shapes=scratch,
        cost_estimate=pl.CostEstimate(flops=flops, bytes_accessed=moved, transcendentals=0),
        compiler_params=pltpu.CompilerParams(vmem_limit_bytes=VMEM_BYTES),
    )(*operands, *(away(array) for array in streamed))


def away(array):
    return pltpu.with_memory_space_constraint(array, pltpu.HBM)


def held(array):
    return pltpu.with_memory_space_constraint(array, pltpu.VMEM)


def exchange(array):
    return lax.all_to_all(array, "space", split_axis=0, concat_axis=0, tiled=True)


def sum_over_space(array, devices):
    step = devices // 2
    while step:
        array = array + lax.ppermute(
            array, "space", [(index, index ^ step) for index in range(devices)]
        )
        step //= 2
    return array


def body(grid_in, upstream, mix_weight, degree_filter):
    devices = lax.axis_size("space")
    me = lax.axis_index("space")
    lats, lon_count, channels = grid_in.shape
    lat_count = lats * devices
    slots = MODES // devices
    half = lon_count // 2
    dft_rows, dft_columns = (jnp.asarray(t) for t in fourier_constant(devices, lon_count))
    constants = table_constants(devices, lat_count)
    if constants is None:
        leg_tables = made = made_tables(devices, lat_count, me)
    else:
        leg_tables = [lax.dynamic_index_in_dim(t, me, 0, keepdims=False) for t in constants]
    angles = np.pi * (np.arange(lat_count) + 0.5) / lat_count
    lat_weight = jnp.asarray(
        np.broadcast_to((np.pi / lat_count * np.sin(angles))[:, None], (lat_count, channels)), F32
    )
    alpha = jnp.where(me == 0, 1.0, 2.0) * jnp.ones((1, 2 * channels), F32)
    wide = mixing_matrix(mix_weight)
    mode_rows = lats * 2 * slots
    grid_shape = jax.ShapeDtypeStruct((devices // 2, 2, mode_rows, channels), BF16)
    grid_out = pltpu.HBM(grid_shape.shape, BF16)
    block_shape = (devices, mode_rows, channels)
    mode_shape = jax.ShapeDtypeStruct((lat_count, 2 * slots, channels), BF16)
    spread_shape = pltpu.VMEM((lat_count * 2 * slots, channels), F32)
    modes_scratch = pltpu.VMEM((2, MODES, lats * channels), BF16)
    folded_scratch = pltpu.VMEM((2, half, lats * channels), BF16)
    dft_flops = 2 * MODES * lon_count * lats * channels
    leg_flops = 4 * degree_starts(devices)[2] * lat_count * channels
    modes_shape = (devices, mode_rows, channels)
    modes_landing = pltpu.VMEM(modes_shape, BF16)
    block_sems = pltpu.SemaphoreType.DMA((devices,))
    weight_rows = 2 * channels // devices
    extra = MODES // devices + weight_rows
    joined = (MODES // devices) % 16 == 0 and weight_rows % 16 == 0

    fourier = call(
        functools.partial(analyse_kernel, slots),
        grid_out,
        [
            pltpu.VMEM(grid_in.shape, BF16),
            pltpu.VMEM(dft_columns.shape, BF16),
            folded_scratch,
            pltpu.SemaphoreType.DMA((lats + 4,)),
        ],
        dft_flops,
        [],
        [grid_in, dft_columns],
    )
    held_upstream, held_rows = (
        held(
            call(
                fetch_kernel,
                pltpu.VMEM(array.shape, array.dtype),
                [pltpu.SemaphoreType.DMA((1,))],
                0,
                [],
                [array],
            )
        )
        for array in (upstream, dft_rows)
    )
    modes = exchange(fourier.reshape(block_shape))
    returned = call(
        functools.partial(spectrum_kernel, devices),
        pltpu.HBM(mode_shape.shape, BF16),
        [modes_landing, spread_shape, spread_shape, block_sems],
        2 * leg_flops,
        [*(held(table) for table in leg_tables), degree_filter, lat_weight, alpha],
        [modes],
    )
    returned = exchange(returned.reshape(block_shape)).reshape(grid_shape.shape)
    mixed_grad, raw_grad = call(
        functools.partial(slope_kernel, slots),
        [grid_out, grid_out],
        [
            pltpu.VMEM(dft_columns.shape, BF16),
            modes_scratch,
            folded_scratch,
            pltpu.SemaphoreType.DMA((2,)),
        ],
        2 * dft_flops,
        [away(returned), wide, wide.T, held_upstream, held_rows],
        [dft_columns],
    )
    late_place, mixed_grad = lax.optimization_barrier((me.reshape(1), mixed_grad))
    if constants is None:
        late_rows, late_columns = made[0], made[1][None]
        late_place = jnp.zeros_like(late_place)
    else:
        late_columns = constants[1]
        late_rows = call(
            fetch_place_kernel,
            pltpu.VMEM(constants[0].shape[1:], BF16),
            [pltpu.SemaphoreType.DMA((1,))],
            0,
            [late_place],
            [constants[0]],
        )
    late_modes, mixed_grad = lax.optimization_barrier((modes, mixed_grad))
    pairs = call(
        functools.partial(pairs_kernel, devices),
        pltpu.VMEM((lat_count * slots, 2 * channels), BF16),
        [modes_landing, spread_shape, block_sems],
        0,
        [lat_weight],
        [late_modes],
    )
    grads = exchange(mixed_grad.reshape(block_shape))
    weight_part = call(
        functools.partial(weight_kernel, slots),
        jax.ShapeDtypeStruct((2 * channels, channels), F32),
        [],
        4 * 2 * MODES * lats * channels * channels,
        [away(returned), away(raw_grad)],
    )
    gfield, filter_part = call(
        functools.partial(gradient_kernel, devices),
        [
            jax.ShapeDtypeStruct((devices, mode_rows + (extra if joined else 0), channels), BF16),
            jax.ShapeDtypeStruct((MODES, channels), F32),
        ],
        [
            modes_landing,
            pltpu.VMEM(late_columns.shape[1:], BF16),
            spread_shape,
            spread_shape,
            block_sems,
            pltpu.SemaphoreType.DMA((1,)),
        ],
        3 * leg_flops,
        [
            held(pairs),
            held(late_rows),
            degree_filter,
            lat_weight,
            alpha,
            weight_part,
            late_place,
        ],
        [grads, late_columns],
    )
    gfield = exchange(gfield)
    if joined:
        sums = call(
            total_kernel, jax.ShapeDtypeStruct((devices, extra, channels), BF16), [], 0, [gfield]
        )
        sums = exchange(sums).astype(F32)
        filter_sum = sums[:, : MODES // devices].reshape(MODES, channels)
        weight_sum = sums[:, MODES // devices :].reshape(2 * channels, channels)
    else:
        filter_sum = sum_over_space(filter_part, devices)
        weight_sum = sum_over_space(weight_part, devices)
    grad_in = call(
        functools.partial(synthesis_kernel, slots),
        jax.ShapeDtypeStruct(grid_in.shape, BF16),
        [
            pltpu.VMEM(upstream.shape, BF16),
            pltpu.VMEM(dft_rows.shape, BF16),
            modes_scratch,
            pltpu.SemaphoreType.DMA((2 + lats,)),
        ],
        dft_flops,
        [gfield.reshape(devices // 2, 2, -1, channels)],
        [upstream, dft_rows],
    )
    grad_weight = (weight_sum * (1.0 / MODES)).reshape(2, channels, channels)
    return (grad_in, grad_weight, filter_sum * 0.125)


def solution(mesh):
    return jax.shard_map(
        body,
        mesh=mesh,
        in_specs=(P(("groups", "space"), None, None), P(("groups", "space"), None, None), P(), P()),
        out_specs=(P(("groups", "space"), None, None), P("groups", None, None), P("groups", None)),
        check_vma=False,
    )
```

```python
import functools
import math

import jax
import jax.numpy as jnp
import ml_dtypes
import numpy as np
from jax import lax
from jax.experimental import pallas as pl
from jax.experimental.pallas import tpu as pltpu
from jax.sharding import PartitionSpec as P

MODES = 512
TABLE_BYTES = 64 * 1024 * 1024
VMEM_BYTES = 18 * 1024 * 1024
DELAY = 4
BF16 = jnp.bfloat16
F32 = jnp.float32


def latitude_angles(lat_count):
    lat_index = jnp.arange(lat_count, dtype=jnp.float32)
    return math.pi * (lat_index + 0.5) / lat_count


def legendre_rows(m_values, lat_count, mode_count):
    angles = latitude_angles(lat_count)
    cosine = jnp.cos(angles)[None, :]
    sine_lat = jnp.sin(angles)[None, :]
    orders = m_values.astype(jnp.float32)[:, None]
    log_start = 0.5 * (jnp.log(2.0 * orders + 1.0) - math.log(2.0))
    log_start = log_start + 0.5 * (
        lax.lgamma(2.0 * orders + 1.0) - 2.0 * lax.lgamma(orders + 1.0) - orders * math.log(4.0)
    )
    log_start = log_start + orders * jnp.log(sine_lat)

    def degree_block(carry, block_index):
        p_now, p_prev, log_scale = carry
        outputs = []
        for inner_step in range(32):
            degree = (block_index * 32 + inner_step).astype(jnp.float32)
            active = degree > orders
            denom = jnp.maximum(degree * degree - orders * orders, 1.0)
            coef_a = jnp.sqrt((4.0 * degree * degree - 1.0) / denom)
            lower = jnp.maximum((degree - 1.0) * (degree - 1.0) - orders * orders, 0.0)
            coef_b = jnp.sqrt(
                lower * (2.0 * degree + 1.0) / (jnp.maximum(2.0 * degree - 3.0, 1.0) * denom)
            )
            p_next = jnp.where(active, coef_a * cosine * p_now - coef_b * p_prev, p_now)
            p_prev = jnp.where(active, p_now, p_prev)
            p_now = p_next
            outputs.append(jnp.where(degree >= orders, p_now * jnp.exp(log_scale), 0.0))
        magnitude = jnp.maximum(jnp.abs(p_now), jnp.abs(p_prev))
        next_carry = (p_now / magnitude, p_prev / magnitude, log_scale + jnp.log(magnitude))
        return (next_carry, jnp.stack(outputs, 1))

    ones_grid = jnp.ones((m_values.shape[0], lat_count), jnp.float32)
    start_carry = (ones_grid, jnp.zeros_like(ones_grid), log_start * ones_grid)
    block_ids = jnp.arange(mode_count // 32, dtype=jnp.int32)
    final_carry, stacked = lax.scan(degree_block, start_carry, block_ids)
    return jnp.transpose(stacked, (1, 0, 2, 3)).reshape(m_values.shape[0], mode_count, lat_count)


@functools.lru_cache(maxsize=2)
def legendre_constant(lat_count, mode_count):
    angles = np.pi * (np.arange(lat_count) + 0.5) / lat_count
    cosine = np.cos(angles)[None, :]
    orders = np.arange(mode_count, dtype=np.float64)[:, None]
    gamma_2m = np.array([math.lgamma(2.0 * m + 1.0) for m in range(mode_count)])[:, None]
    gamma_m = np.array([math.lgamma(m + 1.0) for m in range(mode_count)])[:, None]
    log_scale = 0.5 * np.log((2.0 * orders + 1.0) / 2.0)
    log_scale = log_scale + 0.5 * (gamma_2m - 2.0 * gamma_m - orders * math.log(4.0))
    log_scale = log_scale + orders * np.log(np.sin(angles))[None, :]
    p_now, p_prev = np.ones_like(log_scale), np.zeros_like(log_scale)
    table = np.zeros((mode_count, mode_count, lat_count), ml_dtypes.bfloat16)
    for degree in range(mode_count):
        active = degree > orders
        denom = np.maximum(degree * degree - orders * orders, 1.0)
        coef_a = np.sqrt(max(4.0 * degree * degree - 1.0, 0.0) / denom)
        lower = np.maximum((degree - 1.0) ** 2 - orders * orders, 0.0)
        coef_b = np.sqrt(lower * (2.0 * degree + 1.0) / (max(2.0 * degree - 3.0, 1.0) * denom))
        p_next = np.where(active, coef_a * cosine * p_now - coef_b * p_prev, p_now)
        p_prev = np.where(active, p_now, p_prev)
        p_now = p_next
        value = np.where(degree >= orders, p_now * np.exp(log_scale), 0.0)
        table[:, degree, :] = value.astype(np.float32).astype(ml_dtypes.bfloat16)
        if degree % 32 == 31:
            magnitude = np.maximum(np.abs(p_now), np.abs(p_prev))
            p_now, p_prev = p_now / magnitude, p_prev / magnitude
            log_scale = log_scale + np.log(magnitude)
    return table


@functools.lru_cache(maxsize=2)
def fourier_constant(devices, lon_count):
    half, slots = lon_count // 2, MODES // devices
    tables = []
    for parity in range(2):
        owner = 2 * np.arange(devices // 2)[:, None] + parity
        orders = (np.arange(slots)[None, :] * devices + owner).reshape(-1)
        phases = (orders[None, :] * np.arange(half)[:, None]) % lon_count
        angles = 2.0 * np.pi / lon_count * phases
        both = np.concatenate([np.cos(angles), -np.sin(angles)], 1) / math.sqrt(lon_count)
        tables.append(both.astype(np.float32).astype(ml_dtypes.bfloat16))
    table = np.stack(tables, 0)
    return np.ascontiguousarray(table), np.ascontiguousarray(table.transpose(0, 2, 1))


def degree_starts(devices):
    firsts = [slot * devices // 16 * 16 for slot in range(MODES // devices)]
    rows = [MODES - first for first in firsts]
    offsets = [sum(rows[:slot]) for slot in range(len(rows))]
    return firsts, offsets, sum(rows)


@functools.lru_cache(maxsize=2)
def packed_legendre(devices, lat_count):
    firsts, offsets, total = degree_starts(devices)
    table = legendre_constant(lat_count, MODES)
    packed = np.concatenate(
        [
            table[slot * devices : (slot + 1) * devices, first:]
            for slot, first in enumerate(firsts)
        ],
        1,
    )
    return np.ascontiguousarray(packed), np.ascontiguousarray(packed.transpose(0, 2, 1))


def table_constants(devices, lat_count):
    _, _, total = degree_starts(devices)
    if devices * total * 2 * (lat_count + max(lat_count, 128)) > TABLE_BYTES:
        return None
    return tuple(jnp.asarray(table) for table in packed_legendre(devices, lat_count))


def made_tables(devices, lat_count, me):
    firsts, _, _ = degree_starts(devices)
    slot_orders = jnp.arange(MODES // devices, dtype=jnp.int32) * devices + me
    legendre = legendre_rows(slot_orders, lat_count, MODES).astype(BF16)
    rows = jnp.concatenate([legendre[slot, first:] for slot, first in enumerate(firsts)], 0)
    return rows, rows.T


def mixing_matrix(mix_weight):
    upper = jnp.concatenate([mix_weight[0], mix_weight[1]], 1)
    lower = jnp.concatenate([-mix_weight[1], mix_weight[0]], 1)
    return jnp.concatenate([upper, lower], 0)


def gelu_slope(field):
    return 0.5 * (1.0 + lax.erf(field * (1.0 / math.sqrt(2.0)))) + field * jnp.exp(
        -0.5 * field * field
    ) * (1.0 / math.sqrt(2.0 * math.pi))


def dot(left, right):
    return jnp.dot(left, right, preferred_element_type=F32)


def row_chunks(count):
    size = count // 3 if count % 48 == 0 else count
    return [(start, size) for start in range(0, count, size)]


def store_rows(out_ref, slots, parity, lat, part, value):
    start = (2 * lat + part) * slots
    out_ref[:, parity, start : start + slots, :] = value.reshape(-1, slots, value.shape[1])


def load_rows(ref, slots, parity, lat, part):
    start = (2 * lat + part) * slots
    return ref[:, parity, start : start + slots, :].reshape(-1, ref.shape[3])


def load_pair(ref, slots, parity, lat):
    return jnp.concatenate([load_rows(ref, slots, parity, lat, part) for part in range(2)], 1)


def fetch_kernel(*refs):
    count = (len(refs) - 1) // 2
    sems = refs[-1]
    copies = [
        pltpu.make_async_copy(refs[index], refs[count + index], sems.at[index])
        for index in range(count)
    ]
    for copy in copies:
        copy.start()
    for copy in copies:
        copy.wait()


def fetch_place_kernel(place_ref, source_hbm, out_ref, sems):
    copy = pltpu.make_async_copy(source_hbm.at[place_ref[0]], out_ref, sems.at[0])
    copy.start()
    copy.wait()


def analyse_kernel(
    slots, grid_hbm, columns_hbm, out_ref, grid_ref, columns_ref, folded_ref, sems
):
    lats, lon_count, channels = grid_ref.shape
    half = lon_count // 2
    block = columns_ref.shape[1] // 2
    grid_copies = [
        pltpu.make_async_copy(grid_hbm.at[lat], grid_ref.at[lat], sems.at[lat])
        for lat in range(lats)
    ]
    table_copies = [
        pltpu.make_async_copy(
            columns_hbm.at[parity, part * block : (part + 1) * block, :],
            columns_ref.at[parity, part * block : (part + 1) * block, :],
            sems.at[lats + 2 * parity + part],
        )
        for parity in range(2)
        for part in range(2)
    ]
    for copy in grid_copies + table_copies:
        copy.start()
    for lat in range(lats):
        grid_copies[lat].wait()
        near = grid_ref[lat, :half, :].astype(F32)
        far = grid_ref[lat, half:, :].astype(F32)
        folded_ref[0, :, lat * channels : (lat + 1) * channels] = (near + far).astype(BF16)
        folded_ref[1, :, lat * channels : (lat + 1) * channels] = (near - far).astype(BF16)
    for parity in range(2):
        for part in range(2):
            table_copies[2 * parity + part].wait()
            result = dot(
                columns_ref[parity, part * block : (part + 1) * block, :], folded_ref[parity]
            ).astype(BF16)
            for lat in range(lats):
                lanes = slice(lat * channels, (lat + 1) * channels)
                store_rows(out_ref, slots, parity, lat, part, result[:, lanes])


def slot_rows(ref, part, slot, slots, lats):
    return ref[pl.ds(part * slots + slot, lats, stride=ref.shape[0] // lats), :]


def slot_pair(ref, slot, slots, lats, scale):
    return jnp.concatenate(
        [(slot_rows(ref, part, slot, slots, lats) * scale).astype(BF16) for part in range(2)], 1
    )


def slot_halves(slots):
    size = slots // 2 if slots % 32 == 0 else slots
    return [(start, size) for start in range(0, slots, size)]


class Landing:
    def __init__(self, slots, spread_ref, array_hbm, array_ref, sems):
        lats, rows, channels = array_ref.shape
        self.halves = slot_halves(slots)
        self.spread_ref = spread_ref.reshape(lats, spread_ref.shape[0] // lats, channels)
        self.array_ref = array_ref
        self.copies = {}
        for half, (start, size) in enumerate(self.halves):
            group = []
            for part in range(2):
                span = slice(part * slots + start, part * slots + start + size)
                if len(self.halves) == 1:
                    span = slice(0, rows)
                for piece in range(2):
                    block = slice(piece * lats // 2, (piece + 1) * lats // 2)
                    copy = pltpu.make_async_copy(
                        array_hbm.at[block, span, :],
                        array_ref.at[block, span, :],
                        sems.at[4 * half + 2 * part + piece],
                    )
                    group.append((copy, block, span))
                if len(self.halves) == 1:
                    break
            self.copies[start] = group
        for group in self.copies.values():
            for copy, _, _ in group:
                copy.start()

    def need(self, slot):
        for copy, block, span in self.copies.pop(slot, ()):
            copy.wait()
            self.spread_ref[block, span, :] = self.array_ref[block, span, :].astype(F32)


def staggered(count, delay, first_stage, second_stage):
    waiting = []
    for index in range(count):
        waiting.append((index, first_stage(index)))
        if len(waiting) > delay:
            second_stage(*waiting.pop(0))
    for item in waiting:
        second_stage(*item)


def spectrum_kernel(
    devices,
    rows_ref,
    columns_ref,
    gain_ref,
    weight_ref,
    alpha_ref,
    modes_hbm,
    out_hbm,
    modes_ref,
    in_s,
    out_s,
    out_ref,
    sems,
    out_sems,
):
    slots = MODES // devices
    lats = weight_ref.shape[0]
    firsts, offsets, _ = degree_starts(devices)
    landing = Landing(slots, in_s, modes_hbm, modes_ref, sems)
    stores = []
    gain = gain_ref[...]
    channels = gain.shape[1]
    lat_weight = weight_ref[...]

    def forward(slot):
        first, offset = firsts[slot], offsets[slot]
        landing.need(slot)
        modes = slot_pair(in_s, slot, slots, lats, lat_weight)
        spectrum = dot(rows_ref[offset : offset + MODES - first, :], modes).astype(BF16)
        return spectrum * jnp.concatenate([gain[first:], gain[first:]], 1)

    def back(slot, scaled):
        first, offset = firsts[slot], offsets[slot]
        result = dot(columns_ref[:, offset : offset + MODES - first], scaled)
        result = result * (alpha_ref[...] if slot == 0 else 2.0)
        for part in range(2):
            out_s[pl.ds(part * slots + slot, lats, stride=out_s.shape[0] // lats), :] = result[
                :, part * channels : (part + 1) * channels
            ]
        for start, size in landing.halves:
            if slot == start + size - 1:
                store(start, size)

    def store(start, size):
        view = out_s.reshape(lats, out_s.shape[0] // lats, channels)
        for part in range(2):
            span = slice(part * slots + start, part * slots + start + size)
            out_ref[:, span, :] = view[:, span, :].astype(BF16)
            if size < slots:
                copy = pltpu.make_async_copy(
                    out_ref.at[:, span, :], out_hbm.at[:, span, :], out_sems.at[len(stores)]
                )
                copy.start()
                stores.append(copy)
        if size == slots:
            copy = pltpu.make_async_copy(out_ref, out_hbm, out_sems.at[0])
            copy.start()
            stores.append(copy)

    staggered(slots, DELAY, forward, back)
    for copy in stores:
        copy.wait()


def pairs_kernel(devices, weight_ref, modes_hbm, out_ref, modes_ref, in_s, sems):
    slots = MODES // devices
    lats = weight_ref.shape[0]
    landing = Landing(slots, in_s, modes_hbm, modes_ref, sems)
    lat_weight = weight_ref[...]
    for slot in range(slots):
        landing.need(slot)
        out_ref[slot * lats : (slot + 1) * lats, :] = slot_pair(
            in_s, slot, slots, lats, lat_weight
        )


def gradient_kernel(
    devices,
    pairs_ref,
    rows_ref,
    gain_ref,
    weight_ref,
    alpha_ref,
    part_ref,
    place_ref,
    grads_hbm,
    columns_hbm,
    out_ref,
    filter_ref,
    grads_ref,
    columns_ref,
    grad_s,
    out_s,
    sems,
    columns_sem,
):
    slots = MODES // devices
    lats = weight_ref.shape[0]
    firsts, offsets, _ = degree_starts(devices)
    columns_copy = pltpu.make_async_copy(
        columns_hbm.at[place_ref[0]], columns_ref, columns_sem.at[0]
    )
    landing = Landing(slots, grad_s, grads_hbm, grads_ref, sems)
    columns_copy.start()
    gain = gain_ref[...].astype(F32)
    lat_weight = weight_ref[...]
    channels = gain.shape[1]
    filter_ref[...] = jnp.zeros_like(filter_ref)

    def forward(slot):
        first, offset = firsts[slot], offsets[slot]
        landing.need(slot)
        scale = alpha_ref[:, :channels] if slot == 0 else 2.0
        modes = pairs_ref[slot * lats : (slot + 1) * lats, :]
        grads = slot_pair(grad_s, slot, slots, lats, scale)
        table = rows_ref[offset : offset + MODES - first, :]
        spectrum = dot(table, modes)
        gscaled = dot(table, grads)
        product = gscaled * spectrum
        filter_ref[first:, :] += product[:, :channels] + product[:, channels:]
        return (gscaled * jnp.concatenate([gain[first:], gain[first:]], 1)).astype(BF16)

    def back(slot, gspectrum):
        first, offset = firsts[slot], offsets[slot]
        if slot == 0:
            columns_copy.wait()
        result = dot(columns_ref[:, offset : offset + MODES - first], gspectrum)
        for part in range(2):
            out_s[pl.ds(part * slots + slot, lats, stride=out_s.shape[0] // lats), :] = (
                result[:, part * channels : (part + 1) * channels] * lat_weight
            )

    staggered(slots, DELAY, forward, back)
    rows = lats // devices * 2 * slots
    view = out_s.reshape(lats, out_s.shape[0] // lats, channels)
    out_ref[:, :rows, :] = (
        view[:, : 2 * slots, :].astype(BF16).reshape(devices, rows, channels)
    )
    if out_ref.shape[1] > rows:
        split = rows + MODES // devices
        out_ref[:, rows:split, :] = (
            filter_ref[...].reshape(devices, MODES // devices, channels).astype(BF16)
        )
        out_ref[:, split:, :] = part_ref[...].reshape(devices, -1, channels).astype(BF16)


def slope_kernel(
    slots,
    wide_ref,
    wide_t_ref,
    upstream_ref,
    rows_ref,
    modes_hbm,
    columns_hbm,
    out_hbm,
    weight_ref,
    modes_ref,
    columns_ref,
    modes_s,
    folded_s,
    out_ref,
    sems,
    columns_sems,
    out_sems,
):
    lats, lon_count, channels = upstream_ref.shape
    half = lon_count // 2
    block = modes_s.shape[1] // 2

    def lat_copy(source, target, sem_refs, parity, lat):
        span = slice(2 * lat * slots, 2 * (lat + 1) * slots)
        return pltpu.make_async_copy(
            source.at[:, parity, span, :],
            target.at[:, parity, span, :],
            sem_refs.at[parity * lats + lat],
        )

    places = [(parity, lat) for parity in range(2) for lat in range(lats)]
    modes_copies = [lat_copy(modes_hbm, modes_ref, sems, *place) for place in places]
    columns_copies = [
        pltpu.make_async_copy(
            columns_hbm.at[parity], columns_ref.at[parity], columns_sems.at[parity]
        )
        for parity in range(2)
    ]
    for copy in modes_copies + columns_copies:
        copy.start()
    for (parity, lat), copy in zip(places, modes_copies):
        copy.wait()
        mixed = dot(load_pair(modes_ref, slots, parity, lat), wide_ref[...]).astype(BF16)
        for part in range(2):
            modes_s[
                parity,
                part * block : (part + 1) * block,
                lat * channels : (lat + 1) * channels,
            ] = mixed[:, part * channels : (part + 1) * channels]
    for start, size in row_chunks(half):
        even = dot(rows_ref[0, start : start + size, :], modes_s[0])
        odd = dot(rows_ref[1, start : start + size, :], modes_s[1])
        for lat in range(lats):
            lanes = slice(lat * channels, (lat + 1) * channels)
            near = upstream_ref[lat, start : start + size, :].astype(F32) * gelu_slope(
                even[:, lanes] + odd[:, lanes]
            )
            far = upstream_ref[lat, half + start : half + start + size, :].astype(
                F32
            ) * gelu_slope(even[:, lanes] - odd[:, lanes])
            folded_s[0, start : start + size, lanes] = (near + far).astype(BF16)
            folded_s[1, start : start + size, lanes] = (near - far).astype(BF16)
    pairs, stores = [], []
    for parity in range(2):
        columns_copies[parity].wait()
        parts = [
            dot(
                columns_ref[parity, part * block : (part + 1) * block, :], folded_s[parity]
            ).astype(BF16)
            for part in range(2)
        ]
        for lat in range(lats):
            lanes = slice(lat * channels, (lat + 1) * channels)
            pair = jnp.concatenate([parts[0][:, lanes], parts[1][:, lanes]], 1)
            mixed = dot(pair, wide_t_ref[...]).astype(BF16)
            for part in range(2):
                store_rows(
                    out_ref,
                    slots,
                    parity,
                    lat,
                    part,
                    mixed[:, part * channels : (part + 1) * channels],
                )
            stores.append(lat_copy(out_ref, out_hbm, out_sems, parity, lat))
            stores[-1].start()
            pairs.append(pair)
    total = jnp.zeros((2 * channels, 2 * channels), F32)
    for (parity, lat), pair in zip(places, pairs):
        total = total + lax.dot_general(
            load_pair(modes_ref, slots, parity, lat),
            pair,
            (((0,), (0,)), ((), ())),
            preferred_element_type=F32,
        )
    weight_ref[:channels, :] = total[:channels, :channels] + total[channels:, channels:]
    weight_ref[channels:, :] = total[:channels, channels:] - total[channels:, :channels]
    for copy in stores:
        copy.wait()


def synthesis_kernel(
    slots, modes_ref, upstream_hbm, rows_hbm, out_ref, upstream_ref, rows_ref, modes_s, sems
):
    lats, lon_count, channels = upstream_ref.shape
    copies = [
        pltpu.make_async_copy(rows_hbm.at[parity], rows_ref.at[parity], sems.at[parity])
        for parity in range(2)
    ]
    copies += [
        pltpu.make_async_copy(upstream_hbm.at[lat], upstream_ref.at[lat], sems.at[2 + lat])
        for lat in range(lats)
    ]
    for copy in copies:
        copy.start()
    half = lon_count // 2
    block = modes_s.shape[1] // 2
    for parity in range(2):
        for part in range(2):
            for lat in range(lats):
                modes_s[
                    parity,
                    part * block : (part + 1) * block,
                    lat * channels : (lat + 1) * channels,
                ] = load_rows(modes_ref, slots, parity, lat, part)
    for copy in copies:
        copy.wait()
    for start, size in row_chunks(half):
        even = dot(rows_ref[0, start : start + size, :], modes_s[0])
        odd = dot(rows_ref[1, start : start + size, :], modes_s[1])
        for lat in range(lats):
            lanes = slice(lat * channels, (lat + 1) * channels)
            for sign, base in ((1.0, start), (-1.0, half + start)):
                total = even[:, lanes] + sign * odd[:, lanes]
                total = total + upstream_ref[lat, base : base + size, :].astype(F32)
                out_ref[lat, base : base + size, :] = total.astype(BF16)


def total_kernel(received_ref, out_ref):
    rows = out_ref.shape[1]
    start = received_ref.shape[1] - rows
    total = received_ref[0, start:, :].astype(F32)
    for device in range(1, received_ref.shape[0]):
        total = total + received_ref[device, start:, :].astype(F32)
    out_ref[...] = jnp.broadcast_to(total.astype(BF16)[None], out_ref.shape)


def finish_kernel(received_ref, filter_ref, weight_ref):
    devices, rows, channels = received_ref.shape
    split = filter_ref.shape[0] // devices
    filter_ref[...] = (
        received_ref[:, :split, :].astype(F32).reshape(filter_ref.shape) * 0.125
    )
    weight_ref[...] = received_ref[:, split:, :].astype(F32).reshape(weight_ref.shape) * (
        1.0 / MODES
    )


def call(kernel, out_shape, scratch, flops, operands, streamed=(), written=0):
    outs = out_shape if isinstance(out_shape, (list, tuple)) else [out_shape]
    moved = sum(2 * math.prod(array.shape) for array in [*operands, *streamed, *outs])
    specs = [
        pl.BlockSpec(memory_space=pl.ANY if index < written else pltpu.VMEM)
        for index in range(len(outs))
    ]
    return pl.pallas_call(
        kernel,
        out_shape=out_shape,
        in_specs=[
            pl.BlockSpec(memory_space=pltpu.SMEM if array.dtype == jnp.int32 else pltpu.VMEM)
            for array in operands
        ]
        + [pl.BlockSpec(memory_space=pl.ANY)] * len(streamed),
        out_specs=specs if isinstance(out_shape, (list, tuple)) else specs[0],
        scratch_shapes=scratch,
        cost_estimate=pl.CostEstimate(flops=flops, bytes_accessed=moved, transcendentals=0),
        compiler_params=pltpu.CompilerParams(vmem_limit_bytes=VMEM_BYTES),
    )(*operands, *(away(array) for array in streamed))


def away(array):
    return pltpu.with_memory_space_constraint(array, pltpu.HBM)


def held(array):
    return pltpu.with_memory_space_constraint(array, pltpu.VMEM)


def exchange(array):
    return lax.all_to_all(array, "space", split_axis=0, concat_axis=0, tiled=True)


def sum_over_space(array, devices):
    step = devices // 2
    while step:
        array = array + lax.ppermute(
            array, "space", [(index, index ^ step) for index in range(devices)]
        )
        step //= 2
    return array


def body(grid_in, upstream, mix_weight, degree_filter):
    devices = lax.axis_size("space")
    me = lax.axis_index("space")
    lats, lon_count, channels = grid_in.shape
    lat_count = lats * devices
    slots = MODES // devices
    half = lon_count // 2
    dft_rows, dft_columns = (jnp.asarray(t) for t in fourier_constant(devices, lon_count))
    constants = table_constants(devices, lat_count)
    if constants is None:
        leg_tables = made = made_tables(devices, lat_count, me)
    else:
        leg_tables = [lax.dynamic_index_in_dim(t, me, 0, keepdims=False) for t in constants]
    angles = np.pi * (np.arange(lat_count) + 0.5) / lat_count
    lat_weight = jnp.asarray(
        np.broadcast_to((np.pi / lat_count * np.sin(angles))[:, None], (lat_count, channels)), F32
    )
    alpha = jnp.where(me == 0, 1.0, 2.0) * jnp.ones((1, 2 * channels), F32)
    wide = mixing_matrix(mix_weight)
    mode_rows = lats * 2 * slots
    grid_shape = jax.ShapeDtypeStruct((devices // 2, 2, mode_rows, channels), BF16)
    grid_out = pltpu.HBM(grid_shape.shape, BF16)
    block_shape = (devices, mode_rows, channels)
    mode_shape = jax.ShapeDtypeStruct((lat_count, 2 * slots, channels), BF16)
    spread_shape = pltpu.VMEM((lat_count * (2 * slots + 8), channels), F32)
    modes_scratch = pltpu.VMEM((2, MODES, lats * channels), BF16)
    folded_scratch = pltpu.VMEM((2, half, lats * channels), BF16)
    dft_flops = 2 * MODES * lon_count * lats * channels
    leg_flops = 4 * degree_starts(devices)[2] * lat_count * channels
    modes_landing = pltpu.VMEM(mode_shape.shape, BF16)
    block_sems = pltpu.SemaphoreType.DMA((8,))
    weight_rows = 2 * channels // devices
    extra = MODES // devices + weight_rows
    joined = (MODES // devices) % 16 == 0 and weight_rows % 16 == 0

    fourier = call(
        functools.partial(analyse_kernel, slots),
        grid_out,
        [
            pltpu.VMEM(grid_in.shape, BF16),
            pltpu.VMEM(dft_columns.shape, BF16),
            folded_scratch,
            pltpu.SemaphoreType.DMA((lats + 4,)),
        ],
        dft_flops,
        [],
        [grid_in, dft_columns],
    )
    held_upstream, held_rows = (
        held(
            call(
                fetch_kernel,
                pltpu.VMEM(array.shape, array.dtype),
                [pltpu.SemaphoreType.DMA((1,))],
                0,
                [],
                [array],
            )
        )
        for array in (upstream, dft_rows)
    )
    modes = exchange(fourier.reshape(block_shape)).reshape(mode_shape.shape)
    returned = call(
        functools.partial(spectrum_kernel, devices),
        pltpu.HBM(mode_shape.shape, BF16),
        [
            modes_landing,
            spread_shape,
            spread_shape,
            modes_landing,
            block_sems,
            pltpu.SemaphoreType.DMA((4,)),
        ],
        2 * leg_flops,
        [*(held(table) for table in leg_tables), degree_filter, lat_weight, alpha],
        [modes],
        written=1,
    )
    returned = exchange(returned.reshape(block_shape)).reshape(grid_shape.shape)
    grid_landing = pltpu.VMEM(grid_shape.shape, BF16)
    mixed_grad, weight_part = call(
        functools.partial(slope_kernel, slots),
        [grid_out, jax.ShapeDtypeStruct((2 * channels, channels), F32)],
        [
            grid_landing,
            pltpu.VMEM(dft_columns.shape, BF16),
            modes_scratch,
            folded_scratch,
            grid_landing,
            pltpu.SemaphoreType.DMA((2 * lats,)),
            pltpu.SemaphoreType.DMA((2,)),
            pltpu.SemaphoreType.DMA((2 * lats,)),
        ],
        2 * dft_flops,
        [wide, wide.T, held_upstream, held_rows],
        [returned, dft_columns],
        written=1,
    )
    late_place, mixed_grad = lax.optimization_barrier((me.reshape(1), mixed_grad))
    if constants is None:
        late_rows, late_columns = made[0], made[1][None]
        late_place = jnp.zeros_like(late_place)
    else:
        late_columns = constants[1]
        late_rows = call(
            fetch_place_kernel,
            pltpu.VMEM(constants[0].shape[1:], BF16),
            [pltpu.SemaphoreType.DMA((1,))],
            0,
            [late_place],
            [constants[0]],
        )
    late_modes, mixed_grad = lax.optimization_barrier((modes, mixed_grad))
    pairs = call(
        functools.partial(pairs_kernel, devices),
        pltpu.VMEM((lat_count * slots, 2 * channels), BF16),
        [modes_landing, spread_shape, block_sems],
        0,
        [lat_weight],
        [late_modes],
    )
    grads = exchange(mixed_grad.reshape(block_shape)).reshape(mode_shape.shape)
    gfield, filter_part = call(
        functools.partial(gradient_kernel, devices),
        [
            jax.ShapeDtypeStruct((devices, mode_rows + (extra if joined else 0), channels), BF16),
            jax.ShapeDtypeStruct((MODES, channels), F32),
        ],
        [
            modes_landing,
            pltpu.VMEM(late_columns.shape[1:], BF16),
            spread_shape,
            spread_shape,
            block_sems,
            pltpu.SemaphoreType.DMA((1,)),
        ],
        3 * leg_flops,
        [
            held(pairs),
            held(late_rows),
            degree_filter,
            lat_weight,
            alpha,
            weight_part,
            late_place,
        ],
        [grads, late_columns],
    )
    gfield = exchange(gfield)
    if joined:
        sums = call(
            total_kernel, jax.ShapeDtypeStruct((devices, extra, channels), BF16), [], 0, [gfield]
        )
        grad_filter, grad_weight = call(
            finish_kernel,
            [
                jax.ShapeDtypeStruct((MODES, channels), F32),
                jax.ShapeDtypeStruct((2 * channels, channels), F32),
            ],
            [],
            0,
            [exchange(sums)],
        )
    else:
        grad_filter = sum_over_space(filter_part, devices) * 0.125
        grad_weight = sum_over_space(weight_part, devices) * (1.0 / MODES)
    grad_in = call(
        functools.partial(synthesis_kernel, slots),
        jax.ShapeDtypeStruct(grid_in.shape, BF16),
        [
            pltpu.VMEM(upstream.shape, BF16),
            pltpu.VMEM(dft_rows.shape, BF16),
            modes_scratch,
            pltpu.SemaphoreType.DMA((2 + lats,)),
        ],
        dft_flops,
        [gfield.reshape(devices // 2, 2, -1, channels)],
        [upstream, dft_rows],
    )
    return (grad_in, grad_weight.reshape(2, channels, channels), grad_filter)


def solution(mesh):
    return jax.shard_map(
        body,
        mesh=mesh,
        in_specs=(P(("groups", "space"), None, None), P(("groups", "space"), None, None), P(), P()),
        out_specs=(P(("groups", "space"), None, None), P("groups", None, None), P("groups", None)),
        check_vma=False,
    )
```

```python
import functools
import math

import jax
import jax.numpy as jnp
import ml_dtypes
import numpy as np
from jax import lax
from jax.experimental import pallas as pl
from jax.experimental.pallas import tpu as pltpu
from jax.sharding import PartitionSpec as P

MODES = 512
TABLE_BYTES = 64 * 1024 * 1024
VMEM_BYTES = 18 * 1024 * 1024
DELAY = 4
BF16 = jnp.bfloat16
F32 = jnp.float32


def latitude_angles(lat_count):
    lat_index = jnp.arange(lat_count, dtype=jnp.float32)
    return math.pi * (lat_index + 0.5) / lat_count


def legendre_rows(m_values, lat_count, mode_count):
    angles = latitude_angles(lat_count)
    cosine = jnp.cos(angles)[None, :]
    sine_lat = jnp.sin(angles)[None, :]
    orders = m_values.astype(jnp.float32)[:, None]
    log_start = 0.5 * (jnp.log(2.0 * orders + 1.0) - math.log(2.0))
    log_start = log_start + 0.5 * (
        lax.lgamma(2.0 * orders + 1.0) - 2.0 * lax.lgamma(orders + 1.0) - orders * math.log(4.0)
    )
    log_start = log_start + orders * jnp.log(sine_lat)

    def degree_block(carry, block_index):
        p_now, p_prev, log_scale = carry
        outputs = []
        for inner_step in range(32):
            degree = (block_index * 32 + inner_step).astype(jnp.float32)
            active = degree > orders
            denom = jnp.maximum(degree * degree - orders * orders, 1.0)
            coef_a = jnp.sqrt((4.0 * degree * degree - 1.0) / denom)
            lower = jnp.maximum((degree - 1.0) * (degree - 1.0) - orders * orders, 0.0)
            coef_b = jnp.sqrt(
                lower * (2.0 * degree + 1.0) / (jnp.maximum(2.0 * degree - 3.0, 1.0) * denom)
            )
            p_next = jnp.where(active, coef_a * cosine * p_now - coef_b * p_prev, p_now)
            p_prev = jnp.where(active, p_now, p_prev)
            p_now = p_next
            outputs.append(jnp.where(degree >= orders, p_now * jnp.exp(log_scale), 0.0))
        magnitude = jnp.maximum(jnp.abs(p_now), jnp.abs(p_prev))
        next_carry = (p_now / magnitude, p_prev / magnitude, log_scale + jnp.log(magnitude))
        return (next_carry, jnp.stack(outputs, 1))

    ones_grid = jnp.ones((m_values.shape[0], lat_count), jnp.float32)
    start_carry = (ones_grid, jnp.zeros_like(ones_grid), log_start * ones_grid)
    block_ids = jnp.arange(mode_count // 32, dtype=jnp.int32)
    final_carry, stacked = lax.scan(degree_block, start_carry, block_ids)
    return jnp.transpose(stacked, (1, 0, 2, 3)).reshape(m_values.shape[0], mode_count, lat_count)


@functools.lru_cache(maxsize=2)
def legendre_constant(lat_count, mode_count):
    angles = np.pi * (np.arange(lat_count) + 0.5) / lat_count
    cosine = np.cos(angles)[None, :]
    orders = np.arange(mode_count, dtype=np.float64)[:, None]
    gamma_2m = np.array([math.lgamma(2.0 * m + 1.0) for m in range(mode_count)])[:, None]
    gamma_m = np.array([math.lgamma(m + 1.0) for m in range(mode_count)])[:, None]
    log_scale = 0.5 * np.log((2.0 * orders + 1.0) / 2.0)
    log_scale = log_scale + 0.5 * (gamma_2m - 2.0 * gamma_m - orders * math.log(4.0))
    log_scale = log_scale + orders * np.log(np.sin(angles))[None, :]
    p_now, p_prev = np.ones_like(log_scale), np.zeros_like(log_scale)
    table = np.zeros((mode_count, mode_count, lat_count), ml_dtypes.bfloat16)
    for degree in range(mode_count):
        active = degree > orders
        denom = np.maximum(degree * degree - orders * orders, 1.0)
        coef_a = np.sqrt(max(4.0 * degree * degree - 1.0, 0.0) / denom)
        lower = np.maximum((degree - 1.0) ** 2 - orders * orders, 0.0)
        coef_b = np.sqrt(lower * (2.0 * degree + 1.0) / (max(2.0 * degree - 3.0, 1.0) * denom))
        p_next = np.where(active, coef_a * cosine * p_now - coef_b * p_prev, p_now)
        p_prev = np.where(active, p_now, p_prev)
        p_now = p_next
        value = np.where(degree >= orders, p_now * np.exp(log_scale), 0.0)
        table[:, degree, :] = value.astype(np.float32).astype(ml_dtypes.bfloat16)
        if degree % 32 == 31:
            magnitude = np.maximum(np.abs(p_now), np.abs(p_prev))
            p_now, p_prev = p_now / magnitude, p_prev / magnitude
            log_scale = log_scale + np.log(magnitude)
    return table


@functools.lru_cache(maxsize=2)
def fourier_constant(devices, lon_count):
    half, slots = lon_count // 2, MODES // devices
    tables = []
    for parity in range(2):
        owner = 2 * np.arange(devices // 2)[:, None] + parity
        orders = (np.arange(slots)[None, :] * devices + owner).reshape(-1)
        phases = (orders[None, :] * np.arange(half)[:, None]) % lon_count
        angles = 2.0 * np.pi / lon_count * phases
        both = np.concatenate([np.cos(angles), -np.sin(angles)], 1) / math.sqrt(lon_count)
        tables.append(both.astype(np.float32).astype(ml_dtypes.bfloat16))
    table = np.stack(tables, 0)
    return np.ascontiguousarray(table), np.ascontiguousarray(table.transpose(0, 2, 1))


def degree_starts(devices):
    firsts = [slot * devices // 16 * 16 for slot in range(MODES // devices)]
    rows = [MODES - first for first in firsts]
    offsets = [sum(rows[:slot]) for slot in range(len(rows))]
    return firsts, offsets, sum(rows)


@functools.lru_cache(maxsize=2)
def packed_legendre(devices, lat_count):
    firsts, offsets, total = degree_starts(devices)
    table = legendre_constant(lat_count, MODES)
    packed = np.concatenate(
        [
            table[slot * devices : (slot + 1) * devices, first:]
            for slot, first in enumerate(firsts)
        ],
        1,
    )
    return np.ascontiguousarray(packed), np.ascontiguousarray(packed.transpose(0, 2, 1))


def table_constants(devices, lat_count):
    _, _, total = degree_starts(devices)
    if devices * total * 2 * (lat_count + max(lat_count, 128)) > TABLE_BYTES:
        return None
    return tuple(jnp.asarray(table) for table in packed_legendre(devices, lat_count))


def made_tables(devices, lat_count, me):
    firsts, _, _ = degree_starts(devices)
    slot_orders = jnp.arange(MODES // devices, dtype=jnp.int32) * devices + me
    legendre = legendre_rows(slot_orders, lat_count, MODES).astype(BF16)
    rows = jnp.concatenate([legendre[slot, first:] for slot, first in enumerate(firsts)], 0)
    return rows, rows.T


def mixing_matrix(mix_weight):
    upper = jnp.concatenate([mix_weight[0], mix_weight[1]], 1)
    lower = jnp.concatenate([-mix_weight[1], mix_weight[0]], 1)
    return jnp.concatenate([upper, lower], 0)


def gelu_slope(field):
    return 0.5 * (1.0 + lax.erf(field * (1.0 / math.sqrt(2.0)))) + field * jnp.exp(
        -0.5 * field * field
    ) * (1.0 / math.sqrt(2.0 * math.pi))


def dot(left, right):
    return jnp.dot(left, right, preferred_element_type=F32)


def row_chunks(count):
    size = count // 3 if count % 48 == 0 else count
    return [(start, size) for start in range(0, count, size)]


def store_rows(out_ref, slots, parity, lat, part, value):
    start = (2 * lat + part) * slots
    out_ref[:, parity, start : start + slots, :] = value.reshape(-1, slots, value.shape[1])


def load_rows(ref, slots, parity, lat, part):
    start = (2 * lat + part) * slots
    return ref[:, parity, start : start + slots, :].reshape(-1, ref.shape[3])


def load_pair(ref, slots, parity, lat):
    return jnp.concatenate([load_rows(ref, slots, parity, lat, part) for part in range(2)], 1)


def fetch_kernel(*refs):
    count = (len(refs) - 1) // 2
    sems = refs[-1]
    copies = [
        pltpu.make_async_copy(refs[index], refs[count + index], sems.at[index])
        for index in range(count)
    ]
    for copy in copies:
        copy.start()
    for copy in copies:
        copy.wait()


def fetch_place_kernel(place_ref, source_hbm, out_ref, sems):
    copy = pltpu.make_async_copy(source_hbm.at[place_ref[0]], out_ref, sems.at[0])
    copy.start()
    copy.wait()


def analyse_kernel(
    slots, grid_hbm, columns_hbm, out_ref, grid_ref, columns_ref, folded_ref, sems
):
    lats, lon_count, channels = grid_ref.shape
    half = lon_count // 2
    block = columns_ref.shape[1] // 2
    grid_copies = [
        pltpu.make_async_copy(grid_hbm.at[lat], grid_ref.at[lat], sems.at[lat])
        for lat in range(lats)
    ]
    table_copies = [
        pltpu.make_async_copy(
            columns_hbm.at[parity, part * block : (part + 1) * block, :],
            columns_ref.at[parity, part * block : (part + 1) * block, :],
            sems.at[lats + 2 * parity + part],
        )
        for parity in range(2)
        for part in range(2)
    ]
    for copy in grid_copies + table_copies:
        copy.start()
    for lat in range(lats):
        grid_copies[lat].wait()
        near = grid_ref[lat, :half, :].astype(F32)
        far = grid_ref[lat, half:, :].astype(F32)
        folded_ref[0, :, lat * channels : (lat + 1) * channels] = (near + far).astype(BF16)
        folded_ref[1, :, lat * channels : (lat + 1) * channels] = (near - far).astype(BF16)
    for parity in range(2):
        for part in range(2):
            table_copies[2 * parity + part].wait()
            result = dot(
                columns_ref[parity, part * block : (part + 1) * block, :], folded_ref[parity]
            ).astype(BF16)
            for lat in range(lats):
                lanes = slice(lat * channels, (lat + 1) * channels)
                store_rows(out_ref, slots, parity, lat, part, result[:, lanes])


def slot_rows(ref, part, slot, slots, lats):
    return ref[pl.ds(part * slots + slot, lats, stride=ref.shape[0] // lats), :]


def slot_pair(ref, slot, slots, lats, scale):
    return jnp.concatenate(
        [(slot_rows(ref, part, slot, slots, lats) * scale).astype(BF16) for part in range(2)], 1
    )


def slot_halves(slots):
    size = slots // 2 if slots % 32 == 0 else slots
    return [(start, size) for start in range(0, slots, size)]


class Spread:
    def __init__(self, slots, spread_ref, array_ref):
        lats, self.rows, channels = array_ref.shape
        self.slots = slots
        self.halves = slot_halves(slots)
        self.spread_ref = spread_ref.reshape(lats, spread_ref.shape[0] // lats, channels)
        self.array_ref = array_ref

    def need(self, slot):
        for start, size in self.halves:
            if slot == start:
                for part in range(2):
                    begin = part * self.slots + start
                    span = slice(begin, begin + size)
                    self.spread_ref[:, span, :] = self.array_ref[:, span, :].astype(F32)


def staggered(count, delay, first_stage, second_stage):
    waiting = []
    for index in range(count):
        waiting.append((index, first_stage(index)))
        if len(waiting) > delay:
            second_stage(*waiting.pop(0))
    for item in waiting:
        second_stage(*item)


def spectrum_kernel(
    devices,
    modes_ref,
    rows_ref,
    gain_ref,
    weight_ref,
    alpha_ref,
    place_ref,
    columns_hbm,
    out_hbm,
    columns_ref,
    in_s,
    out_s,
    out_ref,
    columns_sem,
    out_sems,
):
    columns_copy = pltpu.make_async_copy(
        columns_hbm.at[place_ref[0]], columns_ref, columns_sem.at[0]
    )
    columns_copy.start()
    slots = MODES // devices
    lats = weight_ref.shape[0]
    firsts, offsets, _ = degree_starts(devices)
    landing = Spread(slots, in_s, modes_ref)
    stores = []
    gain = gain_ref[...]
    channels = gain.shape[1]
    lat_weight = weight_ref[...]

    def forward(slot):
        first, offset = firsts[slot], offsets[slot]
        landing.need(slot)
        modes = slot_pair(in_s, slot, slots, lats, lat_weight)
        spectrum = dot(rows_ref[offset : offset + MODES - first, :], modes).astype(BF16)
        return spectrum * jnp.concatenate([gain[first:], gain[first:]], 1)

    def back(slot, scaled):
        first, offset = firsts[slot], offsets[slot]
        if slot == 0:
            columns_copy.wait()
        result = dot(columns_ref[:, offset : offset + MODES - first], scaled)
        result = result * (alpha_ref[...] if slot == 0 else 2.0)
        for part in range(2):
            out_s[pl.ds(part * slots + slot, lats, stride=out_s.shape[0] // lats), :] = result[
                :, part * channels : (part + 1) * channels
            ]
        for start, size in landing.halves:
            if slot == start + size - 1:
                store(start, size)

    def store(start, size):
        view = out_s.reshape(lats, out_s.shape[0] // lats, channels)
        for part in range(2):
            span = slice(part * slots + start, part * slots + start + size)
            out_ref[:, span, :] = view[:, span, :].astype(BF16)
            if size < slots:
                copy = pltpu.make_async_copy(
                    out_ref.at[:, span, :], out_hbm.at[:, span, :], out_sems.at[len(stores)]
                )
                copy.start()
                stores.append(copy)
        if size == slots:
            copy = pltpu.make_async_copy(out_ref, out_hbm, out_sems.at[0])
            copy.start()
            stores.append(copy)

    staggered(slots, DELAY, forward, back)
    for copy in stores:
        copy.wait()


def pairs_kernel(devices, weight_ref, modes_ref, out_ref, in_s):
    slots = MODES // devices
    lats = weight_ref.shape[0]
    landing = Spread(slots, in_s, modes_ref)
    lat_weight = weight_ref[...]
    for slot in range(slots):
        landing.need(slot)
        out_ref[slot * lats : (slot + 1) * lats, :] = slot_pair(
            in_s, slot, slots, lats, lat_weight
        )


def gradient_kernel(
    devices,
    grads_ref,
    rows_ref,
    gain_ref,
    weight_ref,
    alpha_ref,
    part_ref,
    place_ref,
    pairs_hbm,
    columns_hbm,
    out_ref,
    filter_ref,
    pairs_ref,
    columns_ref,
    grad_s,
    out_s,
    pairs_sems,
    columns_sem,
):
    slots = MODES // devices
    lats = weight_ref.shape[0]
    firsts, offsets, _ = degree_starts(devices)
    columns_copy = pltpu.make_async_copy(
        columns_hbm.at[place_ref[0]], columns_ref, columns_sem.at[0]
    )
    pairs_copies = {}
    for index, (start, size) in enumerate(slot_halves(slots)):
        span = slice(start * lats, (start + size) * lats)
        pairs_copies[start] = pltpu.make_async_copy(
            pairs_hbm.at[span, :], pairs_ref.at[span, :], pairs_sems.at[index]
        )
    for copy in [*pairs_copies.values(), columns_copy]:
        copy.start()
    landing = Spread(slots, grad_s, grads_ref)
    gain = gain_ref[...].astype(F32)
    lat_weight = weight_ref[...]
    channels = gain.shape[1]
    filter_ref[...] = jnp.zeros_like(filter_ref)

    def forward(slot):
        first, offset = firsts[slot], offsets[slot]
        landing.need(slot)
        if slot in pairs_copies:
            pairs_copies[slot].wait()
        scale = alpha_ref[:, :channels] if slot == 0 else 2.0
        modes = pairs_ref[slot * lats : (slot + 1) * lats, :]
        grads = slot_pair(grad_s, slot, slots, lats, scale)
        table = rows_ref[offset : offset + MODES - first, :]
        spectrum = dot(table, modes)
        gscaled = dot(table, grads)
        product = gscaled * spectrum
        filter_ref[first:, :] += product[:, :channels] + product[:, channels:]
        return (gscaled * jnp.concatenate([gain[first:], gain[first:]], 1)).astype(BF16)

    def back(slot, gspectrum):
        first, offset = firsts[slot], offsets[slot]
        if slot == 0:
            columns_copy.wait()
        result = dot(columns_ref[:, offset : offset + MODES - first], gspectrum)
        for part in range(2):
            out_s[pl.ds(part * slots + slot, lats, stride=out_s.shape[0] // lats), :] = (
                result[:, part * channels : (part + 1) * channels] * lat_weight
            )

    staggered(slots, DELAY, forward, back)
    rows = lats // devices * 2 * slots
    view = out_s.reshape(lats, out_s.shape[0] // lats, channels)
    out_ref[:, :rows, :] = (
        view[:, : 2 * slots, :].astype(BF16).reshape(devices, rows, channels)
    )
    if out_ref.shape[1] > rows:
        split = rows + MODES // devices
        out_ref[:, rows:split, :] = (
            filter_ref[...].reshape(devices, MODES // devices, channels).astype(BF16)
        )
        out_ref[:, split:, :] = part_ref[...].reshape(devices, -1, channels).astype(BF16)


def slope_kernel(
    slots,
    modes_ref,
    wide_ref,
    wide_t_ref,
    rows_ref,
    upstream_hbm,
    columns_hbm,
    out_hbm,
    weight_ref,
    upstream_ref,
    columns_ref,
    modes_s,
    folded_s,
    out_ref,
    upstream_sems,
    columns_sems,
    out_sems,
):
    lats, lon_count, channels = upstream_ref.shape
    half = lon_count // 2
    block = modes_s.shape[1] // 2

    def lat_copy(source, target, sem_refs, parity, lat):
        span = slice(2 * lat * slots, 2 * (lat + 1) * slots)
        return pltpu.make_async_copy(
            source.at[:, parity, span, :],
            target.at[:, parity, span, :],
            sem_refs.at[parity * lats + lat],
        )

    places = [(parity, lat) for parity in range(2) for lat in range(lats)]
    upstream_copies = [
        pltpu.make_async_copy(upstream_hbm.at[lat], upstream_ref.at[lat], upstream_sems.at[lat])
        for lat in range(lats)
    ]
    columns_copies = [
        pltpu.make_async_copy(
            columns_hbm.at[parity], columns_ref.at[parity], columns_sems.at[parity]
        )
        for parity in range(2)
    ]
    for copy in upstream_copies + columns_copies:
        copy.start()
    for parity, lat in places:
        mixed = dot(load_pair(modes_ref, slots, parity, lat), wide_ref[...]).astype(BF16)
        for part in range(2):
            modes_s[
                parity,
                part * block : (part + 1) * block,
                lat * channels : (lat + 1) * channels,
            ] = mixed[:, part * channels : (part + 1) * channels]
    for copy in upstream_copies:
        copy.wait()
    for start, size in row_chunks(half):
        even = dot(rows_ref[0, start : start + size, :], modes_s[0])
        odd = dot(rows_ref[1, start : start + size, :], modes_s[1])
        for lat in range(lats):
            lanes = slice(lat * channels, (lat + 1) * channels)
            near = upstream_ref[lat, start : start + size, :].astype(F32) * gelu_slope(
                even[:, lanes] + odd[:, lanes]
            )
            far = upstream_ref[lat, half + start : half + start + size, :].astype(
                F32
            ) * gelu_slope(even[:, lanes] - odd[:, lanes])
            folded_s[0, start : start + size, lanes] = (near + far).astype(BF16)
            folded_s[1, start : start + size, lanes] = (near - far).astype(BF16)
    pairs, stores = [], []
    for parity in range(2):
        columns_copies[parity].wait()
        parts = [
            dot(
                columns_ref[parity, part * block : (part + 1) * block, :], folded_s[parity]
            ).astype(BF16)
            for part in range(2)
        ]
        for lat in range(lats):
            lanes = slice(lat * channels, (lat + 1) * channels)
            pair = jnp.concatenate([parts[0][:, lanes], parts[1][:, lanes]], 1)
            mixed = dot(pair, wide_t_ref[...]).astype(BF16)
            for part in range(2):
                store_rows(
                    out_ref,
                    slots,
                    parity,
                    lat,
                    part,
                    mixed[:, part * channels : (part + 1) * channels],
                )
            stores.append(lat_copy(out_ref, out_hbm, out_sems, parity, lat))
            stores[-1].start()
            pairs.append(pair)
    total = jnp.zeros((2 * channels, 2 * channels), F32)
    for (parity, lat), pair in zip(places, pairs):
        total = total + lax.dot_general(
            load_pair(modes_ref, slots, parity, lat),
            pair,
            (((0,), (0,)), ((), ())),
            preferred_element_type=F32,
        )
    weight_ref[:channels, :] = total[:channels, :channels] + total[channels:, channels:]
    weight_ref[channels:, :] = total[:channels, channels:] - total[channels:, :channels]
    for copy in stores:
        copy.wait()


def synthesis_kernel(
    slots, modes_ref, upstream_hbm, rows_hbm, out_ref, upstream_ref, rows_ref, modes_s, sems
):
    lats, lon_count, channels = upstream_ref.shape
    copies = [
        pltpu.make_async_copy(rows_hbm.at[parity], rows_ref.at[parity], sems.at[parity])
        for parity in range(2)
    ]
    copies += [
        pltpu.make_async_copy(upstream_hbm.at[lat], upstream_ref.at[lat], sems.at[2 + lat])
        for lat in range(lats)
    ]
    for copy in copies:
        copy.start()
    half = lon_count // 2
    block = modes_s.shape[1] // 2
    for parity in range(2):
        for part in range(2):
            for lat in range(lats):
                modes_s[
                    parity,
                    part * block : (part + 1) * block,
                    lat * channels : (lat + 1) * channels,
                ] = load_rows(modes_ref, slots, parity, lat, part)
    for copy in copies:
        copy.wait()
    for start, size in row_chunks(half):
        even = dot(rows_ref[0, start : start + size, :], modes_s[0])
        odd = dot(rows_ref[1, start : start + size, :], modes_s[1])
        for lat in range(lats):
            lanes = slice(lat * channels, (lat + 1) * channels)
            for sign, base in ((1.0, start), (-1.0, half + start)):
                total = even[:, lanes] + sign * odd[:, lanes]
                total = total + upstream_ref[lat, base : base + size, :].astype(F32)
                out_ref[lat, base : base + size, :] = total.astype(BF16)


def total_kernel(received_ref, out_ref):
    rows = out_ref.shape[1]
    start = received_ref.shape[1] - rows
    total = received_ref[0, start:, :].astype(F32)
    for device in range(1, received_ref.shape[0]):
        total = total + received_ref[device, start:, :].astype(F32)
    out_ref[...] = jnp.broadcast_to(total.astype(BF16)[None], out_ref.shape)


def finish_kernel(received_ref, filter_ref, weight_ref):
    devices, rows, channels = received_ref.shape
    split = filter_ref.shape[0] // devices
    filter_ref[...] = (
        received_ref[:, :split, :].astype(F32).reshape(filter_ref.shape) * 0.125
    )
    weight_ref[...] = received_ref[:, split:, :].astype(F32).reshape(weight_ref.shape) * (
        1.0 / MODES
    )


def call(kernel, out_shape, scratch, flops, operands, streamed=(), written=0):
    outs = out_shape if isinstance(out_shape, (list, tuple)) else [out_shape]
    moved = sum(2 * math.prod(array.shape) for array in [*operands, *streamed, *outs])
    specs = [
        pl.BlockSpec(memory_space=pl.ANY if index < written else pltpu.VMEM)
        for index in range(len(outs))
    ]
    return pl.pallas_call(
        kernel,
        out_shape=out_shape,
        in_specs=[
            pl.BlockSpec(memory_space=pltpu.SMEM if array.dtype == jnp.int32 else pltpu.VMEM)
            for array in operands
        ]
        + [pl.BlockSpec(memory_space=pl.ANY)] * len(streamed),
        out_specs=specs if isinstance(out_shape, (list, tuple)) else specs[0],
        scratch_shapes=scratch,
        cost_estimate=pl.CostEstimate(flops=flops, bytes_accessed=moved, transcendentals=0),
        compiler_params=pltpu.CompilerParams(vmem_limit_bytes=VMEM_BYTES),
    )(*operands, *(away(array) for array in streamed))


def away(array):
    return pltpu.with_memory_space_constraint(array, pltpu.HBM)


def held(array):
    return pltpu.with_memory_space_constraint(array, pltpu.VMEM)


def exchange(array):
    return lax.all_to_all(array, "space", split_axis=0, concat_axis=0, tiled=True)


def sum_over_space(array, devices):
    step = devices // 2
    while step:
        array = array + lax.ppermute(
            array, "space", [(index, index ^ step) for index in range(devices)]
        )
        step //= 2
    return array


def body(grid_in, upstream, mix_weight, degree_filter):
    devices = lax.axis_size("space")
    me = lax.axis_index("space")
    lats, lon_count, channels = grid_in.shape
    lat_count = lats * devices
    slots = MODES // devices
    half = lon_count // 2
    dft_rows, dft_columns = (jnp.asarray(t) for t in fourier_constant(devices, lon_count))
    constants = table_constants(devices, lat_count)
    place = me.reshape(1)
    if constants is None:
        leg_rows, leg_columns = made_tables(devices, lat_count, me)
        leg_columns = leg_columns[None]
        place = jnp.zeros_like(place)
    else:
        leg_rows = lax.dynamic_index_in_dim(constants[0], me, 0, keepdims=False)
        leg_columns = constants[1]
    angles = np.pi * (np.arange(lat_count) + 0.5) / lat_count
    lat_weight = jnp.asarray(
        np.broadcast_to((np.pi / lat_count * np.sin(angles))[:, None], (lat_count, channels)), F32
    )
    alpha = jnp.where(me == 0, 1.0, 2.0) * jnp.ones((1, 2 * channels), F32)
    wide = mixing_matrix(mix_weight)
    mode_rows = lats * 2 * slots
    grid_shape = jax.ShapeDtypeStruct((devices // 2, 2, mode_rows, channels), BF16)
    grid_out = pltpu.HBM(grid_shape.shape, BF16)
    block_shape = (devices, mode_rows, channels)
    mode_shape = jax.ShapeDtypeStruct((lat_count, 2 * slots, channels), BF16)
    spread_shape = pltpu.VMEM((lat_count * (2 * slots + 8), channels), F32)
    modes_scratch = pltpu.VMEM((2, MODES, lats * channels), BF16)
    folded_scratch = pltpu.VMEM((2, half, lats * channels), BF16)
    dft_flops = 2 * MODES * lon_count * lats * channels
    leg_flops = 4 * degree_starts(devices)[2] * lat_count * channels
    modes_landing = pltpu.VMEM(mode_shape.shape, BF16)
    columns_landing = pltpu.VMEM(leg_columns.shape[1:], BF16)
    weight_rows = 2 * channels // devices
    extra = MODES // devices + weight_rows
    joined = (MODES // devices) % 16 == 0 and weight_rows % 16 == 0

    fourier = call(
        functools.partial(analyse_kernel, slots),
        grid_out,
        [
            pltpu.VMEM(grid_in.shape, BF16),
            pltpu.VMEM(dft_columns.shape, BF16),
            folded_scratch,
            pltpu.SemaphoreType.DMA((lats + 4,)),
        ],
        dft_flops,
        [],
        [grid_in, dft_columns],
    )
    held_rows = held(
        call(
            fetch_kernel,
            pltpu.VMEM(dft_rows.shape, BF16),
            [pltpu.SemaphoreType.DMA((1,))],
            0,
            [],
            [dft_rows],
        )
    )
    modes = exchange(fourier.reshape(block_shape)).reshape(mode_shape.shape)
    returned = call(
        functools.partial(spectrum_kernel, devices),
        pltpu.HBM(mode_shape.shape, BF16),
        [
            columns_landing,
            spread_shape,
            spread_shape,
            modes_landing,
            pltpu.SemaphoreType.DMA((1,)),
            pltpu.SemaphoreType.DMA((4,)),
        ],
        2 * leg_flops,
        [held(modes), held(leg_rows), degree_filter, lat_weight, alpha, place],
        [leg_columns],
        written=1,
    )
    returned = exchange(returned.reshape(block_shape)).reshape(grid_shape.shape)
    grid_landing = pltpu.VMEM(grid_shape.shape, BF16)
    mixed_grad, weight_part = call(
        functools.partial(slope_kernel, slots),
        [grid_out, jax.ShapeDtypeStruct((2 * channels, channels), F32)],
        [
            pltpu.VMEM(upstream.shape, BF16),
            pltpu.VMEM(dft_columns.shape, BF16),
            modes_scratch,
            folded_scratch,
            grid_landing,
            pltpu.SemaphoreType.DMA((lats,)),
            pltpu.SemaphoreType.DMA((2,)),
            pltpu.SemaphoreType.DMA((2 * lats,)),
        ],
        2 * dft_flops,
        [held(returned), wide, wide.T, held_rows],
        [upstream, dft_columns],
        written=1,
    )
    late_place, late_modes, mixed_grad = lax.optimization_barrier((place, modes, mixed_grad))
    late_rows = leg_rows
    if constants is not None:
        late_rows = call(
            fetch_place_kernel,
            pltpu.VMEM(leg_rows.shape, BF16),
            [pltpu.SemaphoreType.DMA((1,))],
            0,
            [late_place],
            [constants[0]],
        )
    pairs = call(
        functools.partial(pairs_kernel, devices),
        pltpu.HBM((lat_count * slots, 2 * channels), BF16),
        [spread_shape],
        0,
        [lat_weight, away(late_modes)],
    )
    grads = exchange(mixed_grad.reshape(block_shape)).reshape(mode_shape.shape)
    gfield, filter_part = call(
        functools.partial(gradient_kernel, devices),
        [
            jax.ShapeDtypeStruct((devices, mode_rows + (extra if joined else 0), channels), BF16),
            jax.ShapeDtypeStruct((MODES, channels), F32),
        ],
        [
            pltpu.VMEM(pairs.shape, BF16),
            columns_landing,
            spread_shape,
            spread_shape,
            pltpu.SemaphoreType.DMA((2,)),
            pltpu.SemaphoreType.DMA((1,)),
        ],
        3 * leg_flops,
        [
            held(grads),
            held(late_rows),
            degree_filter,
            lat_weight,
            alpha,
            weight_part,
            late_place,
        ],
        [pairs, leg_columns],
    )
    gfield = exchange(gfield)
    if joined:
        sums = call(
            total_kernel, jax.ShapeDtypeStruct((devices, extra, channels), BF16), [], 0, [gfield]
        )
        grad_filter, grad_weight = call(
            finish_kernel,
            [
                jax.ShapeDtypeStruct((MODES, channels), F32),
                jax.ShapeDtypeStruct((2 * channels, channels), F32),
            ],
            [],
            0,
            [exchange(sums)],
        )
    else:
        grad_filter = sum_over_space(filter_part, devices) * 0.125
        grad_weight = sum_over_space(weight_part, devices) * (1.0 / MODES)
    grad_in = call(
        functools.partial(synthesis_kernel, slots),
        jax.ShapeDtypeStruct(grid_in.shape, BF16),
        [
            pltpu.VMEM(upstream.shape, BF16),
            pltpu.VMEM(dft_rows.shape, BF16),
            modes_scratch,
            pltpu.SemaphoreType.DMA((2 + lats,)),
        ],
        dft_flops,
        [gfield.reshape(devices // 2, 2, -1, channels)],
        [upstream, dft_rows],
    )
    return (grad_in, grad_weight.reshape(2, channels, channels), grad_filter)


def solution(mesh):
    return jax.shard_map(
        body,
        mesh=mesh,
        in_specs=(P(("groups", "space"), None, None), P(("groups", "space"), None, None), P(), P()),
        out_specs=(P(("groups", "space"), None, None), P("groups", None, None), P("groups", None)),
        check_vma=False,
    )
```

```python
import functools
import math

import jax
import jax.numpy as jnp
import ml_dtypes
import numpy as np
from jax import lax
from jax.experimental import pallas as pl
from jax.experimental.pallas import tpu as pltpu
from jax.sharding import PartitionSpec as P

MODES = 512
TABLE_BYTES = 64 * 1024 * 1024
VMEM_BYTES = 18 * 1024 * 1024
DELAY = 7
BF16 = jnp.bfloat16
F32 = jnp.float32


def latitude_angles(lat_count):
    lat_index = jnp.arange(lat_count, dtype=jnp.float32)
    return math.pi * (lat_index + 0.5) / lat_count


def legendre_rows(m_values, lat_count, mode_count):
    angles = latitude_angles(lat_count)
    cosine = jnp.cos(angles)[None, :]
    sine_lat = jnp.sin(angles)[None, :]
    orders = m_values.astype(jnp.float32)[:, None]
    log_start = 0.5 * (jnp.log(2.0 * orders + 1.0) - math.log(2.0))
    log_start = log_start + 0.5 * (
        lax.lgamma(2.0 * orders + 1.0) - 2.0 * lax.lgamma(orders + 1.0) - orders * math.log(4.0)
    )
    log_start = log_start + orders * jnp.log(sine_lat)

    def degree_block(carry, block_index):
        p_now, p_prev, log_scale = carry
        outputs = []
        for inner_step in range(32):
            degree = (block_index * 32 + inner_step).astype(jnp.float32)
            active = degree > orders
            denom = jnp.maximum(degree * degree - orders * orders, 1.0)
            coef_a = jnp.sqrt((4.0 * degree * degree - 1.0) / denom)
            lower = jnp.maximum((degree - 1.0) * (degree - 1.0) - orders * orders, 0.0)
            coef_b = jnp.sqrt(
                lower * (2.0 * degree + 1.0) / (jnp.maximum(2.0 * degree - 3.0, 1.0) * denom)
            )
            p_next = jnp.where(active, coef_a * cosine * p_now - coef_b * p_prev, p_now)
            p_prev = jnp.where(active, p_now, p_prev)
            p_now = p_next
            outputs.append(jnp.where(degree >= orders, p_now * jnp.exp(log_scale), 0.0))
        magnitude = jnp.maximum(jnp.abs(p_now), jnp.abs(p_prev))
        next_carry = (p_now / magnitude, p_prev / magnitude, log_scale + jnp.log(magnitude))
        return (next_carry, jnp.stack(outputs, 1))

    ones_grid = jnp.ones((m_values.shape[0], lat_count), jnp.float32)
    start_carry = (ones_grid, jnp.zeros_like(ones_grid), log_start * ones_grid)
    block_ids = jnp.arange(mode_count // 32, dtype=jnp.int32)
    final_carry, stacked = lax.scan(degree_block, start_carry, block_ids)
    return jnp.transpose(stacked, (1, 0, 2, 3)).reshape(m_values.shape[0], mode_count, lat_count)


@functools.lru_cache(maxsize=2)
def legendre_constant(lat_count, mode_count):
    angles = np.pi * (np.arange(lat_count) + 0.5) / lat_count
    cosine = np.cos(angles)[None, :]
    orders = np.arange(mode_count, dtype=np.float64)[:, None]
    gamma_2m = np.array([math.lgamma(2.0 * m + 1.0) for m in range(mode_count)])[:, None]
    gamma_m = np.array([math.lgamma(m + 1.0) for m in range(mode_count)])[:, None]
    log_scale = 0.5 * np.log((2.0 * orders + 1.0) / 2.0)
    log_scale = log_scale + 0.5 * (gamma_2m - 2.0 * gamma_m - orders * math.log(4.0))
    log_scale = log_scale + orders * np.log(np.sin(angles))[None, :]
    p_now, p_prev = np.ones_like(log_scale), np.zeros_like(log_scale)
    table = np.zeros((mode_count, mode_count, lat_count), ml_dtypes.bfloat16)
    for degree in range(mode_count):
        active = degree > orders
        denom = np.maximum(degree * degree - orders * orders, 1.0)
        coef_a = np.sqrt(max(4.0 * degree * degree - 1.0, 0.0) / denom)
        lower = np.maximum((degree - 1.0) ** 2 - orders * orders, 0.0)
        coef_b = np.sqrt(lower * (2.0 * degree + 1.0) / (max(2.0 * degree - 3.0, 1.0) * denom))
        p_next = np.where(active, coef_a * cosine * p_now - coef_b * p_prev, p_now)
        p_prev = np.where(active, p_now, p_prev)
        p_now = p_next
        value = np.where(degree >= orders, p_now * np.exp(log_scale), 0.0)
        table[:, degree, :] = value.astype(np.float32).astype(ml_dtypes.bfloat16)
        if degree % 32 == 31:
            magnitude = np.maximum(np.abs(p_now), np.abs(p_prev))
            p_now, p_prev = p_now / magnitude, p_prev / magnitude
            log_scale = log_scale + np.log(magnitude)
    return table


@functools.lru_cache(maxsize=2)
def fourier_constant(devices, lon_count):
    half, slots = lon_count // 2, MODES // devices
    tables = []
    for parity in range(2):
        owner = 2 * np.arange(devices // 2)[:, None] + parity
        orders = (np.arange(slots)[None, :] * devices + owner).reshape(-1)
        phases = (orders[None, :] * np.arange(half)[:, None]) % lon_count
        angles = 2.0 * np.pi / lon_count * phases
        both = np.concatenate([np.cos(angles), -np.sin(angles)], 1) / math.sqrt(lon_count)
        tables.append(both.astype(np.float32).astype(ml_dtypes.bfloat16))
    table = np.stack(tables, 0)
    return np.ascontiguousarray(table), np.ascontiguousarray(table.transpose(0, 2, 1))


def degree_starts(devices):
    firsts = [slot * devices // 16 * 16 for slot in range(MODES // devices)]
    rows = [MODES - first for first in firsts]
    offsets = [sum(rows[:slot]) for slot in range(len(rows))]
    return firsts, offsets, sum(rows)


@functools.lru_cache(maxsize=2)
def packed_legendre(devices, lat_count):
    firsts, offsets, total = degree_starts(devices)
    table = legendre_constant(lat_count, MODES)
    packed = np.concatenate(
        [
            table[slot * devices : (slot + 1) * devices, first:]
            for slot, first in enumerate(firsts)
        ],
        1,
    )
    return np.ascontiguousarray(packed), np.ascontiguousarray(packed.transpose(0, 2, 1))


def table_constants(devices, lat_count):
    _, _, total = degree_starts(devices)
    if devices * total * 2 * (lat_count + max(lat_count, 128)) > TABLE_BYTES:
        return None
    return tuple(jnp.asarray(table) for table in packed_legendre(devices, lat_count))


def made_tables(devices, lat_count, me):
    firsts, _, _ = degree_starts(devices)
    slot_orders = jnp.arange(MODES // devices, dtype=jnp.int32) * devices + me
    legendre = legendre_rows(slot_orders, lat_count, MODES).astype(BF16)
    rows = jnp.concatenate([legendre[slot, first:] for slot, first in enumerate(firsts)], 0)
    return rows, rows.T


def mixing_matrix(mix_weight):
    upper = jnp.concatenate([mix_weight[0], mix_weight[1]], 1)
    lower = jnp.concatenate([-mix_weight[1], mix_weight[0]], 1)
    return jnp.concatenate([upper, lower], 0)


def gelu_slope(field):
    return 0.5 * (1.0 + lax.erf(field * (1.0 / math.sqrt(2.0)))) + field * jnp.exp(
        -0.5 * field * field
    ) * (1.0 / math.sqrt(2.0 * math.pi))


def dot(left, right):
    return jnp.dot(left, right, preferred_element_type=F32)


def row_chunks(count):
    size = count // 3 if count % 48 == 0 else count
    return [(start, size) for start in range(0, count, size)]


def store_rows(out_ref, slots, parity, lat, part, value):
    start = (2 * lat + part) * slots
    out_ref[:, parity, start : start + slots, :] = value.reshape(-1, slots, value.shape[1])


def load_rows(ref, slots, parity, lat, part):
    start = (2 * lat + part) * slots
    return ref[:, parity, start : start + slots, :].reshape(-1, ref.shape[3])


def load_pair(ref, slots, parity, lat):
    return jnp.concatenate([load_rows(ref, slots, parity, lat, part) for part in range(2)], 1)


def fetch_kernel(*refs):
    count = (len(refs) - 1) // 2
    sems = refs[-1]
    copies = [
        pltpu.make_async_copy(refs[index], refs[count + index], sems.at[index])
        for index in range(count)
    ]
    for copy in copies:
        copy.start()
    for copy in copies:
        copy.wait()


def fetch_place_kernel(place_ref, source_hbm, out_ref, sems):
    copy = pltpu.make_async_copy(
        source_hbm.at[place_ref[0], : out_ref.shape[0], :], out_ref, sems.at[0]
    )
    copy.start()
    copy.wait()


def analyse_kernel(
    slots, grid_hbm, columns_hbm, out_ref, grid_ref, columns_ref, folded_ref, sems
):
    lats, lon_count, channels = grid_ref.shape
    half = lon_count // 2
    block = columns_ref.shape[1] // 2
    grid_copies = [
        pltpu.make_async_copy(grid_hbm.at[lat], grid_ref.at[lat], sems.at[lat])
        for lat in range(lats)
    ]
    table_copies = [
        pltpu.make_async_copy(
            columns_hbm.at[parity, part * block : (part + 1) * block, :],
            columns_ref.at[parity, part * block : (part + 1) * block, :],
            sems.at[lats + 2 * parity + part],
        )
        for parity in range(2)
        for part in range(2)
    ]
    for copy in grid_copies + table_copies:
        copy.start()
    for lat in range(lats):
        grid_copies[lat].wait()
        near = grid_ref[lat, :half, :].astype(F32)
        far = grid_ref[lat, half:, :].astype(F32)
        folded_ref[0, :, lat * channels : (lat + 1) * channels] = (near + far).astype(BF16)
        folded_ref[1, :, lat * channels : (lat + 1) * channels] = (near - far).astype(BF16)
    for parity in range(2):
        for part in range(2):
            table_copies[2 * parity + part].wait()
        result = dot(columns_ref[parity], folded_ref[parity]).astype(BF16)
        for part in range(2):
            for lat in range(lats):
                lanes = slice(lat * channels, (lat + 1) * channels)
                rows = slice(part * block, (part + 1) * block)
                store_rows(out_ref, slots, parity, lat, part, result[rows, lanes])


def slot_rows(ref, part, slot, slots, lats):
    return ref[pl.ds(part * slots + slot, lats, stride=ref.shape[0] // lats), :]


def slot_pair(ref, slot, slots, lats, scale):
    return jnp.concatenate(
        [(slot_rows(ref, part, slot, slots, lats) * scale).astype(BF16) for part in range(2)], 1
    )


def slot_halves(slots):
    size = slots // 2 if slots % 32 == 0 else slots
    return [(start, size) for start in range(0, slots, size)]


class Spread:
    def __init__(self, slots, spread_ref, array_ref):
        lats, self.rows, channels = array_ref.shape
        self.slots = slots
        self.halves = slot_halves(slots)
        self.spread_ref = spread_ref.reshape(lats, spread_ref.shape[0] // lats, channels)
        self.array_ref = array_ref

    def need(self, slot):
        for start, size in self.halves:
            if slot == start:
                for part in range(2):
                    begin = part * self.slots + start
                    span = slice(begin, begin + size)
                    self.spread_ref[:, span, :] = self.array_ref[:, span, :].astype(F32)


def staggered(count, delay, first_stage, second_stage):
    waiting = []
    for index in range(count):
        waiting.append((index, first_stage(index)))
        if len(waiting) > delay:
            second_stage(*waiting.pop(0))
    for item in waiting:
        second_stage(*item)


def spectrum_kernel(
    devices,
    modes_ref,
    rows_ref,
    gain_ref,
    weight_ref,
    alpha_ref,
    place_ref,
    columns_hbm,
    out_hbm,
    columns_ref,
    in_s,
    out_s,
    out_ref,
    columns_sem,
    out_sems,
):
    columns_copy = pltpu.make_async_copy(
        columns_hbm.at[place_ref[0]], columns_ref, columns_sem.at[0]
    )
    columns_copy.start()
    slots = MODES // devices
    lats = weight_ref.shape[0]
    firsts, offsets, _ = degree_starts(devices)
    landing = Spread(slots, in_s, modes_ref)
    stores = []
    gain = gain_ref[...]
    channels = gain.shape[1]
    lat_weight = weight_ref[...]

    def forward(slot):
        first, offset = firsts[slot], offsets[slot]
        landing.need(slot)
        modes = slot_pair(in_s, slot, slots, lats, lat_weight)
        spectrum = dot(rows_ref[offset : offset + MODES - first, :], modes).astype(BF16)
        return spectrum * jnp.concatenate([gain[first:], gain[first:]], 1)

    def back(slot, scaled):
        first, offset = firsts[slot], offsets[slot]
        if slot == 0:
            columns_copy.wait()
        result = dot(columns_ref[:, offset : offset + MODES - first], scaled)
        result = result * (alpha_ref[...] if slot == 0 else 2.0)
        for part in range(2):
            out_s[pl.ds(part * slots + slot, lats, stride=out_s.shape[0] // lats), :] = result[
                :, part * channels : (part + 1) * channels
            ]
        for start, size in landing.halves:
            if slot == start + size - 1:
                store(start, size)

    def store(start, size):
        view = out_s.reshape(lats, out_s.shape[0] // lats, channels)
        for part in range(2):
            span = slice(part * slots + start, part * slots + start + size)
            out_ref[:, span, :] = view[:, span, :].astype(BF16)
            if size < slots:
                copy = pltpu.make_async_copy(
                    out_ref.at[:, span, :], out_hbm.at[:, span, :], out_sems.at[len(stores)]
                )
                copy.start()
                stores.append(copy)
        if size == slots:
            copy = pltpu.make_async_copy(out_ref, out_hbm, out_sems.at[0])
            copy.start()
            stores.append(copy)

    staggered(slots, DELAY, forward, back)
    for copy in stores:
        copy.wait()


def pairs_kernel(devices, weight_ref, modes_ref, near_ref, far_ref, in_s):
    slots = MODES // devices
    lats = weight_ref.shape[0]
    landing = Spread(slots, in_s, modes_ref)
    lat_weight = weight_ref[...]
    near = near_ref.shape[0] // lats
    for slot in range(slots):
        landing.need(slot)
        pair = slot_pair(in_s, slot, slots, lats, lat_weight)
        if slot < near:
            near_ref[slot * lats : (slot + 1) * lats, :] = pair
        else:
            far_ref[(slot - near) * lats : (slot - near + 1) * lats, :] = pair


def gradient_kernel(
    devices,
    grads_ref,
    near_rows_ref,
    near_pairs_ref,
    gain_ref,
    weight_ref,
    alpha_ref,
    part_ref,
    place_ref,
    far_pairs_hbm,
    rows_hbm,
    columns_hbm,
    out_ref,
    filter_ref,
    far_pairs_ref,
    far_rows_ref,
    columns_ref,
    grad_s,
    out_s,
    far_sems,
    columns_sem,
):
    slots = MODES // devices
    lats = weight_ref.shape[0]
    firsts, offsets, _ = degree_starts(devices)
    columns_copy = pltpu.make_async_copy(
        columns_hbm.at[place_ref[0]], columns_ref, columns_sem.at[0]
    )
    near = near_pairs_ref.shape[0] // lats
    split = near_rows_ref.shape[0]
    far_copies = [
        pltpu.make_async_copy(far_pairs_hbm, far_pairs_ref, far_sems.at[0]),
        pltpu.make_async_copy(
            rows_hbm.at[place_ref[0], split:, :], far_rows_ref, far_sems.at[1]
        ),
    ]
    for copy in [columns_copy, *far_copies]:
        copy.start()
    landing = Spread(slots, grad_s, grads_ref)
    gain = gain_ref[...].astype(F32)
    lat_weight = weight_ref[...]
    channels = gain.shape[1]
    filter_ref[...] = jnp.zeros_like(filter_ref)

    def forward(slot):
        first, offset = firsts[slot], offsets[slot]
        landing.need(slot)
        if slot == near:
            for copy in far_copies:
                copy.wait()
        scale = alpha_ref[:, :channels] if slot == 0 else 2.0
        pairs_ref, rows_ref = near_pairs_ref, near_rows_ref
        place = slot
        if slot >= near:
            pairs_ref, rows_ref = far_pairs_ref, far_rows_ref
            place, offset = slot - near, offset - split
        modes = pairs_ref[place * lats : (place + 1) * lats, :]
        grads = slot_pair(grad_s, slot, slots, lats, scale)
        table = rows_ref[offset : offset + MODES - first, :]
        spectrum = dot(table, modes)
        gscaled = dot(table, grads)
        product = gscaled * spectrum
        filter_ref[first:, :] += product[:, :channels] + product[:, channels:]
        return (gscaled * jnp.concatenate([gain[first:], gain[first:]], 1)).astype(BF16)

    def back(slot, gspectrum):
        first, offset = firsts[slot], offsets[slot]
        if slot == 0:
            columns_copy.wait()
        result = dot(columns_ref[:, offset : offset + MODES - first], gspectrum)
        for part in range(2):
            out_s[pl.ds(part * slots + slot, lats, stride=out_s.shape[0] // lats), :] = (
                result[:, part * channels : (part + 1) * channels] * lat_weight
            )

    staggered(slots, DELAY, forward, back)
    rows = lats // devices * 2 * slots
    view = out_s.reshape(lats, out_s.shape[0] // lats, channels)
    out_ref[:, :rows, :] = (
        view[:, : 2 * slots, :].astype(BF16).reshape(devices, rows, channels)
    )
    if out_ref.shape[1] > rows:
        split = rows + MODES // devices
        out_ref[:, rows:split, :] = (
            filter_ref[...].reshape(devices, MODES // devices, channels).astype(BF16)
        )
        out_ref[:, split:, :] = part_ref[...].reshape(devices, -1, channels).astype(BF16)


def slope_kernel(
    slots,
    modes_ref,
    wide_ref,
    wide_t_ref,
    upstream_ref,
    first_ref,
    rows_hbm,
    columns_hbm,
    out_hbm,
    weight_ref,
    rows_ref,
    columns_ref,
    modes_s,
    folded_s,
    out_ref,
    rows_sems,
    columns_sems,
    out_sems,
):
    lats, lon_count, channels = upstream_ref.shape
    half = lon_count // 2
    block = modes_s.shape[1] // 2

    def lat_copy(source, target, sem_refs, parity, lat):
        span = slice(2 * lat * slots, 2 * (lat + 1) * slots)
        return pltpu.make_async_copy(
            source.at[:, parity, span, :],
            target.at[:, parity, span, :],
            sem_refs.at[parity * lats + lat],
        )

    places = [(parity, lat) for parity in range(2) for lat in range(lats)]
    rows_copies = [
        [
            pltpu.make_async_copy(
                rows_hbm.at[parity, start : start + size, :],
                rows_ref.at[parity, start : start + size, :],
                rows_sems.at[2 * chunk + parity],
            )
            for parity in range(2)
        ]
        for chunk, (start, size) in enumerate(row_chunks(half))
        if chunk
    ]
    columns_copies = [
        pltpu.make_async_copy(
            columns_hbm.at[parity], columns_ref.at[parity], columns_sems.at[parity]
        )
        for parity in range(2)
    ]
    for copy in [*sum(rows_copies, []), *columns_copies]:
        copy.start()
    mixed = dot(
        jnp.concatenate([load_pair(modes_ref, slots, *place) for place in places], 0), wide_ref[...]
    ).astype(BF16)
    for index, (parity, lat) in enumerate(places):
        for part in range(2):
            modes_s[
                parity,
                part * block : (part + 1) * block,
                lat * channels : (lat + 1) * channels,
            ] = mixed[
                index * block : (index + 1) * block, part * channels : (part + 1) * channels
            ]
    for chunk, (start, size) in enumerate(row_chunks(half)):
        for copy in rows_copies[chunk - 1] if chunk else ():
            copy.wait()
        table = rows_ref if chunk else first_ref
        even = dot(table[0, start : start + size, :], modes_s[0])
        odd = dot(table[1, start : start + size, :], modes_s[1])
        for lat in range(lats):
            lanes = slice(lat * channels, (lat + 1) * channels)
            near = upstream_ref[lat, start : start + size, :].astype(F32) * gelu_slope(
                even[:, lanes] + odd[:, lanes]
            )
            far = upstream_ref[lat, half + start : half + start + size, :].astype(
                F32
            ) * gelu_slope(even[:, lanes] - odd[:, lanes])
            folded_s[0, start : start + size, lanes] = (near + far).astype(BF16)
            folded_s[1, start : start + size, lanes] = (near - far).astype(BF16)
    pairs, stores = [], []
    for parity in range(2):
        columns_copies[parity].wait()
        raw = dot(columns_ref[parity], folded_s[parity]).astype(BF16)
        parity_pairs = [
            jnp.concatenate(
                [
                    raw[
                        part * block : (part + 1) * block, lat * channels : (lat + 1) * channels
                    ]
                    for part in range(2)
                ],
                1,
            )
            for lat in range(lats)
        ]
        mixed = dot(jnp.concatenate(parity_pairs, 0), wide_t_ref[...]).astype(BF16)
        for lat in range(lats):
            for part in range(2):
                store_rows(
                    out_ref,
                    slots,
                    parity,
                    lat,
                    part,
                    mixed[
                        lat * block : (lat + 1) * block, part * channels : (part + 1) * channels
                    ],
                )
            stores.append(lat_copy(out_ref, out_hbm, out_sems, parity, lat))
            stores[-1].start()
        pairs += parity_pairs
    total = jnp.zeros((2 * channels, 2 * channels), F32)
    for (parity, lat), pair in zip(places, pairs):
        total = total + lax.dot_general(
            load_pair(modes_ref, slots, parity, lat),
            pair,
            (((0,), (0,)), ((), ())),
            preferred_element_type=F32,
        )
    weight_ref[:channels, :] = total[:channels, :channels] + total[channels:, channels:]
    weight_ref[channels:, :] = total[:channels, channels:] - total[channels:, :channels]
    for copy in stores:
        copy.wait()


def synthesis_kernel(
    slots, modes_ref, upstream_hbm, rows_hbm, out_ref, upstream_ref, rows_ref, modes_s, sems
):
    lats, lon_count, channels = upstream_ref.shape
    copies = [
        pltpu.make_async_copy(rows_hbm.at[parity], rows_ref.at[parity], sems.at[parity])
        for parity in range(2)
    ]
    copies += [
        pltpu.make_async_copy(upstream_hbm.at[lat], upstream_ref.at[lat], sems.at[2 + lat])
        for lat in range(lats)
    ]
    for copy in copies:
        copy.start()
    half = lon_count // 2
    block = modes_s.shape[1] // 2
    for parity in range(2):
        for part in range(2):
            for lat in range(lats):
                modes_s[
                    parity,
                    part * block : (part + 1) * block,
                    lat * channels : (lat + 1) * channels,
                ] = load_rows(modes_ref, slots, parity, lat, part)
    for copy in copies:
        copy.wait()
    for start, size in row_chunks(half):
        even = dot(rows_ref[0, start : start + size, :], modes_s[0])
        odd = dot(rows_ref[1, start : start + size, :], modes_s[1])
        for lat in range(lats):
            lanes = slice(lat * channels, (lat + 1) * channels)
            for sign, base in ((1.0, start), (-1.0, half + start)):
                total = even[:, lanes] + sign * odd[:, lanes]
                total = total + upstream_ref[lat, base : base + size, :].astype(F32)
                out_ref[lat, base : base + size, :] = total.astype(BF16)


def total_kernel(received_ref, out_ref):
    rows = out_ref.shape[1]
    start = received_ref.shape[1] - rows
    total = received_ref[0, start:, :].astype(F32)
    for device in range(1, received_ref.shape[0]):
        total = total + received_ref[device, start:, :].astype(F32)
    out_ref[...] = jnp.broadcast_to(total.astype(BF16)[None], out_ref.shape)


def finish_kernel(received_ref, filter_ref, weight_ref):
    devices, rows, channels = received_ref.shape
    split = filter_ref.shape[0] // devices
    filter_ref[...] = (
        received_ref[:, :split, :].astype(F32).reshape(filter_ref.shape) * 0.125
    )
    weight_ref[...] = received_ref[:, split:, :].astype(F32).reshape(weight_ref.shape) * (
        1.0 / MODES
    )


def call(kernel, out_shape, scratch, flops, operands, streamed=(), written=0):
    outs = out_shape if isinstance(out_shape, (list, tuple)) else [out_shape]
    moved = sum(2 * math.prod(array.shape) for array in [*operands, *streamed, *outs])
    specs = [
        pl.BlockSpec(memory_space=pl.ANY if index < written else pltpu.VMEM)
        for index in range(len(outs))
    ]
    return pl.pallas_call(
        kernel,
        out_shape=out_shape,
        in_specs=[
            pl.BlockSpec(memory_space=pltpu.SMEM if array.dtype == jnp.int32 else pltpu.VMEM)
            for array in operands
        ]
        + [pl.BlockSpec(memory_space=pl.ANY)] * len(streamed),
        out_specs=specs if isinstance(out_shape, (list, tuple)) else specs[0],
        scratch_shapes=scratch,
        cost_estimate=pl.CostEstimate(flops=flops, bytes_accessed=moved, transcendentals=0),
        compiler_params=pltpu.CompilerParams(vmem_limit_bytes=VMEM_BYTES),
    )(*operands, *(away(array) for array in streamed))


def away(array):
    return pltpu.with_memory_space_constraint(array, pltpu.HBM)


def held(array):
    return pltpu.with_memory_space_constraint(array, pltpu.VMEM)


def exchange(array):
    return lax.all_to_all(array, "space", split_axis=0, concat_axis=0, tiled=True)


def sum_over_space(array, devices):
    step = devices // 2
    while step:
        array = array + lax.ppermute(
            array, "space", [(index, index ^ step) for index in range(devices)]
        )
        step //= 2
    return array


def body(grid_in, upstream, mix_weight, degree_filter):
    devices = lax.axis_size("space")
    me = lax.axis_index("space")
    lats, lon_count, channels = grid_in.shape
    lat_count = lats * devices
    slots = MODES // devices
    half = lon_count // 2
    dft_rows, dft_columns = fourier_constant(devices, lon_count)
    first_rows = jnp.asarray(dft_rows[:, : row_chunks(half)[0][1]])
    dft_rows, dft_columns = jnp.asarray(dft_rows), jnp.asarray(dft_columns)
    constants = table_constants(devices, lat_count)
    place = me.reshape(1)
    if constants is None:
        leg_rows, leg_columns = made_tables(devices, lat_count, me)
        leg_columns = leg_columns[None]
        place = jnp.zeros_like(place)
    else:
        leg_rows = lax.dynamic_index_in_dim(constants[0], me, 0, keepdims=False)
        leg_columns = constants[1]
    angles = np.pi * (np.arange(lat_count) + 0.5) / lat_count
    lat_weight = jnp.asarray(
        np.broadcast_to((np.pi / lat_count * np.sin(angles))[:, None], (lat_count, channels)), F32
    )
    alpha = jnp.where(me == 0, 1.0, 2.0) * jnp.ones((1, 2 * channels), F32)
    wide = mixing_matrix(mix_weight)
    mode_rows = lats * 2 * slots
    grid_shape = jax.ShapeDtypeStruct((devices // 2, 2, mode_rows, channels), BF16)
    grid_out = pltpu.HBM(grid_shape.shape, BF16)
    block_shape = (devices, mode_rows, channels)
    mode_shape = jax.ShapeDtypeStruct((lat_count, 2 * slots, channels), BF16)
    spread_shape = pltpu.VMEM((lat_count * (2 * slots + 8), channels), F32)
    modes_scratch = pltpu.VMEM((2, MODES, lats * channels), BF16)
    folded_scratch = pltpu.VMEM((2, half, lats * channels), BF16)
    dft_flops = 2 * MODES * lon_count * lats * channels
    leg_flops = 4 * degree_starts(devices)[2] * lat_count * channels
    modes_landing = pltpu.VMEM(mode_shape.shape, BF16)
    columns_landing = pltpu.VMEM(leg_columns.shape[1:], BF16)
    weight_rows = 2 * channels // devices
    extra = MODES // devices + weight_rows
    joined = (MODES // devices) % 16 == 0 and weight_rows % 16 == 0

    fourier = call(
        functools.partial(analyse_kernel, slots),
        grid_out,
        [
            pltpu.VMEM(grid_in.shape, BF16),
            pltpu.VMEM(dft_columns.shape, BF16),
            folded_scratch,
            pltpu.SemaphoreType.DMA((lats + 4,)),
        ],
        dft_flops,
        [],
        [grid_in, dft_columns],
    )
    held_upstream, held_first = (
        held(
            call(
                fetch_kernel,
                pltpu.VMEM(array.shape, BF16),
                [pltpu.SemaphoreType.DMA((1,))],
                0,
                [],
                [array],
            )
        )
        for array in (upstream, first_rows)
    )
    modes = exchange(fourier.reshape(block_shape)).reshape(mode_shape.shape)
    returned = call(
        functools.partial(spectrum_kernel, devices),
        pltpu.HBM(mode_shape.shape, BF16),
        [
            columns_landing,
            spread_shape,
            spread_shape,
            modes_landing,
            pltpu.SemaphoreType.DMA((1,)),
            pltpu.SemaphoreType.DMA((4,)),
        ],
        2 * leg_flops,
        [held(modes), held(leg_rows), degree_filter, lat_weight, alpha, place],
        [leg_columns],
        written=1,
    )
    returned = exchange(returned.reshape(block_shape)).reshape(grid_shape.shape)
    grid_landing = pltpu.VMEM(grid_shape.shape, BF16)
    mixed_grad, weight_part = call(
        functools.partial(slope_kernel, slots),
        [grid_out, jax.ShapeDtypeStruct((2 * channels, channels), F32)],
        [
            pltpu.VMEM(dft_rows.shape, BF16),
            pltpu.VMEM(dft_columns.shape, BF16),
            modes_scratch,
            folded_scratch,
            grid_landing,
            pltpu.SemaphoreType.DMA((2 * len(row_chunks(half)),)),
            pltpu.SemaphoreType.DMA((2,)),
            pltpu.SemaphoreType.DMA((2 * lats,)),
        ],
        2 * dft_flops,
        [held(returned), wide, wide.T, held_upstream, held_first],
        [dft_rows, dft_columns],
        written=1,
    )
    late_place, late_modes, mixed_grad = lax.optimization_barrier((place, modes, mixed_grad))
    near = slot_halves(slots)[0][1]
    if near == slots:
        near = slots // 2
    split = degree_starts(devices)[1][near]
    late_rows, near_rows = leg_rows[None], leg_rows[:split]
    if constants is not None:
        late_rows = constants[0]
        near_rows = call(
            fetch_place_kernel,
            pltpu.VMEM((split, lat_count), BF16),
            [pltpu.SemaphoreType.DMA((1,))],
            0,
            [late_place],
            [late_rows],
        )
    far_pairs_shape = ((slots - near) * lat_count, 2 * channels)
    near_pairs, far_pairs = call(
        functools.partial(pairs_kernel, devices),
        [
            pltpu.VMEM((near * lat_count, 2 * channels), BF16),
            pltpu.HBM(far_pairs_shape, BF16),
        ],
        [spread_shape],
        0,
        [lat_weight, away(late_modes)],
    )
    grads = exchange(mixed_grad.reshape(block_shape)).reshape(mode_shape.shape)
    gfield, filter_part = call(
        functools.partial(gradient_kernel, devices),
        [
            jax.ShapeDtypeStruct((devices, mode_rows + (extra if joined else 0), channels), BF16),
            jax.ShapeDtypeStruct((MODES, channels), F32),
        ],
        [
            pltpu.VMEM(far_pairs_shape, BF16),
            pltpu.VMEM((leg_rows.shape[0] - split, lat_count), BF16),
            columns_landing,
            spread_shape,
            spread_shape,
            pltpu.SemaphoreType.DMA((2,)),
            pltpu.SemaphoreType.DMA((1,)),
        ],
        3 * leg_flops,
        [
            held(grads),
            held(near_rows),
            held(near_pairs),
            degree_filter,
            lat_weight,
            alpha,
            weight_part,
            late_place,
        ],
        [far_pairs, late_rows, leg_columns],
    )
    gfield = exchange(gfield)
    if joined:
        sums = call(
            total_kernel, jax.ShapeDtypeStruct((devices, extra, channels), BF16), [], 0, [gfield]
        )
        grad_filter, grad_weight = call(
            finish_kernel,
            [
                jax.ShapeDtypeStruct((MODES, channels), F32),
                jax.ShapeDtypeStruct((2 * channels, channels), F32),
            ],
            [],
            0,
            [exchange(sums)],
        )
    else:
        grad_filter = sum_over_space(filter_part, devices) * 0.125
        grad_weight = sum_over_space(weight_part, devices) * (1.0 / MODES)
    grad_in = call(
        functools.partial(synthesis_kernel, slots),
        jax.ShapeDtypeStruct(grid_in.shape, BF16),
        [
            pltpu.VMEM(upstream.shape, BF16),
            pltpu.VMEM(dft_rows.shape, BF16),
            modes_scratch,
            pltpu.SemaphoreType.DMA((2 + lats,)),
        ],
        dft_flops,
        [gfield.reshape(devices // 2, 2, -1, channels)],
        [upstream, dft_rows],
    )
    return (grad_in, grad_weight.reshape(2, channels, channels), grad_filter)


def solution(mesh):
    return jax.shard_map(
        body,
        mesh=mesh,
        in_specs=(P(("groups", "space"), None, None), P(("groups", "space"), None, None), P(), P()),
        out_specs=(P(("groups", "space"), None, None), P("groups", None, None), P("groups", None)),
        check_vma=False,
    )
```

```python
import functools
import math

import jax
import jax.numpy as jnp
import ml_dtypes
import numpy as np
from jax import lax
from jax.experimental import pallas as pl
from jax.experimental.pallas import tpu as pltpu
from jax.sharding import PartitionSpec as P

MODES = 512
TABLE_BYTES = 64 * 1024 * 1024
VMEM_BYTES = 18 * 1024 * 1024
DELAY = 12
BF16 = jnp.bfloat16
F32 = jnp.float32


def latitude_angles(lat_count):
    lat_index = jnp.arange(lat_count, dtype=jnp.float32)
    return math.pi * (lat_index + 0.5) / lat_count


def legendre_rows(m_values, lat_count, mode_count):
    angles = latitude_angles(lat_count)
    cosine = jnp.cos(angles)[None, :]
    sine_lat = jnp.sin(angles)[None, :]
    orders = m_values.astype(jnp.float32)[:, None]
    log_start = 0.5 * (jnp.log(2.0 * orders + 1.0) - math.log(2.0))
    log_start = log_start + 0.5 * (
        lax.lgamma(2.0 * orders + 1.0) - 2.0 * lax.lgamma(orders + 1.0) - orders * math.log(4.0)
    )
    log_start = log_start + orders * jnp.log(sine_lat)

    def degree_block(carry, block_index):
        p_now, p_prev, log_scale = carry
        outputs = []
        for inner_step in range(32):
            degree = (block_index * 32 + inner_step).astype(jnp.float32)
            active = degree > orders
            denom = jnp.maximum(degree * degree - orders * orders, 1.0)
            coef_a = jnp.sqrt((4.0 * degree * degree - 1.0) / denom)
            lower = jnp.maximum((degree - 1.0) * (degree - 1.0) - orders * orders, 0.0)
            coef_b = jnp.sqrt(
                lower * (2.0 * degree + 1.0) / (jnp.maximum(2.0 * degree - 3.0, 1.0) * denom)
            )
            p_next = jnp.where(active, coef_a * cosine * p_now - coef_b * p_prev, p_now)
            p_prev = jnp.where(active, p_now, p_prev)
            p_now = p_next
            outputs.append(jnp.where(degree >= orders, p_now * jnp.exp(log_scale), 0.0))
        magnitude = jnp.maximum(jnp.abs(p_now), jnp.abs(p_prev))
        next_carry = (p_now / magnitude, p_prev / magnitude, log_scale + jnp.log(magnitude))
        return (next_carry, jnp.stack(outputs, 1))

    ones_grid = jnp.ones((m_values.shape[0], lat_count), jnp.float32)
    start_carry = (ones_grid, jnp.zeros_like(ones_grid), log_start * ones_grid)
    block_ids = jnp.arange(mode_count // 32, dtype=jnp.int32)
    final_carry, stacked = lax.scan(degree_block, start_carry, block_ids)
    return jnp.transpose(stacked, (1, 0, 2, 3)).reshape(m_values.shape[0], mode_count, lat_count)


@functools.lru_cache(maxsize=2)
def legendre_constant(lat_count, mode_count):
    angles = np.pi * (np.arange(lat_count) + 0.5) / lat_count
    cosine = np.cos(angles)[None, :]
    orders = np.arange(mode_count, dtype=np.float64)[:, None]
    gamma_2m = np.array([math.lgamma(2.0 * m + 1.0) for m in range(mode_count)])[:, None]
    gamma_m = np.array([math.lgamma(m + 1.0) for m in range(mode_count)])[:, None]
    log_scale = 0.5 * np.log((2.0 * orders + 1.0) / 2.0)
    log_scale = log_scale + 0.5 * (gamma_2m - 2.0 * gamma_m - orders * math.log(4.0))
    log_scale = log_scale + orders * np.log(np.sin(angles))[None, :]
    p_now, p_prev = np.ones_like(log_scale), np.zeros_like(log_scale)
    table = np.zeros((mode_count, mode_count, lat_count), ml_dtypes.bfloat16)
    for degree in range(mode_count):
        active = degree > orders
        denom = np.maximum(degree * degree - orders * orders, 1.0)
        coef_a = np.sqrt(max(4.0 * degree * degree - 1.0, 0.0) / denom)
        lower = np.maximum((degree - 1.0) ** 2 - orders * orders, 0.0)
        coef_b = np.sqrt(lower * (2.0 * degree + 1.0) / (max(2.0 * degree - 3.0, 1.0) * denom))
        p_next = np.where(active, coef_a * cosine * p_now - coef_b * p_prev, p_now)
        p_prev = np.where(active, p_now, p_prev)
        p_now = p_next
        value = np.where(degree >= orders, p_now * np.exp(log_scale), 0.0)
        table[:, degree, :] = value.astype(np.float32).astype(ml_dtypes.bfloat16)
        if degree % 32 == 31:
            magnitude = np.maximum(np.abs(p_now), np.abs(p_prev))
            p_now, p_prev = p_now / magnitude, p_prev / magnitude
            log_scale = log_scale + np.log(magnitude)
    return table


@functools.lru_cache(maxsize=2)
def fourier_constant(devices, lon_count):
    half, slots = lon_count // 2, MODES // devices
    tables = []
    for parity in range(2):
        owner = 2 * np.arange(devices // 2)[:, None] + parity
        orders = (np.arange(slots)[None, :] * devices + owner).reshape(-1)
        phases = (orders[None, :] * np.arange(half)[:, None]) % lon_count
        angles = 2.0 * np.pi / lon_count * phases
        both = np.concatenate([np.cos(angles), -np.sin(angles)], 1) / math.sqrt(lon_count)
        tables.append(both.astype(np.float32).astype(ml_dtypes.bfloat16))
    table = np.stack(tables, 0)
    return np.ascontiguousarray(table), np.ascontiguousarray(table.transpose(0, 2, 1))


def degree_starts(devices):
    firsts = [slot * devices // 16 * 16 for slot in range(MODES // devices)]
    rows = [MODES - first for first in firsts]
    offsets = [sum(rows[:slot]) for slot in range(len(rows))]
    return firsts, offsets, sum(rows)


@functools.lru_cache(maxsize=2)
def packed_legendre(devices, lat_count):
    firsts, offsets, total = degree_starts(devices)
    table = legendre_constant(lat_count, MODES)
    packed = np.concatenate(
        [
            table[slot * devices : (slot + 1) * devices, first:]
            for slot, first in enumerate(firsts)
        ],
        1,
    )
    return np.ascontiguousarray(packed), np.ascontiguousarray(packed.transpose(0, 2, 1))


def table_constants(devices, lat_count):
    _, _, total = degree_starts(devices)
    if devices * total * 2 * (lat_count + max(lat_count, 128)) > TABLE_BYTES:
        return None
    return tuple(jnp.asarray(table) for table in packed_legendre(devices, lat_count))


def made_tables(devices, lat_count, me):
    firsts, _, _ = degree_starts(devices)
    slot_orders = jnp.arange(MODES // devices, dtype=jnp.int32) * devices + me
    legendre = legendre_rows(slot_orders, lat_count, MODES).astype(BF16)
    rows = jnp.concatenate([legendre[slot, first:] for slot, first in enumerate(firsts)], 0)
    return rows, rows.T


def mixing_matrix(mix_weight):
    upper = jnp.concatenate([mix_weight[0], mix_weight[1]], 1)
    lower = jnp.concatenate([-mix_weight[1], mix_weight[0]], 1)
    return jnp.concatenate([upper, lower], 0)


def gelu_slope(field):
    return 0.5 * (1.0 + lax.erf(field * (1.0 / math.sqrt(2.0)))) + field * jnp.exp(
        -0.5 * field * field
    ) * (1.0 / math.sqrt(2.0 * math.pi))


def dot(left, right):
    return jnp.dot(left, right, preferred_element_type=F32)


def row_chunks(count):
    size = count // 3 if count % 48 == 0 else count
    return [(start, size) for start in range(0, count, size)]


def store_rows(out_ref, slots, parity, lat, part, value):
    start = (2 * lat + part) * slots
    out_ref[:, parity, start : start + slots, :] = value.reshape(-1, slots, value.shape[1])


def load_rows(ref, slots, parity, lat, part):
    start = (2 * lat + part) * slots
    return ref[:, parity, start : start + slots, :].reshape(-1, ref.shape[3])


def load_pair(ref, slots, parity, lat):
    return jnp.concatenate([load_rows(ref, slots, parity, lat, part) for part in range(2)], 1)


def fetch_kernel(*refs):
    count = (len(refs) - 1) // 2
    sems = refs[-1]
    copies = [
        pltpu.make_async_copy(refs[index], refs[count + index], sems.at[index])
        for index in range(count)
    ]
    for copy in copies:
        copy.start()
    for copy in copies:
        copy.wait()


def fetch_place_kernel(place_ref, source_hbm, out_ref, sems):
    copy = pltpu.make_async_copy(
        source_hbm.at[place_ref[0], : out_ref.shape[0], :], out_ref, sems.at[0]
    )
    copy.start()
    copy.wait()


def analyse_kernel(
    slots, grid_hbm, columns_hbm, out_ref, grid_ref, columns_ref, folded_ref, sems
):
    lats, lon_count, channels = grid_ref.shape
    half = lon_count // 2
    block = columns_ref.shape[1] // 2
    grid_copies = [
        pltpu.make_async_copy(grid_hbm.at[lat], grid_ref.at[lat], sems.at[lat])
        for lat in range(lats)
    ]
    table_copies = [
        pltpu.make_async_copy(
            columns_hbm.at[parity, part * block : (part + 1) * block, :],
            columns_ref.at[parity, part * block : (part + 1) * block, :],
            sems.at[lats + 2 * parity + part],
        )
        for parity in range(2)
        for part in range(2)
    ]
    for copy in grid_copies + table_copies:
        copy.start()
    for lat in range(lats):
        grid_copies[lat].wait()
        near = grid_ref[lat, :half, :].astype(F32)
        far = grid_ref[lat, half:, :].astype(F32)
        folded_ref[0, :, lat * channels : (lat + 1) * channels] = (near + far).astype(BF16)
        folded_ref[1, :, lat * channels : (lat + 1) * channels] = (near - far).astype(BF16)
    for parity in range(2):
        for part in range(2):
            table_copies[2 * parity + part].wait()
        result = dot(columns_ref[parity], folded_ref[parity]).astype(BF16)
        for part in range(2):
            for lat in range(lats):
                lanes = slice(lat * channels, (lat + 1) * channels)
                rows = slice(part * block, (part + 1) * block)
                store_rows(out_ref, slots, parity, lat, part, result[rows, lanes])


def slot_rows(ref, part, slot, slots, lats):
    return ref[pl.ds(part * slots + slot, lats, stride=ref.shape[0] // lats), :]


def slot_pair(ref, slot, slots, lats, scale):
    return jnp.concatenate(
        [(slot_rows(ref, part, slot, slots, lats) * scale).astype(BF16) for part in range(2)], 1
    )


def slot_halves(slots):
    size = slots // 2 if slots % 32 == 0 else slots
    return [(start, size) for start in range(0, slots, size)]


class Spread:
    def __init__(self, slots, spread_ref, array_ref):
        lats, self.rows, channels = array_ref.shape
        self.slots = slots
        self.halves = slot_halves(slots)
        self.spread_ref = spread_ref.reshape(lats, spread_ref.shape[0] // lats, channels)
        self.array_ref = array_ref

    def need(self, slot):
        for start, size in self.halves:
            if slot == start:
                for part in range(2):
                    begin = part * self.slots + start
                    span = slice(begin, begin + size)
                    self.spread_ref[:, span, :] = self.array_ref[:, span, :].astype(F32)


def staggered(count, delay, first_stage, second_stage):
    waiting = []
    for index in range(count):
        waiting.append((index, first_stage(index)))
        if len(waiting) > delay:
            second_stage(*waiting.pop(0))
    for item in waiting:
        second_stage(*item)


def spectrum_kernel(
    devices,
    modes_ref,
    rows_ref,
    gain_ref,
    weight_ref,
    alpha_ref,
    place_ref,
    columns_hbm,
    out_hbm,
    columns_ref,
    in_s,
    out_s,
    out_ref,
    columns_sem,
    out_sems,
):
    columns_copy = pltpu.make_async_copy(
        columns_hbm.at[place_ref[0]], columns_ref, columns_sem.at[0]
    )
    columns_copy.start()
    slots = MODES // devices
    lats = weight_ref.shape[0]
    firsts, offsets, _ = degree_starts(devices)
    landing = Spread(slots, in_s, modes_ref)
    stores = []
    gain = gain_ref[...]
    channels = gain.shape[1]
    lat_weight = weight_ref[...]

    def forward(slot):
        first, offset = firsts[slot], offsets[slot]
        landing.need(slot)
        modes = slot_pair(in_s, slot, slots, lats, lat_weight)
        spectrum = dot(rows_ref[offset : offset + MODES - first, :], modes).astype(BF16)
        return spectrum * jnp.concatenate([gain[first:], gain[first:]], 1)

    def back(slot, scaled):
        first, offset = firsts[slot], offsets[slot]
        if slot == 0:
            columns_copy.wait()
        result = dot(columns_ref[:, offset : offset + MODES - first], scaled)
        result = result * (alpha_ref[...] if slot == 0 else 2.0)
        for part in range(2):
            out_s[pl.ds(part * slots + slot, lats, stride=out_s.shape[0] // lats), :] = result[
                :, part * channels : (part + 1) * channels
            ]
        for start, size in landing.halves:
            if slot == start + size - 1:
                store(start, size)

    def store(start, size):
        view = out_s.reshape(lats, out_s.shape[0] // lats, channels)
        for part in range(2):
            span = slice(part * slots + start, part * slots + start + size)
            out_ref[:, span, :] = view[:, span, :].astype(BF16)
            if size < slots:
                copy = pltpu.make_async_copy(
                    out_ref.at[:, span, :], out_hbm.at[:, span, :], out_sems.at[len(stores)]
                )
                copy.start()
                stores.append(copy)
        if size == slots:
            copy = pltpu.make_async_copy(out_ref, out_hbm, out_sems.at[0])
            copy.start()
            stores.append(copy)

    staggered(slots, DELAY, forward, back)
    for copy in stores:
        copy.wait()


def pairs_kernel(devices, weight_ref, modes_ref, near_ref, far_ref, in_s):
    slots = MODES // devices
    lats = weight_ref.shape[0]
    landing = Spread(slots, in_s, modes_ref)
    lat_weight = weight_ref[...]
    near = near_ref.shape[0] // lats
    for slot in range(slots):
        landing.need(slot)
        pair = slot_pair(in_s, slot, slots, lats, lat_weight)
        if slot < near:
            near_ref[slot * lats : (slot + 1) * lats, :] = pair
        else:
            far_ref[(slot - near) * lats : (slot - near + 1) * lats, :] = pair


def gradient_kernel(
    devices,
    grads_ref,
    near_rows_ref,
    near_pairs_ref,
    gain_ref,
    weight_ref,
    alpha_ref,
    part_ref,
    place_ref,
    far_pairs_hbm,
    rows_hbm,
    columns_hbm,
    out_ref,
    filter_ref,
    far_pairs_ref,
    far_rows_ref,
    columns_ref,
    grad_s,
    out_s,
    far_sems,
    columns_sem,
):
    slots = MODES // devices
    lats = weight_ref.shape[0]
    firsts, offsets, _ = degree_starts(devices)
    columns_copy = pltpu.make_async_copy(
        columns_hbm.at[place_ref[0]], columns_ref, columns_sem.at[0]
    )
    near = near_pairs_ref.shape[0] // lats
    split = near_rows_ref.shape[0]
    far_copies = [
        pltpu.make_async_copy(far_pairs_hbm, far_pairs_ref, far_sems.at[0]),
        pltpu.make_async_copy(
            rows_hbm.at[place_ref[0], split:, :], far_rows_ref, far_sems.at[1]
        ),
    ]
    for copy in [columns_copy, *far_copies]:
        copy.start()
    landing = Spread(slots, grad_s, grads_ref)
    gain = gain_ref[...].astype(F32)
    lat_weight = weight_ref[...]
    channels = gain.shape[1]
    filter_ref[...] = jnp.zeros_like(filter_ref)

    def forward(slot):
        first, offset = firsts[slot], offsets[slot]
        landing.need(slot)
        if slot == near:
            for copy in far_copies:
                copy.wait()
        scale = alpha_ref[:, :channels] if slot == 0 else 2.0
        pairs_ref, rows_ref = near_pairs_ref, near_rows_ref
        place = slot
        if slot >= near:
            pairs_ref, rows_ref = far_pairs_ref, far_rows_ref
            place, offset = slot - near, offset - split
        modes = pairs_ref[place * lats : (place + 1) * lats, :]
        grads = slot_pair(grad_s, slot, slots, lats, scale)
        table = rows_ref[offset : offset + MODES - first, :]
        spectrum = dot(table, modes)
        gscaled = dot(table, grads)
        product = gscaled * spectrum
        filter_ref[first:, :] += product[:, :channels] + product[:, channels:]
        return (gscaled * jnp.concatenate([gain[first:], gain[first:]], 1)).astype(BF16)

    def back(slot, gspectrum):
        first, offset = firsts[slot], offsets[slot]
        if slot == 0:
            columns_copy.wait()
        result = dot(columns_ref[:, offset : offset + MODES - first], gspectrum)
        for part in range(2):
            out_s[pl.ds(part * slots + slot, lats, stride=out_s.shape[0] // lats), :] = (
                result[:, part * channels : (part + 1) * channels] * lat_weight
            )

    staggered(slots, DELAY, forward, back)
    rows = lats // devices * 2 * slots
    view = out_s.reshape(lats, out_s.shape[0] // lats, channels)
    out_ref[:, :rows, :] = (
        view[:, : 2 * slots, :].astype(BF16).reshape(devices, rows, channels)
    )
    if out_ref.shape[1] > rows:
        split = rows + MODES // devices
        out_ref[:, rows:split, :] = (
            filter_ref[...].reshape(devices, MODES // devices, channels).astype(BF16)
        )
        out_ref[:, split:, :] = part_ref[...].reshape(devices, -1, channels).astype(BF16)


def slope_kernel(
    slots,
    modes_ref,
    wide_ref,
    wide_t_ref,
    upstream_ref,
    first_ref,
    rows_hbm,
    columns_hbm,
    out_hbm,
    weight_ref,
    rows_ref,
    columns_ref,
    modes_s,
    folded_s,
    out_ref,
    rows_sems,
    columns_sems,
    out_sems,
):
    lats, lon_count, channels = upstream_ref.shape
    half = lon_count // 2
    block = modes_s.shape[1] // 2

    def lat_copy(source, target, sem_refs, parity, lat):
        span = slice(2 * lat * slots, 2 * (lat + 1) * slots)
        return pltpu.make_async_copy(
            source.at[:, parity, span, :],
            target.at[:, parity, span, :],
            sem_refs.at[parity * lats + lat],
        )

    places = [(parity, lat) for parity in range(2) for lat in range(lats)]
    rows_copies = [
        [
            pltpu.make_async_copy(
                rows_hbm.at[parity, start : start + size, :],
                rows_ref.at[parity, start : start + size, :],
                rows_sems.at[2 * chunk + parity],
            )
            for parity in range(2)
        ]
        for chunk, (start, size) in enumerate(row_chunks(half))
        if chunk
    ]
    columns_copies = [
        pltpu.make_async_copy(
            columns_hbm.at[parity], columns_ref.at[parity], columns_sems.at[parity]
        )
        for parity in range(2)
    ]
    for copy in [*sum(rows_copies, []), *columns_copies]:
        copy.start()
    mixed = dot(
        jnp.concatenate([load_pair(modes_ref, slots, *place) for place in places], 0), wide_ref[...]
    ).astype(BF16)
    for index, (parity, lat) in enumerate(places):
        for part in range(2):
            modes_s[
                parity,
                part * block : (part + 1) * block,
                lat * channels : (lat + 1) * channels,
            ] = mixed[
                index * block : (index + 1) * block, part * channels : (part + 1) * channels
            ]
    for chunk, (start, size) in enumerate(row_chunks(half)):
        for copy in rows_copies[chunk - 1] if chunk else ():
            copy.wait()
        table = rows_ref if chunk else first_ref
        even = dot(table[0, start : start + size, :], modes_s[0])
        odd = dot(table[1, start : start + size, :], modes_s[1])
        for lat in range(lats):
            lanes = slice(lat * channels, (lat + 1) * channels)
            near = upstream_ref[lat, start : start + size, :].astype(F32) * gelu_slope(
                even[:, lanes] + odd[:, lanes]
            )
            far = upstream_ref[lat, half + start : half + start + size, :].astype(
                F32
            ) * gelu_slope(even[:, lanes] - odd[:, lanes])
            folded_s[0, start : start + size, lanes] = (near + far).astype(BF16)
            folded_s[1, start : start + size, lanes] = (near - far).astype(BF16)
    pairs, stores = [], []
    for parity in range(2):
        columns_copies[parity].wait()
        raw = dot(columns_ref[parity], folded_s[parity]).astype(BF16)
        parity_pairs = [
            jnp.concatenate(
                [
                    raw[
                        part * block : (part + 1) * block, lat * channels : (lat + 1) * channels
                    ]
                    for part in range(2)
                ],
                1,
            )
            for lat in range(lats)
        ]
        mixed = dot(jnp.concatenate(parity_pairs, 0), wide_t_ref[...]).astype(BF16)
        for lat in range(lats):
            for part in range(2):
                store_rows(
                    out_ref,
                    slots,
                    parity,
                    lat,
                    part,
                    mixed[
                        lat * block : (lat + 1) * block, part * channels : (part + 1) * channels
                    ],
                )
            stores.append(lat_copy(out_ref, out_hbm, out_sems, parity, lat))
            stores[-1].start()
        pairs += parity_pairs
    total = jnp.zeros((2 * channels, 2 * channels), F32)
    for (parity, lat), pair in zip(places, pairs):
        total = total + lax.dot_general(
            load_pair(modes_ref, slots, parity, lat),
            pair,
            (((0,), (0,)), ((), ())),
            preferred_element_type=F32,
        )
    weight_ref[:channels, :] = total[:channels, :channels] + total[channels:, channels:]
    weight_ref[channels:, :] = total[:channels, channels:] - total[channels:, :channels]
    for copy in stores:
        copy.wait()


def synthesis_kernel(
    slots, modes_ref, upstream_hbm, rows_hbm, out_ref, upstream_ref, rows_ref, modes_s, sems
):
    lats, lon_count, channels = upstream_ref.shape
    copies = [
        pltpu.make_async_copy(rows_hbm.at[parity], rows_ref.at[parity], sems.at[parity])
        for parity in range(2)
    ]
    copies += [
        pltpu.make_async_copy(upstream_hbm.at[lat], upstream_ref.at[lat], sems.at[2 + lat])
        for lat in range(lats)
    ]
    for copy in copies:
        copy.start()
    half = lon_count // 2
    block = modes_s.shape[1] // 2
    for parity in range(2):
        for part in range(2):
            for lat in range(lats):
                modes_s[
                    parity,
                    part * block : (part + 1) * block,
                    lat * channels : (lat + 1) * channels,
                ] = load_rows(modes_ref, slots, parity, lat, part)
    for copy in copies:
        copy.wait()
    for start, size in row_chunks(half):
        even = dot(rows_ref[0, start : start + size, :], modes_s[0])
        odd = dot(rows_ref[1, start : start + size, :], modes_s[1])
        for lat in range(lats):
            lanes = slice(lat * channels, (lat + 1) * channels)
            for sign, base in ((1.0, start), (-1.0, half + start)):
                total = even[:, lanes] + sign * odd[:, lanes]
                total = total + upstream_ref[lat, base : base + size, :].astype(F32)
                out_ref[lat, base : base + size, :] = total.astype(BF16)


def total_kernel(received_ref, out_ref):
    rows = out_ref.shape[1]
    start = received_ref.shape[1] - rows
    total = received_ref[0, start:, :].astype(F32)
    for device in range(1, received_ref.shape[0]):
        total = total + received_ref[device, start:, :].astype(F32)
    out_ref[...] = jnp.broadcast_to(total.astype(BF16)[None], out_ref.shape)


def finish_kernel(received_ref, filter_ref, weight_ref):
    devices, rows, channels = received_ref.shape
    split = filter_ref.shape[0] // devices
    filter_ref[...] = (
        received_ref[:, :split, :].astype(F32).reshape(filter_ref.shape) * 0.125
    )
    weight_ref[...] = received_ref[:, split:, :].astype(F32).reshape(weight_ref.shape) * (
        1.0 / MODES
    )


def call(kernel, out_shape, scratch, flops, operands, streamed=(), written=0):
    outs = out_shape if isinstance(out_shape, (list, tuple)) else [out_shape]
    moved = sum(2 * math.prod(array.shape) for array in [*operands, *streamed, *outs])
    specs = [
        pl.BlockSpec(memory_space=pl.ANY if index < written else pltpu.VMEM)
        for index in range(len(outs))
    ]
    return pl.pallas_call(
        kernel,
        out_shape=out_shape,
        in_specs=[
            pl.BlockSpec(memory_space=pltpu.SMEM if array.dtype == jnp.int32 else pltpu.VMEM)
            for array in operands
        ]
        + [pl.BlockSpec(memory_space=pl.ANY)] * len(streamed),
        out_specs=specs if isinstance(out_shape, (list, tuple)) else specs[0],
        scratch_shapes=scratch,
        cost_estimate=pl.CostEstimate(flops=flops, bytes_accessed=moved, transcendentals=0),
        compiler_params=pltpu.CompilerParams(vmem_limit_bytes=VMEM_BYTES),
    )(*operands, *(away(array) for array in streamed))


def away(array):
    return pltpu.with_memory_space_constraint(array, pltpu.HBM)


def held(array):
    return pltpu.with_memory_space_constraint(array, pltpu.VMEM)


def exchange(array):
    return lax.all_to_all(array, "space", split_axis=0, concat_axis=0, tiled=True)


def sum_over_space(array, devices):
    step = devices // 2
    while step:
        array = array + lax.ppermute(
            array, "space", [(index, index ^ step) for index in range(devices)]
        )
        step //= 2
    return array


def body(grid_in, upstream, mix_weight, degree_filter):
    devices = lax.axis_size("space")
    me = lax.axis_index("space")
    lats, lon_count, channels = grid_in.shape
    lat_count = lats * devices
    slots = MODES // devices
    half = lon_count // 2
    dft_rows, dft_columns = fourier_constant(devices, lon_count)
    first_rows = jnp.asarray(dft_rows[:, : row_chunks(half)[0][1]])
    dft_rows, dft_columns = jnp.asarray(dft_rows), jnp.asarray(dft_columns)
    constants = table_constants(devices, lat_count)
    place = me.reshape(1)
    if constants is None:
        leg_rows, leg_columns = made_tables(devices, lat_count, me)
        leg_columns = leg_columns[None]
        place = jnp.zeros_like(place)
    else:
        leg_rows = lax.dynamic_index_in_dim(constants[0], me, 0, keepdims=False)
        leg_columns = constants[1]
    angles = np.pi * (np.arange(lat_count) + 0.5) / lat_count
    lat_weight = jnp.asarray(
        np.broadcast_to((np.pi / lat_count * np.sin(angles))[:, None], (lat_count, channels)), F32
    )
    alpha = jnp.where(me == 0, 1.0, 2.0) * jnp.ones((1, 2 * channels), F32)
    wide = mixing_matrix(mix_weight)
    mode_rows = lats * 2 * slots
    grid_shape = jax.ShapeDtypeStruct((devices // 2, 2, mode_rows, channels), BF16)
    grid_out = pltpu.HBM(grid_shape.shape, BF16)
    block_shape = (devices, mode_rows, channels)
    mode_shape = jax.ShapeDtypeStruct((lat_count, 2 * slots, channels), BF16)
    spread_shape = pltpu.VMEM((lat_count * (2 * slots + 8), channels), F32)
    modes_scratch = pltpu.VMEM((2, MODES, lats * channels), BF16)
    folded_scratch = pltpu.VMEM((2, half, lats * channels), BF16)
    dft_flops = 2 * MODES * lon_count * lats * channels
    leg_flops = 4 * degree_starts(devices)[2] * lat_count * channels
    modes_landing = pltpu.VMEM(mode_shape.shape, BF16)
    columns_landing = pltpu.VMEM(leg_columns.shape[1:], BF16)
    weight_rows = 2 * channels // devices
    extra = MODES // devices + weight_rows
    joined = (MODES // devices) % 16 == 0 and weight_rows % 16 == 0

    fourier = call(
        functools.partial(analyse_kernel, slots),
        grid_out,
        [
            pltpu.VMEM(grid_in.shape, BF16),
            pltpu.VMEM(dft_columns.shape, BF16),
            folded_scratch,
            pltpu.SemaphoreType.DMA((lats + 4,)),
        ],
        dft_flops,
        [],
        [grid_in, dft_columns],
    )
    held_upstream, held_first = (
        held(
            call(
                fetch_kernel,
                pltpu.VMEM(array.shape, BF16),
                [pltpu.SemaphoreType.DMA((1,))],
                0,
                [],
                [array],
            )
        )
        for array in (upstream, first_rows)
    )
    modes = exchange(fourier.reshape(block_shape)).reshape(mode_shape.shape)
    returned = call(
        functools.partial(spectrum_kernel, devices),
        pltpu.HBM(mode_shape.shape, BF16),
        [
            columns_landing,
            spread_shape,
            spread_shape,
            modes_landing,
            pltpu.SemaphoreType.DMA((1,)),
            pltpu.SemaphoreType.DMA((4,)),
        ],
        2 * leg_flops,
        [held(modes), held(leg_rows), degree_filter, lat_weight, alpha, place],
        [leg_columns],
        written=1,
    )
    returned = exchange(returned.reshape(block_shape)).reshape(grid_shape.shape)
    grid_landing = pltpu.VMEM(grid_shape.shape, BF16)
    mixed_grad, weight_part = call(
        functools.partial(slope_kernel, slots),
        [grid_out, jax.ShapeDtypeStruct((2 * channels, channels), F32)],
        [
            pltpu.VMEM(dft_rows.shape, BF16),
            pltpu.VMEM(dft_columns.shape, BF16),
            modes_scratch,
            folded_scratch,
            grid_landing,
            pltpu.SemaphoreType.DMA((2 * len(row_chunks(half)),)),
            pltpu.SemaphoreType.DMA((2,)),
            pltpu.SemaphoreType.DMA((2 * lats,)),
        ],
        2 * dft_flops,
        [held(returned), wide, wide.T, held_upstream, held_first],
        [dft_rows, dft_columns],
        written=1,
    )
    late_place, late_modes, mixed_grad = lax.optimization_barrier((place, modes, mixed_grad))
    near = slot_halves(slots)[0][1]
    if near == slots:
        near = slots // 2
    split = degree_starts(devices)[1][near]
    late_rows, near_rows = leg_rows[None], leg_rows[:split]
    if constants is not None:
        late_rows = constants[0]
        near_rows = call(
            fetch_place_kernel,
            pltpu.VMEM((split, lat_count), BF16),
            [pltpu.SemaphoreType.DMA((1,))],
            0,
            [late_place],
            [late_rows],
        )
    far_pairs_shape = ((slots - near) * lat_count, 2 * channels)
    near_pairs, far_pairs = call(
        functools.partial(pairs_kernel, devices),
        [
            pltpu.VMEM((near * lat_count, 2 * channels), BF16),
            pltpu.HBM(far_pairs_shape, BF16),
        ],
        [spread_shape],
        0,
        [lat_weight, away(late_modes)],
    )
    grads = exchange(mixed_grad.reshape(block_shape)).reshape(mode_shape.shape)
    gfield, filter_part = call(
        functools.partial(gradient_kernel, devices),
        [
            jax.ShapeDtypeStruct((devices, mode_rows + (extra if joined else 0), channels), BF16),
            jax.ShapeDtypeStruct((MODES, channels), F32),
        ],
        [
            pltpu.VMEM(far_pairs_shape, BF16),
            pltpu.VMEM((leg_rows.shape[0] - split, lat_count), BF16),
            columns_landing,
            spread_shape,
            spread_shape,
            pltpu.SemaphoreType.DMA((2,)),
            pltpu.SemaphoreType.DMA((1,)),
        ],
        3 * leg_flops,
        [
            held(grads),
            held(near_rows),
            held(near_pairs),
            degree_filter,
            lat_weight,
            alpha,
            weight_part,
            late_place,
        ],
        [far_pairs, late_rows, leg_columns],
    )
    gfield = exchange(gfield)
    if joined:
        sums = call(
            total_kernel, jax.ShapeDtypeStruct((devices, extra, channels), BF16), [], 0, [gfield]
        )
        grad_filter, grad_weight = call(
            finish_kernel,
            [
                jax.ShapeDtypeStruct((MODES, channels), F32),
                jax.ShapeDtypeStruct((2 * channels, channels), F32),
            ],
            [],
            0,
            [exchange(sums)],
        )
    else:
        grad_filter = sum_over_space(filter_part, devices) * 0.125
        grad_weight = sum_over_space(weight_part, devices) * (1.0 / MODES)
    grad_in = call(
        functools.partial(synthesis_kernel, slots),
        jax.ShapeDtypeStruct(grid_in.shape, BF16),
        [
            pltpu.VMEM(upstream.shape, BF16),
            pltpu.VMEM(dft_rows.shape, BF16),
            modes_scratch,
            pltpu.SemaphoreType.DMA((2 + lats,)),
        ],
        dft_flops,
        [gfield.reshape(devices // 2, 2, -1, channels)],
        [upstream, dft_rows],
    )
    return (grad_in, grad_weight.reshape(2, channels, channels), grad_filter)


def solution(mesh):
    return jax.shard_map(
        body,
        mesh=mesh,
        in_specs=(P(("groups", "space"), None, None), P(("groups", "space"), None, None), P(), P()),
        out_specs=(P(("groups", "space"), None, None), P("groups", None, None), P("groups", None)),
        check_vma=False,
    )
```

```python
import functools
import math

import jax
import jax.numpy as jnp
import ml_dtypes
import numpy as np
from jax import lax
from jax.experimental import pallas as pl
from jax.experimental.pallas import tpu as pltpu
from jax.sharding import PartitionSpec as P

MODES = 512
TABLE_BYTES = 64 * 1024 * 1024
VMEM_BYTES = 18 * 1024 * 1024
DELAY = 20
BF16 = jnp.bfloat16
F32 = jnp.float32


def latitude_angles(lat_count):
    lat_index = jnp.arange(lat_count, dtype=jnp.float32)
    return math.pi * (lat_index + 0.5) / lat_count


def legendre_rows(m_values, lat_count, mode_count):
    angles = latitude_angles(lat_count)
    cosine = jnp.cos(angles)[None, :]
    sine_lat = jnp.sin(angles)[None, :]
    orders = m_values.astype(jnp.float32)[:, None]
    log_start = 0.5 * (jnp.log(2.0 * orders + 1.0) - math.log(2.0))
    log_start = log_start + 0.5 * (
        lax.lgamma(2.0 * orders + 1.0) - 2.0 * lax.lgamma(orders + 1.0) - orders * math.log(4.0)
    )
    log_start = log_start + orders * jnp.log(sine_lat)

    def degree_block(carry, block_index):
        p_now, p_prev, log_scale = carry
        outputs = []
        for inner_step in range(32):
            degree = (block_index * 32 + inner_step).astype(jnp.float32)
            active = degree > orders
            denom = jnp.maximum(degree * degree - orders * orders, 1.0)
            coef_a = jnp.sqrt((4.0 * degree * degree - 1.0) / denom)
            lower = jnp.maximum((degree - 1.0) * (degree - 1.0) - orders * orders, 0.0)
            coef_b = jnp.sqrt(
                lower * (2.0 * degree + 1.0) / (jnp.maximum(2.0 * degree - 3.0, 1.0) * denom)
            )
            p_next = jnp.where(active, coef_a * cosine * p_now - coef_b * p_prev, p_now)
            p_prev = jnp.where(active, p_now, p_prev)
            p_now = p_next
            outputs.append(jnp.where(degree >= orders, p_now * jnp.exp(log_scale), 0.0))
        magnitude = jnp.maximum(jnp.abs(p_now), jnp.abs(p_prev))
        next_carry = (p_now / magnitude, p_prev / magnitude, log_scale + jnp.log(magnitude))
        return (next_carry, jnp.stack(outputs, 1))

    ones_grid = jnp.ones((m_values.shape[0], lat_count), jnp.float32)
    start_carry = (ones_grid, jnp.zeros_like(ones_grid), log_start * ones_grid)
    block_ids = jnp.arange(mode_count // 32, dtype=jnp.int32)
    final_carry, stacked = lax.scan(degree_block, start_carry, block_ids)
    return jnp.transpose(stacked, (1, 0, 2, 3)).reshape(m_values.shape[0], mode_count, lat_count)


@functools.lru_cache(maxsize=2)
def legendre_constant(lat_count, mode_count):
    angles = np.pi * (np.arange(lat_count) + 0.5) / lat_count
    cosine = np.cos(angles)[None, :]
    orders = np.arange(mode_count, dtype=np.float64)[:, None]
    gamma_2m = np.array([math.lgamma(2.0 * m + 1.0) for m in range(mode_count)])[:, None]
    gamma_m = np.array([math.lgamma(m + 1.0) for m in range(mode_count)])[:, None]
    log_scale = 0.5 * np.log((2.0 * orders + 1.0) / 2.0)
    log_scale = log_scale + 0.5 * (gamma_2m - 2.0 * gamma_m - orders * math.log(4.0))
    log_scale = log_scale + orders * np.log(np.sin(angles))[None, :]
    p_now, p_prev = np.ones_like(log_scale), np.zeros_like(log_scale)
    table = np.zeros((mode_count, mode_count, lat_count), ml_dtypes.bfloat16)
    for degree in range(mode_count):
        active = degree > orders
        denom = np.maximum(degree * degree - orders * orders, 1.0)
        coef_a = np.sqrt(max(4.0 * degree * degree - 1.0, 0.0) / denom)
        lower = np.maximum((degree - 1.0) ** 2 - orders * orders, 0.0)
        coef_b = np.sqrt(lower * (2.0 * degree + 1.0) / (max(2.0 * degree - 3.0, 1.0) * denom))
        p_next = np.where(active, coef_a * cosine * p_now - coef_b * p_prev, p_now)
        p_prev = np.where(active, p_now, p_prev)
        p_now = p_next
        value = np.where(degree >= orders, p_now * np.exp(log_scale), 0.0)
        table[:, degree, :] = value.astype(np.float32).astype(ml_dtypes.bfloat16)
        if degree % 32 == 31:
            magnitude = np.maximum(np.abs(p_now), np.abs(p_prev))
            p_now, p_prev = p_now / magnitude, p_prev / magnitude
            log_scale = log_scale + np.log(magnitude)
    return table


@functools.lru_cache(maxsize=2)
def fourier_constant(devices, lon_count):
    half, slots = lon_count // 2, MODES // devices
    tables = []
    for parity in range(2):
        owner = 2 * np.arange(devices // 2)[:, None] + parity
        orders = (np.arange(slots)[None, :] * devices + owner).reshape(-1)
        phases = (orders[None, :] * np.arange(half)[:, None]) % lon_count
        angles = 2.0 * np.pi / lon_count * phases
        both = np.concatenate([np.cos(angles), -np.sin(angles)], 1) / math.sqrt(lon_count)
        tables.append(both.astype(np.float32).astype(ml_dtypes.bfloat16))
    table = np.stack(tables, 0)
    return np.ascontiguousarray(table), np.ascontiguousarray(table.transpose(0, 2, 1))


def degree_starts(devices):
    firsts = [slot * devices // 16 * 16 for slot in range(MODES // devices)]
    rows = [MODES - first for first in firsts]
    offsets = [sum(rows[:slot]) for slot in range(len(rows))]
    return firsts, offsets, sum(rows)


@functools.lru_cache(maxsize=2)
def packed_legendre(devices, lat_count):
    firsts, offsets, total = degree_starts(devices)
    table = legendre_constant(lat_count, MODES)
    packed = np.concatenate(
        [
            table[slot * devices : (slot + 1) * devices, first:]
            for slot, first in enumerate(firsts)
        ],
        1,
    )
    return np.ascontiguousarray(packed), np.ascontiguousarray(packed.transpose(0, 2, 1))


def table_constants(devices, lat_count):
    _, _, total = degree_starts(devices)
    if devices * total * 2 * (lat_count + max(lat_count, 128)) > TABLE_BYTES:
        return None
    return tuple(jnp.asarray(table) for table in packed_legendre(devices, lat_count))


def made_tables(devices, lat_count, me):
    firsts, _, _ = degree_starts(devices)
    slot_orders = jnp.arange(MODES // devices, dtype=jnp.int32) * devices + me
    legendre = legendre_rows(slot_orders, lat_count, MODES).astype(BF16)
    rows = jnp.concatenate([legendre[slot, first:] for slot, first in enumerate(firsts)], 0)
    return rows, rows.T


def mixing_matrix(mix_weight):
    upper = jnp.concatenate([mix_weight[0], mix_weight[1]], 1)
    lower = jnp.concatenate([-mix_weight[1], mix_weight[0]], 1)
    return jnp.concatenate([upper, lower], 0)


def gelu_slope(field):
    return 0.5 * (1.0 + lax.erf(field * (1.0 / math.sqrt(2.0)))) + field * jnp.exp(
        -0.5 * field * field
    ) * (1.0 / math.sqrt(2.0 * math.pi))


def dot(left, right):
    return jnp.dot(left, right, preferred_element_type=F32)


def row_chunks(count):
    size = count // 3 if count % 48 == 0 else count
    return [(start, size) for start in range(0, count, size)]


def store_rows(out_ref, slots, parity, lat, part, value):
    start = (2 * lat + part) * slots
    out_ref[:, parity, start : start + slots, :] = value.reshape(-1, slots, value.shape[1])


def load_rows(ref, slots, parity, lat, part):
    start = (2 * lat + part) * slots
    return ref[:, parity, start : start + slots, :].reshape(-1, ref.shape[3])


def load_pair(ref, slots, parity, lat):
    return jnp.concatenate([load_rows(ref, slots, parity, lat, part) for part in range(2)], 1)


def fetch_kernel(*refs):
    count = (len(refs) - 1) // 2
    sems = refs[-1]
    copies = [
        pltpu.make_async_copy(refs[index], refs[count + index], sems.at[index])
        for index in range(count)
    ]
    for copy in copies:
        copy.start()
    for copy in copies:
        copy.wait()


def fetch_place_kernel(place_ref, source_hbm, out_ref, sems):
    copy = pltpu.make_async_copy(
        source_hbm.at[place_ref[0], : out_ref.shape[0], :], out_ref, sems.at[0]
    )
    copy.start()
    copy.wait()


def analyse_kernel(
    slots, grid_hbm, columns_hbm, out_ref, grid_ref, columns_ref, folded_ref, sems
):
    lats, lon_count, channels = grid_ref.shape
    half = lon_count // 2
    block = columns_ref.shape[1] // 2
    grid_copies = [
        pltpu.make_async_copy(grid_hbm.at[lat], grid_ref.at[lat], sems.at[lat])
        for lat in range(lats)
    ]
    table_copies = [
        pltpu.make_async_copy(
            columns_hbm.at[parity, part * block : (part + 1) * block, :],
            columns_ref.at[parity, part * block : (part + 1) * block, :],
            sems.at[lats + 2 * parity + part],
        )
        for parity in range(2)
        for part in range(2)
    ]
    for copy in grid_copies + table_copies:
        copy.start()
    for lat in range(lats):
        grid_copies[lat].wait()
        near = grid_ref[lat, :half, :].astype(F32)
        far = grid_ref[lat, half:, :].astype(F32)
        folded_ref[0, :, lat * channels : (lat + 1) * channels] = (near + far).astype(BF16)
        folded_ref[1, :, lat * channels : (lat + 1) * channels] = (near - far).astype(BF16)
    for parity in range(2):
        for part in range(2):
            table_copies[2 * parity + part].wait()
        result = dot(columns_ref[parity], folded_ref[parity]).astype(BF16)
        for part in range(2):
            for lat in range(lats):
                lanes = slice(lat * channels, (lat + 1) * channels)
                rows = slice(part * block, (part + 1) * block)
                store_rows(out_ref, slots, parity, lat, part, result[rows, lanes])


def slot_rows(ref, part, slot, slots, lats):
    return ref[pl.ds(part * slots + slot, lats, stride=ref.shape[0] // lats), :]


def slot_pair(ref, slot, slots, lats, scale):
    return jnp.concatenate(
        [(slot_rows(ref, part, slot, slots, lats) * scale).astype(BF16) for part in range(2)], 1
    )


def slot_halves(slots):
    size = slots // 2 if slots % 32 == 0 else slots
    return [(start, size) for start in range(0, slots, size)]


class Spread:
    def __init__(self, slots, spread_ref, array_ref):
        lats, self.rows, channels = array_ref.shape
        self.slots = slots
        self.halves = slot_halves(slots)
        self.spread_ref = spread_ref.reshape(lats, spread_ref.shape[0] // lats, channels)
        self.array_ref = array_ref

    def need(self, slot):
        for start, size in self.halves:
            if slot == start:
                for part in range(2):
                    begin = part * self.slots + start
                    span = slice(begin, begin + size)
                    self.spread_ref[:, span, :] = self.array_ref[:, span, :].astype(F32)


def staggered(count, delay, first_stage, second_stage):
    waiting = []
    for index in range(count):
        waiting.append((index, first_stage(index)))
        if len(waiting) > delay:
            second_stage(*waiting.pop(0))
    for item in waiting:
        second_stage(*item)


def spectrum_kernel(
    devices,
    modes_ref,
    rows_ref,
    gain_ref,
    weight_ref,
    alpha_ref,
    place_ref,
    columns_hbm,
    out_hbm,
    columns_ref,
    in_s,
    out_s,
    out_ref,
    columns_sem,
    out_sems,
):
    columns_copy = pltpu.make_async_copy(
        columns_hbm.at[place_ref[0]], columns_ref, columns_sem.at[0]
    )
    columns_copy.start()
    slots = MODES // devices
    lats = weight_ref.shape[0]
    firsts, offsets, _ = degree_starts(devices)
    landing = Spread(slots, in_s, modes_ref)
    stores = []
    gain = gain_ref[...]
    channels = gain.shape[1]
    lat_weight = weight_ref[...]

    def forward(slot):
        first, offset = firsts[slot], offsets[slot]
        landing.need(slot)
        modes = slot_pair(in_s, slot, slots, lats, lat_weight)
        spectrum = dot(rows_ref[offset : offset + MODES - first, :], modes).astype(BF16)
        return spectrum * jnp.concatenate([gain[first:], gain[first:]], 1)

    def back(slot, scaled):
        first, offset = firsts[slot], offsets[slot]
        if slot == 0:
            columns_copy.wait()
        result = dot(columns_ref[:, offset : offset + MODES - first], scaled)
        result = result * (alpha_ref[...] if slot == 0 else 2.0)
        for part in range(2):
            out_s[pl.ds(part * slots + slot, lats, stride=out_s.shape[0] // lats), :] = result[
                :, part * channels : (part + 1) * channels
            ]
        for start, size in landing.halves:
            if slot == start + size - 1:
                store(start, size)

    def store(start, size):
        view = out_s.reshape(lats, out_s.shape[0] // lats, channels)
        for part in range(2):
            span = slice(part * slots + start, part * slots + start + size)
            out_ref[:, span, :] = view[:, span, :].astype(BF16)
            if size < slots:
                copy = pltpu.make_async_copy(
                    out_ref.at[:, span, :], out_hbm.at[:, span, :], out_sems.at[len(stores)]
                )
                copy.start()
                stores.append(copy)
        if size == slots:
            copy = pltpu.make_async_copy(out_ref, out_hbm, out_sems.at[0])
            copy.start()
            stores.append(copy)

    staggered(slots, DELAY, forward, back)
    for copy in stores:
        copy.wait()


def pairs_kernel(devices, weight_ref, modes_ref, near_ref, far_ref, in_s):
    slots = MODES // devices
    lats = weight_ref.shape[0]
    landing = Spread(slots, in_s, modes_ref)
    lat_weight = weight_ref[...]
    near = near_ref.shape[0] // lats
    for slot in range(slots):
        landing.need(slot)
        pair = slot_pair(in_s, slot, slots, lats, lat_weight)
        if slot < near:
            near_ref[slot * lats : (slot + 1) * lats, :] = pair
        else:
            far_ref[(slot - near) * lats : (slot - near + 1) * lats, :] = pair


def gradient_kernel(
    devices,
    grads_ref,
    near_rows_ref,
    near_pairs_ref,
    gain_ref,
    weight_ref,
    alpha_ref,
    part_ref,
    place_ref,
    far_pairs_hbm,
    rows_hbm,
    columns_hbm,
    out_ref,
    filter_ref,
    far_pairs_ref,
    far_rows_ref,
    columns_ref,
    grad_s,
    out_s,
    far_sems,
    columns_sem,
):
    slots = MODES // devices
    lats = weight_ref.shape[0]
    firsts, offsets, _ = degree_starts(devices)
    columns_copy = pltpu.make_async_copy(
        columns_hbm.at[place_ref[0]], columns_ref, columns_sem.at[0]
    )
    near = near_pairs_ref.shape[0] // lats
    split = near_rows_ref.shape[0]
    far_copies = [
        pltpu.make_async_copy(far_pairs_hbm, far_pairs_ref, far_sems.at[0]),
        pltpu.make_async_copy(
            rows_hbm.at[place_ref[0], split:, :], far_rows_ref, far_sems.at[1]
        ),
    ]
    for copy in [columns_copy, *far_copies]:
        copy.start()
    landing = Spread(slots, grad_s, grads_ref)
    gain = gain_ref[...].astype(F32)
    lat_weight = weight_ref[...]
    channels = gain.shape[1]
    filter_ref[...] = jnp.zeros_like(filter_ref)

    def forward(slot):
        first, offset = firsts[slot], offsets[slot]
        landing.need(slot)
        if slot == near:
            for copy in far_copies:
                copy.wait()
        scale = alpha_ref[:, :channels] if slot == 0 else 2.0
        pairs_ref, rows_ref = near_pairs_ref, near_rows_ref
        place = slot
        if slot >= near:
            pairs_ref, rows_ref = far_pairs_ref, far_rows_ref
            place, offset = slot - near, offset - split
        modes = pairs_ref[place * lats : (place + 1) * lats, :]
        grads = slot_pair(grad_s, slot, slots, lats, scale)
        table = rows_ref[offset : offset + MODES - first, :]
        spectrum = dot(table, modes)
        gscaled = dot(table, grads)
        product = gscaled * spectrum
        filter_ref[first:, :] += product[:, :channels] + product[:, channels:]
        return (gscaled * jnp.concatenate([gain[first:], gain[first:]], 1)).astype(BF16)

    def back(slot, gspectrum):
        first, offset = firsts[slot], offsets[slot]
        if slot == 0:
            columns_copy.wait()
        result = dot(columns_ref[:, offset : offset + MODES - first], gspectrum)
        for part in range(2):
            out_s[pl.ds(part * slots + slot, lats, stride=out_s.shape[0] // lats), :] = (
                result[:, part * channels : (part + 1) * channels] * lat_weight
            )

    staggered(slots, DELAY, forward, back)
    rows = lats // devices * 2 * slots
    view = out_s.reshape(lats, out_s.shape[0] // lats, channels)
    out_ref[:, :rows, :] = (
        view[:, : 2 * slots, :].astype(BF16).reshape(devices, rows, channels)
    )
    if out_ref.shape[1] > rows:
        split = rows + MODES // devices
        out_ref[:, rows:split, :] = (
            filter_ref[...].reshape(devices, MODES // devices, channels).astype(BF16)
        )
        out_ref[:, split:, :] = part_ref[...].reshape(devices, -1, channels).astype(BF16)


def slope_kernel(
    slots,
    modes_ref,
    wide_ref,
    wide_t_ref,
    upstream_ref,
    first_ref,
    rows_hbm,
    columns_hbm,
    out_hbm,
    weight_ref,
    rows_ref,
    columns_ref,
    modes_s,
    folded_s,
    out_ref,
    rows_sems,
    columns_sems,
    out_sems,
):
    lats, lon_count, channels = upstream_ref.shape
    half = lon_count // 2
    block = modes_s.shape[1] // 2

    def lat_copy(source, target, sem_refs, parity, lat):
        span = slice(2 * lat * slots, 2 * (lat + 1) * slots)
        return pltpu.make_async_copy(
            source.at[:, parity, span, :],
            target.at[:, parity, span, :],
            sem_refs.at[parity * lats + lat],
        )

    places = [(parity, lat) for parity in range(2) for lat in range(lats)]
    rows_copies = [
        [
            pltpu.make_async_copy(
                rows_hbm.at[parity, start : start + size, :],
                rows_ref.at[parity, start : start + size, :],
                rows_sems.at[2 * chunk + parity],
            )
            for parity in range(2)
        ]
        for chunk, (start, size) in enumerate(row_chunks(half))
        if chunk
    ]
    columns_copies = [
        pltpu.make_async_copy(
            columns_hbm.at[parity], columns_ref.at[parity], columns_sems.at[parity]
        )
        for parity in range(2)
    ]
    for copy in [*sum(rows_copies, []), *columns_copies]:
        copy.start()
    mixed = dot(
        jnp.concatenate([load_pair(modes_ref, slots, *place) for place in places], 0), wide_ref[...]
    ).astype(BF16)
    for index, (parity, lat) in enumerate(places):
        for part in range(2):
            modes_s[
                parity,
                part * block : (part + 1) * block,
                lat * channels : (lat + 1) * channels,
            ] = mixed[
                index * block : (index + 1) * block, part * channels : (part + 1) * channels
            ]
    for chunk, (start, size) in enumerate(row_chunks(half)):
        for copy in rows_copies[chunk - 1] if chunk else ():
            copy.wait()
        table = rows_ref if chunk else first_ref
        even = dot(table[0, start : start + size, :], modes_s[0])
        odd = dot(table[1, start : start + size, :], modes_s[1])
        for lat in range(lats):
            lanes = slice(lat * channels, (lat + 1) * channels)
            near = upstream_ref[lat, start : start + size, :].astype(F32) * gelu_slope(
                even[:, lanes] + odd[:, lanes]
            )
            far = upstream_ref[lat, half + start : half + start + size, :].astype(
                F32
            ) * gelu_slope(even[:, lanes] - odd[:, lanes])
            folded_s[0, start : start + size, lanes] = (near + far).astype(BF16)
            folded_s[1, start : start + size, lanes] = (near - far).astype(BF16)
    pairs, stores = [], []
    for parity in range(2):
        columns_copies[parity].wait()
        raw = dot(columns_ref[parity], folded_s[parity]).astype(BF16)
        parity_pairs = [
            jnp.concatenate(
                [
                    raw[
                        part * block : (part + 1) * block, lat * channels : (lat + 1) * channels
                    ]
                    for part in range(2)
                ],
                1,
            )
            for lat in range(lats)
        ]
        mixed = dot(jnp.concatenate(parity_pairs, 0), wide_t_ref[...]).astype(BF16)
        for lat in range(lats):
            for part in range(2):
                store_rows(
                    out_ref,
                    slots,
                    parity,
                    lat,
                    part,
                    mixed[
                        lat * block : (lat + 1) * block, part * channels : (part + 1) * channels
                    ],
                )
            stores.append(lat_copy(out_ref, out_hbm, out_sems, parity, lat))
            stores[-1].start()
        pairs += parity_pairs
    total = jnp.zeros((2 * channels, 2 * channels), F32)
    for (parity, lat), pair in zip(places, pairs):
        total = total + lax.dot_general(
            load_pair(modes_ref, slots, parity, lat),
            pair,
            (((0,), (0,)), ((), ())),
            preferred_element_type=F32,
        )
    weight_ref[:channels, :] = total[:channels, :channels] + total[channels:, channels:]
    weight_ref[channels:, :] = total[:channels, channels:] - total[channels:, :channels]
    for copy in stores:
        copy.wait()


def synthesis_kernel(
    slots, modes_ref, upstream_hbm, rows_hbm, out_ref, upstream_ref, rows_ref, modes_s, sems
):
    lats, lon_count, channels = upstream_ref.shape
    copies = [
        pltpu.make_async_copy(rows_hbm.at[parity], rows_ref.at[parity], sems.at[parity])
        for parity in range(2)
    ]
    copies += [
        pltpu.make_async_copy(upstream_hbm.at[lat], upstream_ref.at[lat], sems.at[2 + lat])
        for lat in range(lats)
    ]
    for copy in copies:
        copy.start()
    half = lon_count // 2
    block = modes_s.shape[1] // 2
    for parity in range(2):
        for part in range(2):
            for lat in range(lats):
                modes_s[
                    parity,
                    part * block : (part + 1) * block,
                    lat * channels : (lat + 1) * channels,
                ] = load_rows(modes_ref, slots, parity, lat, part)
    for copy in copies:
        copy.wait()
    for start, size in row_chunks(half):
        even = dot(rows_ref[0, start : start + size, :], modes_s[0])
        odd = dot(rows_ref[1, start : start + size, :], modes_s[1])
        for lat in range(lats):
            lanes = slice(lat * channels, (lat + 1) * channels)
            for sign, base in ((1.0, start), (-1.0, half + start)):
                total = even[:, lanes] + sign * odd[:, lanes]
                total = total + upstream_ref[lat, base : base + size, :].astype(F32)
                out_ref[lat, base : base + size, :] = total.astype(BF16)


def total_kernel(received_ref, out_ref):
    rows = out_ref.shape[1]
    start = received_ref.shape[1] - rows
    total = received_ref[0, start:, :].astype(F32)
    for device in range(1, received_ref.shape[0]):
        total = total + received_ref[device, start:, :].astype(F32)
    out_ref[...] = jnp.broadcast_to(total.astype(BF16)[None], out_ref.shape)


def finish_kernel(received_ref, filter_ref, weight_ref):
    devices, rows, channels = received_ref.shape
    split = filter_ref.shape[0] // devices
    filter_ref[...] = (
        received_ref[:, :split, :].astype(F32).reshape(filter_ref.shape) * 0.125
    )
    weight_ref[...] = received_ref[:, split:, :].astype(F32).reshape(weight_ref.shape) * (
        1.0 / MODES
    )


def call(kernel, out_shape, scratch, flops, operands, streamed=(), written=0):
    outs = out_shape if isinstance(out_shape, (list, tuple)) else [out_shape]
    moved = sum(2 * math.prod(array.shape) for array in [*operands, *streamed, *outs])
    specs = [
        pl.BlockSpec(memory_space=pl.ANY if index < written else pltpu.VMEM)
        for index in range(len(outs))
    ]
    return pl.pallas_call(
        kernel,
        out_shape=out_shape,
        in_specs=[
            pl.BlockSpec(memory_space=pltpu.SMEM if array.dtype == jnp.int32 else pltpu.VMEM)
            for array in operands
        ]
        + [pl.BlockSpec(memory_space=pl.ANY)] * len(streamed),
        out_specs=specs if isinstance(out_shape, (list, tuple)) else specs[0],
        scratch_shapes=scratch,
        cost_estimate=pl.CostEstimate(flops=flops, bytes_accessed=moved, transcendentals=0),
        compiler_params=pltpu.CompilerParams(vmem_limit_bytes=VMEM_BYTES),
    )(*operands, *(away(array) for array in streamed))


def away(array):
    return pltpu.with_memory_space_constraint(array, pltpu.HBM)


def held(array):
    return pltpu.with_memory_space_constraint(array, pltpu.VMEM)


def exchange(array):
    return lax.all_to_all(array, "space", split_axis=0, concat_axis=0, tiled=True)


def sum_over_space(array, devices):
    step = devices // 2
    while step:
        array = array + lax.ppermute(
            array, "space", [(index, index ^ step) for index in range(devices)]
        )
        step //= 2
    return array


def body(grid_in, upstream, mix_weight, degree_filter):
    devices = lax.axis_size("space")
    me = lax.axis_index("space")
    lats, lon_count, channels = grid_in.shape
    lat_count = lats * devices
    slots = MODES // devices
    half = lon_count // 2
    dft_rows, dft_columns = fourier_constant(devices, lon_count)
    first_rows = jnp.asarray(dft_rows[:, : row_chunks(half)[0][1]])
    dft_rows, dft_columns = jnp.asarray(dft_rows), jnp.asarray(dft_columns)
    constants = table_constants(devices, lat_count)
    place = me.reshape(1)
    if constants is None:
        leg_rows, leg_columns = made_tables(devices, lat_count, me)
        leg_columns = leg_columns[None]
        place = jnp.zeros_like(place)
    else:
        leg_rows = lax.dynamic_index_in_dim(constants[0], me, 0, keepdims=False)
        leg_columns = constants[1]
    angles = np.pi * (np.arange(lat_count) + 0.5) / lat_count
    lat_weight = jnp.asarray(
        np.broadcast_to((np.pi / lat_count * np.sin(angles))[:, None], (lat_count, channels)), F32
    )
    alpha = jnp.where(me == 0, 1.0, 2.0) * jnp.ones((1, 2 * channels), F32)
    wide = mixing_matrix(mix_weight)
    mode_rows = lats * 2 * slots
    grid_shape = jax.ShapeDtypeStruct((devices // 2, 2, mode_rows, channels), BF16)
    grid_out = pltpu.HBM(grid_shape.shape, BF16)
    block_shape = (devices, mode_rows, channels)
    mode_shape = jax.ShapeDtypeStruct((lat_count, 2 * slots, channels), BF16)
    spread_shape = pltpu.VMEM((lat_count * (2 * slots + 8), channels), F32)
    modes_scratch = pltpu.VMEM((2, MODES, lats * channels), BF16)
    folded_scratch = pltpu.VMEM((2, half, lats * channels), BF16)
    dft_flops = 2 * MODES * lon_count * lats * channels
    leg_flops = 4 * degree_starts(devices)[2] * lat_count * channels
    modes_landing = pltpu.VMEM(mode_shape.shape, BF16)
    columns_landing = pltpu.VMEM(leg_columns.shape[1:], BF16)
    weight_rows = 2 * channels // devices
    extra = MODES // devices + weight_rows
    joined = (MODES // devices) % 16 == 0 and weight_rows % 16 == 0

    fourier = call(
        functools.partial(analyse_kernel, slots),
        grid_out,
        [
            pltpu.VMEM(grid_in.shape, BF16),
            pltpu.VMEM(dft_columns.shape, BF16),
            folded_scratch,
            pltpu.SemaphoreType.DMA((lats + 4,)),
        ],
        dft_flops,
        [],
        [grid_in, dft_columns],
    )
    held_upstream, held_first = (
        held(
            call(
                fetch_kernel,
                pltpu.VMEM(array.shape, BF16),
                [pltpu.SemaphoreType.DMA((1,))],
                0,
                [],
                [array],
            )
        )
        for array in (upstream, first_rows)
    )
    modes = exchange(fourier.reshape(block_shape)).reshape(mode_shape.shape)
    returned = call(
        functools.partial(spectrum_kernel, devices),
        pltpu.HBM(mode_shape.shape, BF16),
        [
            columns_landing,
            spread_shape,
            spread_shape,
            modes_landing,
            pltpu.SemaphoreType.DMA((1,)),
            pltpu.SemaphoreType.DMA((4,)),
        ],
        2 * leg_flops,
        [held(modes), held(leg_rows), degree_filter, lat_weight, alpha, place],
        [leg_columns],
        written=1,
    )
    returned = exchange(returned.reshape(block_shape)).reshape(grid_shape.shape)
    grid_landing = pltpu.VMEM(grid_shape.shape, BF16)
    mixed_grad, weight_part = call(
        functools.partial(slope_kernel, slots),
        [grid_out, jax.ShapeDtypeStruct((2 * channels, channels), F32)],
        [
            pltpu.VMEM(dft_rows.shape, BF16),
            pltpu.VMEM(dft_columns.shape, BF16),
            modes_scratch,
            folded_scratch,
            grid_landing,
            pltpu.SemaphoreType.DMA((2 * len(row_chunks(half)),)),
            pltpu.SemaphoreType.DMA((2,)),
            pltpu.SemaphoreType.DMA((2 * lats,)),
        ],
        2 * dft_flops,
        [held(returned), wide, wide.T, held_upstream, held_first],
        [dft_rows, dft_columns],
        written=1,
    )
    late_place, late_modes, mixed_grad = lax.optimization_barrier((place, modes, mixed_grad))
    near = slot_halves(slots)[0][1]
    if near == slots:
        near = slots // 2
    split = degree_starts(devices)[1][near]
    late_rows, near_rows = leg_rows[None], leg_rows[:split]
    if constants is not None:
        late_rows = constants[0]
        near_rows = call(
            fetch_place_kernel,
            pltpu.VMEM((split, lat_count), BF16),
            [pltpu.SemaphoreType.DMA((1,))],
            0,
            [late_place],
            [late_rows],
        )
    far_pairs_shape = ((slots - near) * lat_count, 2 * channels)
    near_pairs, far_pairs = call(
        functools.partial(pairs_kernel, devices),
        [
            pltpu.VMEM((near * lat_count, 2 * channels), BF16),
            pltpu.HBM(far_pairs_shape, BF16),
        ],
        [spread_shape],
        0,
        [lat_weight, away(late_modes)],
    )
    grads = exchange(mixed_grad.reshape(block_shape)).reshape(mode_shape.shape)
    gfield, filter_part = call(
        functools.partial(gradient_kernel, devices),
        [
            jax.ShapeDtypeStruct((devices, mode_rows + (extra if joined else 0), channels), BF16),
            jax.ShapeDtypeStruct((MODES, channels), F32),
        ],
        [
            pltpu.VMEM(far_pairs_shape, BF16),
            pltpu.VMEM((leg_rows.shape[0] - split, lat_count), BF16),
            columns_landing,
            spread_shape,
            spread_shape,
            pltpu.SemaphoreType.DMA((2,)),
            pltpu.SemaphoreType.DMA((1,)),
        ],
        3 * leg_flops,
        [
            held(grads),
            held(near_rows),
            held(near_pairs),
            degree_filter,
            lat_weight,
            alpha,
            weight_part,
            late_place,
        ],
        [far_pairs, late_rows, leg_columns],
    )
    gfield = exchange(gfield)
    if joined:
        sums = call(
            total_kernel, jax.ShapeDtypeStruct((devices, extra, channels), BF16), [], 0, [gfield]
        )
        grad_filter, grad_weight = call(
            finish_kernel,
            [
                jax.ShapeDtypeStruct((MODES, channels), F32),
                jax.ShapeDtypeStruct((2 * channels, channels), F32),
            ],
            [],
            0,
            [exchange(sums)],
        )
    else:
        grad_filter = sum_over_space(filter_part, devices) * 0.125
        grad_weight = sum_over_space(weight_part, devices) * (1.0 / MODES)
    grad_in = call(
        functools.partial(synthesis_kernel, slots),
        jax.ShapeDtypeStruct(grid_in.shape, BF16),
        [
            pltpu.VMEM(upstream.shape, BF16),
            pltpu.VMEM(dft_rows.shape, BF16),
            modes_scratch,
            pltpu.SemaphoreType.DMA((2 + lats,)),
        ],
        dft_flops,
        [gfield.reshape(devices // 2, 2, -1, channels)],
        [upstream, dft_rows],
    )
    return (grad_in, grad_weight.reshape(2, channels, channels), grad_filter)


def solution(mesh):
    return jax.shard_map(
        body,
        mesh=mesh,
        in_specs=(P(("groups", "space"), None, None), P(("groups", "space"), None, None), P(), P()),
        out_specs=(P(("groups", "space"), None, None), P("groups", None, None), P("groups", None)),
        check_vma=False,
    )
```
